32 devices in a mesh: dp: 16 (over z, x, core), seq: 2 (over y).
Axes of the slice: x: 2, y: 2, z: 4, core: 2. Of those that a mesh axis runs over, the one named last changes fastest.
Arguments:
- tokens: bfloat16 [64, 1024, 512], P('dp', 'seq'), may hold values from -6 to 6
- segments: int32 [64, 1024], P('dp'), may hold values from 0 to 2, as said below
- keep_flags: int32 [64], P('dp'), may hold values 0 or 1
- query_weight: bfloat16 [512, 512], replicated, may hold values from -0.375 to 0.375
- query_bias: float32 [512], replicated, may hold values from -1.75 to 1.75
- key_weight: bfloat16 [512, 512], replicated, may hold values from -0.375 to 0.375
- value_weight: bfloat16 [512, 512], replicated, may hold values from -0.25 to 0.25
- value_bias: float32 [512], replicated, may hold values from -1.75 to 1.75
- out_weight: bfloat16 [512, 512], replicated, may hold values from -1 to 1
- out_bias: float32 [512], replicated, may hold values from -1.75 to 1.75
- first_gain: float32 [512], replicated, may hold values from 0.5 to 1.5
- first_shift: float32 [512], replicated, may hold values from -1.75 to 1.75
- up_weight: bfloat16 [512, 2048], replicated, may hold values from -0.25 to 0.25
- up_bias: float32 [2048], replicated, may hold values from -1.75 to 1.75
- down_weight: bfloat16 [2048, 512], replicated, may hold values from -0.125 to 0.125
- down_bias: float32 [512], replicated, may hold values from -1.75 to 1.75
- second_gain: float32 [512], replicated, may hold values from 0.5 to 1.5
- second_shift: float32 [512], replicated, may hold values from -1.75 to 1.75
- cotangent: bfloat16 [64, 1024, 512], P('dp', 'seq'), may hold values from -6 to 6
Outputs:
- layer_out: bfloat16 [64, 1024, 512], P('dp', 'seq')
- tokens_grad: bfloat16 [64, 1024, 512], P('dp', 'seq')
- query_weight_grad: float32 [512, 512], replicated
- query_bias_grad: float32 [512], replicated
- key_weight_grad: float32 [512, 512], replicated
- value_weight_grad: float32 [512, 512], replicated
- value_bias_grad: float32 [512], replicated
- out_weight_grad: float32 [512, 512], replicated
- out_bias_grad: float32 [512], replicated
- first_gain_grad: float32 [512], replicated
- first_shift_grad: float32 [512], replicated
- up_weight_grad: float32 [512, 2048], replicated
- up_bias_grad: float32 [2048], replicated
- down_weight_grad: float32 [2048, 512], replicated
- down_bias_grad: float32 [512], replicated
- second_gain_grad: float32 [512], replicated
- second_shift_grad: float32 [512], replicated
The draws below stay inside these ranges and needn't reach their ends.
Inputs may be any that keep to these rules, and one draw needn't show every extreme that they name: `segments`: along each row the ids never fall.
All inputs are finite; a program needn't handle non-finite values. No bound on the sum of `keep_flags` on one device may be relied on, other than what follows from the above.
Results may differ from the reference program's by a relative error of at most 0.025.
Values may be sent and summed in bfloat16 or wider, within the bound.
No kernel may reach another device: no remote copies, remote signals or barrier semaphores. Data moves between devices by JAX's collectives and lax.ppermute only.
A program may use at most 320 MiB of HBM per device.

```python
import jax
import jax.numpy as jnp
from jax import lax

D = 512
HEADS = 8
FF = 2048
SEQ_LEN = 1024
ROWS = 64
TOK_DEV = 512


def draw_segments(key, part):
    key = jax.random.fold_in(key, 11)
    start_key, end_key = jax.random.split(key)
    reach_len = max(TOK_DEV // 2, 1)
    starts = jax.random.randint(start_key, (ROWS, 1), 0, reach_len + 1)
    starts = starts.at[0, 0].set(jnp.maximum(starts[0, 0], 1))
    ends = jax.random.randint(end_key, (ROWS, 1), SEQ_LEN - reach_len, SEQ_LEN)
    position = jnp.arange(SEQ_LEN, dtype=jnp.int32)[None, :]
    return (position >= starts).astype(jnp.int32) + (position >= ends).astype(jnp.int32)


def place_ends(drawn, stream_key, low, top_value):
    spot = [jax.random.randint(jax.random.fold_in(stream_key, axis), (), 0, length) for axis, length in enumerate(drawn.shape)]
    longest = drawn.shape.index(max(drawn.shape))
    beside = spot[:longest] + [(spot[longest] + 1) % drawn.shape[longest]] + spot[longest + 1:]
    return drawn.at[tuple(spot)].set(low).at[tuple(beside)].set(top_value)


def steps_of(rng, dims, cuts, low, high):
    loudness, own = 1.0, jax.random.fold_in(rng, 6)
    for dim, parts in cuts:
        draws = jnp.exp(jax.random.uniform(jax.random.fold_in(own, dim), (parts,), jnp.float32, low / len(cuts), high / len(cuts)))
        loudness = loudness * jnp.repeat(draws, dims[dim] // parts).reshape([-1 if axis == dim else 1 for axis in range(len(dims))])
    return loudness


def noise(key, dims, deviation, reach, shards=(), kind=jnp.bfloat16):
    factor_of = steps_of(key, dims, shards, -0.22, 0.18) if shards else 1.0
    values = jax.random.normal(key, dims, jnp.float32) * deviation * factor_of
    return jnp.minimum(jnp.maximum(values, -reach), reach).astype(kind)


def setup_inputs(seed: int = 0) -> dict:
    streams_of = jax.random.split(jax.random.key(seed), 20)
    return {
        "tokens": noise(streams_of[0], (ROWS, SEQ_LEN, D), 1.0, 6.0, ((0, 16), (1, 2))),
        "segments": draw_segments(jax.random.fold_in(streams_of[19], 71), 0),
        "keep_flags": place_ends((jax.random.randint(streams_of[2], (ROWS,), 0, 4) < 3).astype(jnp.int32), jax.random.fold_in(streams_of[2], 1), 0, 1),
        "query_weight": noise(streams_of[3], (D, D), (D // 2) ** -0.5, 0.375),
        "query_bias": noise(streams_of[4], (D,), 0.3, 1.75, (), jnp.float32),
        "key_weight": noise(streams_of[5], (D, D), (D // 2) ** -0.5, 0.375),
        "value_weight": noise(streams_of[6], (D, D), D ** -0.5, 0.25),
        "value_bias": noise(streams_of[7], (D,), 0.3, 1.75, (), jnp.float32),
        "out_weight": noise(streams_of[8], (D, D), (D // 16) ** -0.5, 1.0),
        "out_bias": noise(streams_of[9], (D,), 0.3, 1.75, (), jnp.float32),
        "first_gain": jnp.clip(1.0 + 0.1 * jax.random.normal(streams_of[10], (D,), jnp.float32), 0.5, 1.5),
        "first_shift": noise(streams_of[11], (D,), 0.3, 1.75, (), jnp.float32),
        "up_weight": noise(streams_of[12], (D, FF), D ** -0.5, 0.25),
        "up_bias": noise(streams_of[13], (FF,), 0.3, 1.75, (), jnp.float32),
        "down_weight": noise(streams_of[14], (FF, D), FF ** -0.5, 0.125),
        "down_bias": noise(streams_of[15], (D,), 0.3, 1.75, (), jnp.float32),
        "second_gain": jnp.clip(1.0 + 0.1 * jax.random.normal(streams_of[16], (D,), jnp.float32), 0.5, 1.5),
        "second_shift": noise(streams_of[17], (D,), 0.3, 1.75, (), jnp.float32),
        "cotangent": noise(streams_of[18], (ROWS, SEQ_LEN, D), 1.0, 6.0, ((0, 16), (1, 2))),
    }


@jax.custom_vjp
def low(v):
    return lax.optimization_barrier(v.astype(jnp.bfloat16)).astype(jnp.float32)

@jax.custom_vjp
def low_back(v):
    return v

def low_keep(v):
    return (low(v), None)

def low_pass(kept, grad):
    return (grad,)

def back_keep(v):
    return (v, None)

def back_low(kept, grad):
    return (low(grad),)
low.defvjp(low_keep, low_pass)
low_back.defvjp(back_keep, back_low)
PRECISE = lax.Precision.HIGHEST
NEG_FILL = -1e+30
EPSILON = 1e-05

def both_ways(values):
    return low(low_back(values))

def matmul_high(left, right):
    return jnp.dot(left, right, precision=PRECISE)

def norm_rows(values, gain, shift):
    row_mean = lax.optimization_barrier(jnp.mean(values, -1, keepdims=True))
    centred = values - row_mean
    variance = lax.optimization_barrier(jnp.mean(centred * centred, -1, keepdims=True))
    return centred * lax.rsqrt(variance + EPSILON) * gain + shift

def layer_row(params, row_tokens, row_ids):
    query_weight, query_bias, key_weight, value_weight, value_bias, out_weight, out_bias, first_gain, first_shift, up_weight, up_bias, down_weight, down_bias, second_gain, second_shift = params
    length = row_tokens.shape[0]
    head_dim = row_tokens.shape[1] // HEADS
    query = both_ways(matmul_high(row_tokens, query_weight) + query_bias).reshape(length, HEADS, head_dim)
    key_rows = both_ways(matmul_high(row_tokens, key_weight)).reshape(length, HEADS, head_dim)
    values = both_ways(matmul_high(row_tokens, value_weight) + value_bias).reshape(length, HEADS, head_dim)
    scores = low_back(jnp.einsum('qhd,khd->hqk', query, key_rows, precision=PRECISE) * head_dim ** (-0.5))
    same_doc = row_ids[:, None] == row_ids[None, :]
    scores = jnp.where(same_doc[None], scores, NEG_FILL)
    largest = lax.optimization_barrier(jnp.max(scores, -1, keepdims=True))
    raised = jnp.exp(scores - largest)
    weights = raised / lax.optimization_barrier(jnp.sum(raised, -1, keepdims=True))
    context = jnp.einsum('hqk,khd->qhd', low(weights), values, precision=PRECISE)
    context = both_ways(context.reshape(length, HEADS * head_dim))
    first_sum = row_tokens + low_back(matmul_high(context, out_weight) + out_bias)
    hidden = norm_rows(first_sum, first_gain, first_shift)
    pre_act = low_back(matmul_high(low(hidden), up_weight) + up_bias)
    branch = low_back(matmul_high(low(jax.nn.gelu(pre_act, approximate=False)), down_weight) + down_bias)
    return norm_rows(hidden + branch, second_gain, second_shift)

def reference(tokens, segments, keep_flags, query_weight, query_bias, key_weight, value_weight, value_bias, out_weight, out_bias, first_gain, first_shift, up_weight, up_bias, down_weight, down_bias, second_gain, second_shift, cotangent):
    params = tuple((argument.astype(jnp.float32) for argument in (query_weight, query_bias, key_weight, value_weight, value_bias, out_weight, out_bias, first_gain, first_shift, up_weight, up_bias, down_weight, down_bias, second_gain, second_shift)))

    def one_row(totals, inputs):
        row_tokens, row_ids, row_flag, row_cotangent = inputs

        def forward(weights, values):
            return jnp.where(row_flag != 0, layer_row(weights, values, row_ids), values)
        result, pullback = jax.vjp(forward, params, row_tokens)
        weight_grads, row_grad = pullback(row_cotangent)
        totals = jax.tree.map(jnp.add, totals, weight_grads)
        return (totals, (result.astype(jnp.bfloat16), row_grad.astype(jnp.bfloat16)))
    zero_grads = tuple((jnp.zeros_like(argument) for argument in params))
    totals, (layer_out, tokens_grad) = lax.scan(one_row, zero_grads, (tokens.astype(jnp.float32), segments, keep_flags, cotangent.astype(jnp.float32)))
    return (layer_out, tokens_grad, totals[0], totals[1], totals[2], totals[3], totals[4], totals[5], totals[6], totals[7], totals[8], totals[9], totals[10], totals[11], totals[12], totals[13], totals[14])
```

```python
import functools
import math

import jax
import jax.numpy as jnp
from jax import lax
from jax.experimental import pallas as pl
from jax.experimental.pallas import tpu as pltpu
from jax.sharding import PartitionSpec as P

HEADS = 8
EXTRA = 16
LANES = 128
LINE_ROWS = 2
NEG_FILL = -1e30
EPSILON = 1e-05
BLOCK_CAP = 512
LOG2E = 1.4426950408889634
LN2 = 0.6931471805599453
MIB = 1 << 20


def dot(left, right, left_dim, right_dim):
    return lax.dot_general(
        left, right, (((left_dim,), (right_dim,)), ((), ())), preferred_element_type=jnp.float32
    )


def three_parts(values):
    high = values.astype(jnp.bfloat16)
    rest = values - high.astype(jnp.float32)
    middle = rest.astype(jnp.bfloat16)
    low = (rest - middle.astype(jnp.float32)).astype(jnp.bfloat16)
    return high.astype(jnp.float32), middle.astype(jnp.float32), low.astype(jnp.float32)


def extra_rows(base, values, first):
    row = lax.broadcasted_iota(jnp.int32, base.shape, 0)
    for offset, part in enumerate(three_parts(values)):
        base = jnp.where(row == first + offset, part, base)
    return base


def attend_kernel(pieces, width, block, *refs):
    _, refs = refs[0], refs[1:]
    token_refs, refs = refs[:pieces], refs[pieces:]
    (
        query_extra,
        key_extra,
        query_weight,
        query_bias,
        key_weight,
        value_weight,
        value_bias,
        query_out,
        key_out,
        value_out,
        context_out,
        scores_even,
        scores_odd,
        largest_even,
        largest_odd,
    ) = refs
    query_out, key_out, value_out = (ref.at[0] for ref in (query_out, key_out, value_out))
    length = query_out.shape[2]
    local = length // pieces
    for piece in range(pieces):
        span = pl.ds(piece * local, local)
        tokens = token_refs[piece][0]
        query = (dot(query_weight[...], tokens, 0, 1) + query_bias[...]) * (LOG2E * width**-0.5)
        query_out[:, :width, span] = query.astype(jnp.bfloat16).reshape(HEADS, width, local)
        key = dot(key_weight[...], tokens, 0, 1)
        key_out[:, :width, span] = key.astype(jnp.bfloat16).reshape(HEADS, width, local)
        value = dot(value_weight[...], tokens, 0, 1) + value_bias[...]
        value_out[:, :width, span] = value.astype(jnp.bfloat16).reshape(HEADS, width, local)
    row = lax.broadcasted_iota(jnp.int32, (EXTRA, length), 0)
    ones = (row < 3).astype(jnp.bfloat16)
    query_base = query_extra[...]
    for head in range(HEADS):
        query_out[head, width:] = query_base.astype(jnp.bfloat16)
        key_out[head, width:] = key_extra[...].astype(jnp.bfloat16)
        value_out[head, width:] = ones

    def score(head, scores_ref, largest_ref, start):
        span = pl.ds(start, block)
        scores = dot(key_out[head], query_out[head, :, span], 0, 0)
        scores_ref[:, span] = scores
        largest_ref[:, span] = jnp.max(scores, 0, keepdims=True)

    def weigh(head, scores_ref, largest_ref, start):
        span = pl.ds(start, block)
        largest = largest_ref[:, span]
        weights = jnp.exp2(scores_ref[:, span] - largest).astype(jnp.bfloat16)
        update = dot(value_out[head], weights, 1, 0)
        total = update[width : width + 1]
        context_out[pl.ds(pl.multiple_of(head * width, width), width), span] = (
            update[:width] / total
        )
        log_total = largest + jnp.log(total) * LOG2E
        query_out[head, width:, span] = extra_rows(
            query_base[:, start : start + block], -log_total, 3
        ).astype(jnp.bfloat16)

    starts = range(0, length, block)
    for start in starts:
        score(0, scores_even, largest_even, start)

    def head_pair(pair, carry):
        head = pair * 2
        for start in starts:
            score(head + 1, scores_odd, largest_odd, start)
            weigh(head, scores_even, largest_even, start)
        following = jnp.minimum(head + 2, HEADS - 1)
        for start in starts:
            score(following, scores_even, largest_even, start)
            weigh(head + 1, scores_odd, largest_odd, start)
        return carry

    lax.fori_loop(0, HEADS // 2, head_pair, 0)


def attend(row_index, tokens, remote, query_extra, key_extra, weights):
    pieces = 1 + len(remote)
    local, model = tokens.shape[1:]
    length = pieces * local
    width = model // HEADS
    whole = lambda array: pl.BlockSpec(array.shape, lambda i, s: (0,) * array.ndim)
    own_spec = pl.BlockSpec((1, local, model), lambda i, s: (s[0], 0, 0))
    low = jax.ShapeDtypeStruct((1, HEADS, width + EXTRA, length), jnp.bfloat16)
    outs = (low, low, low, jax.ShapeDtypeStruct((model, length), jnp.float32))
    operands = (tokens, *remote, query_extra, key_extra, *weights)
    return pl.pallas_call(
        functools.partial(attend_kernel, pieces, width, min(256, length)),
        out_shape=outs,
        grid_spec=pltpu.PrefetchScalarGridSpec(
            num_scalar_prefetch=1,
            grid=(1,),
            in_specs=[own_spec] + [whole(a) for a in operands[1:]],
            out_specs=[whole(a) for a in outs],
            scratch_shapes=[
                pltpu.VMEM((length, length), jnp.float32),
                pltpu.VMEM((length, length), jnp.float32),
                pltpu.VMEM((1, length), jnp.float32),
                pltpu.VMEM((1, length), jnp.float32),
            ],
        ),
        compiler_params=pltpu.CompilerParams(vmem_limit_bytes=48 * MIB),
        cost_estimate=pl.CostEstimate(flops=1, bytes_accessed=1, transcendentals=0),
        name="attend",
    )(row_index, *operands)


def row_mean(values):
    return jnp.mean(values, -1, keepdims=True)


def normalise(values):
    centred = values - row_mean(values)
    scale = lax.rsqrt(row_mean(centred * centred) + EPSILON)
    return centred * scale, scale


def norm_back(grad, gain, normed, scale):
    entering = grad * gain
    return (entering - row_mean(entering) - normed * row_mean(entering * normed)) * scale


def gelu_parts(values):
    bell = jnp.exp2(values * values * (-0.5 * LOG2E))
    t = 1.0 / (1.0 + (0.3275911 * 0.5**0.5) * jnp.abs(values))
    poly = t * (
        0.5 * 0.254829592
        + t
        * (
            0.5 * -0.284496736
            + t * (0.5 * 1.421413741 + t * (0.5 * -1.453152027 + t * (0.5 * 1.061405429)))
        )
    )
    tail = poly * bell
    phi = jnp.where(values >= 0, 1.0 - tail, tail)
    return values * phi, phi + values * bell * 0.3989422804014327


def token_kernel(rows, pieces, steps, width, chunk, *refs):
    _, keep_ref, me_ref, refs = *refs[:3], refs[3:]
    own_tokens, own_cotangent, refs = *refs[:2], refs[2:]
    remote_count = rows * (pieces - 1)
    remote_tokens, refs = refs[:remote_count], refs[remote_count:]
    remote_cotangents, refs = refs[:remote_count], refs[remote_count:]
    context_refs, refs = refs[:rows], refs[rows:]
    (
        out_weight,
        out_bias,
        first_gain,
        first_shift,
        up_weight,
        up_bias,
        down_weight,
        down_bias,
        second_gain,
        second_shift,
    ) = refs[:10]
    refs = refs[10:]
    layer_outs, refs = refs[:pieces], refs[pieces:]
    (
        grad_out_heads,
        grad_first_out,
        packed_near,
        packed_far,
        tokens_scratch,
        cotangent_scratch,
        context_scratch,
        act_scratch,
        slope_scratch,
        totals,
        lines,
        *line_sums,
    ) = refs
    (
        grad_out_bias,
        grad_first_gain,
        grad_first_shift,
        grad_down_bias,
        grad_second_gain,
        grad_second_shift,
        grad_value_bias,
        grad_up_bias,
    ) = line_sums
    row_index = pl.program_id(0)
    piece_index = pl.program_id(1)
    step_index = pl.program_id(2)
    tokens_len, model = tokens_scratch.shape
    hidden_units = up_weight.shape[1]
    kept = keep_ref[row_index] != 0
    span = pl.ds(pl.multiple_of(step_index * tokens_len, tokens_len), tokens_len)

    @pl.when(piece_index == 0)
    def _():
        tokens_scratch[...] = own_tokens[0, span]
        cotangent_scratch[...] = own_cotangent[0, span]

    for row in range(rows):

        @pl.when(row_index == row)
        def _():
            context_scratch[...] = context_refs[row][...]

        for piece in range(1, pieces):

            @pl.when((row_index == row) & (piece_index == piece))
            def _():
                position = row * (pieces - 1) + piece - 1
                tokens_scratch[...] = remote_tokens[position][0, span]
                cotangent_scratch[...] = remote_cotangents[position][0, span]

    @pl.when((row_index == 0) & (piece_index == 0) & (step_index == 0))
    def _():
        for ref in (totals, lines, *line_sums):
            ref[...] = jnp.zeros(ref.shape, ref.dtype)

    def column_sum(values):
        return jnp.sum(values, 0, keepdims=True)

    tokens = tokens_scratch[...].astype(jnp.float32)
    context = context_scratch[...]
    context_low = context.astype(jnp.bfloat16)
    first_sum = tokens + (dot(context_low, out_weight[...], 0, 0) + out_bias[...])
    first_normed, first_scale = normalise(first_sum)
    hidden = first_normed * first_gain[...] + first_shift[...]
    hidden_low = hidden.astype(jnp.bfloat16)
    branch = down_bias[...]
    for start in range(0, hidden_units, chunk):
        units = pl.ds(start, chunk)
        pre_act = dot(hidden_low, up_weight[:, units], 1, 0) + up_bias[:, units]
        activated, slope = gelu_parts(pre_act)
        act_low = activated.astype(jnp.bfloat16)
        act_scratch[:, units] = act_low
        slope_scratch[:, units] = slope
        branch = branch + dot(act_low, down_weight[units, :], 1, 0)
    second_normed, second_scale = normalise(hidden + branch)
    result = jnp.where(
        kept, second_normed * second_gain[...] + second_shift[...], tokens
    ).astype(jnp.bfloat16)
    for piece in range(pieces):

        @pl.when(piece_index == piece)
        def _():
            layer_outs[piece][0, span] = result

    cotangent = cotangent_scratch[...].astype(jnp.float32)
    grad_out = jnp.where(kept, cotangent, 0.0)
    grad_second_gain[...] += column_sum(grad_out * second_normed)
    grad_second_shift[...] += column_sum(grad_out)
    grad_second = norm_back(grad_out, second_gain[...], second_normed, second_scale)
    grad_branch_low = grad_second.astype(jnp.bfloat16)
    grad_down_bias[...] += column_sum(grad_branch_low.astype(jnp.float32))
    grad_hidden = grad_second
    for start in range(0, hidden_units, chunk):
        units = pl.ds(start, chunk)
        grad_pre = dot(grad_branch_low, down_weight[units, :], 1, 1) * slope_scratch[:, units]
        grad_pre_low = grad_pre.astype(jnp.bfloat16)
        grad_up_bias[:, units] += column_sum(grad_pre_low.astype(jnp.float32))
        totals[units, :] += dot(hidden_low, grad_pre_low, 0, 0)
        totals[pl.ds(hidden_units + start, chunk), :] += dot(
            act_scratch[:, units], grad_branch_low, 0, 0
        )
        grad_hidden = grad_hidden + dot(grad_pre_low, up_weight[:, units], 1, 1)
    grad_first_gain[...] += column_sum(grad_hidden * first_normed)
    grad_first_shift[...] += column_sum(grad_hidden)
    grad_first = norm_back(grad_hidden, first_gain[...], first_normed, first_scale)
    grad_first_out[0] = jnp.where(kept, grad_first, cotangent)
    grad_attn_low = grad_first.astype(jnp.bfloat16)
    grad_out_bias[...] += column_sum(grad_attn_low.astype(jnp.float32))
    totals[pl.ds(2 * hidden_units, model), :] += dot(context_low, grad_attn_low, 1, 0)
    grad_context = dot(out_weight[...], grad_attn_low, 1, 1).astype(jnp.bfloat16)
    grad_context_wide = grad_context.astype(jnp.float32)
    ones = jnp.ones((EXTRA, tokens_len), jnp.bfloat16)
    grad_value_bias[...] += dot(ones, grad_context, 1, 1)[:1]
    product = grad_context_wide * context
    blank = jnp.zeros((EXTRA, tokens_len), jnp.float32)
    for head in range(HEADS):
        columns = slice(head * width, (head + 1) * width)
        grad_out_heads[0, head, :width] = grad_context[columns]
        spread = jnp.sum(product[columns], 0, keepdims=True)
        grad_out_heads[0, head, width:] = extra_rows(blank, -spread, 0).astype(jnp.bfloat16)

    @pl.when((row_index == rows - 1) & (piece_index == pieces - 1) & (step_index == steps - 1))
    def _():
        first = 0
        for ref in line_sums:
            set_lines(lines, first, ref[...])
            first += ref.shape[1] // LANES
        pack([totals], lines, packed_near, packed_far, me_ref[0])


def set_lines(lines, first, values):
    width = lines.shape[2]
    for block in range(values.shape[1] // width):
        slot, row = divmod(first + block, LINE_ROWS)
        lines[slot, row : row + 1] = values[:, block * width : (block + 1) * width]


def pack(parts, lines, near, far, me):
    half, size, width = near.shape
    columns = [(ref, start) for ref in parts for start in range(0, ref.shape[1], width)]
    height = parts[0].shape[0] // (2 * half)

    def one(slot, carry):
        for ref, first in ((near, 0), (far, half)):
            piece = (slot + first) ^ me
            rows = pl.ds(pl.multiple_of(piece * height, EXTRA), height)
            for block, (source, start) in enumerate(columns):
                ref[slot, pl.ds(block * height, height), :] = source[
                    rows, pl.ds(start, width)
                ].astype(jnp.bfloat16)
            ref[slot, pl.ds(len(columns) * height, EXTRA), :] = jnp.concatenate(
                [lines[piece], jnp.zeros_like(lines[piece])], 0
            ).astype(jnp.bfloat16)
        return carry

    lax.fori_loop(0, half, one, 0)


def packed_shape(slots, rows, model):
    return jax.ShapeDtypeStruct(
        (slots // 2, rows * (model // LANES) // slots + EXTRA, LANES), jnp.bfloat16
    )


def lines_shape(slots):
    return pltpu.VMEM((slots, EXTRA // 2, LANES), jnp.float32)


def by_token(
    row_index, keep, me, tokens, remote, cotangent, remote_cotangent, contexts, weights, slots
):
    rows = len(contexts)
    pieces = 1 + len(remote[0])
    local, model = tokens.shape[1:]
    length = pieces * local
    width = model // HEADS
    hidden_units = weights[4].shape[1]
    tokens_len = min(512, local)
    steps = local // tokens_len
    whole = lambda array: pl.BlockSpec(array.shape, lambda r, i, j, s, k, m: (0,) * array.ndim)
    own_spec = pl.BlockSpec((1, local, model), lambda r, i, j, s, k, m: (s[0] + r, 0, 0))
    f32 = lambda *shape: jax.ShapeDtypeStruct(shape, jnp.float32)
    total_rows = 2 * hidden_units + model
    packed = packed_shape(slots, total_rows, model)
    piece_out = jax.ShapeDtypeStruct((rows, local, model), jnp.bfloat16)
    gradient_outs = (packed, packed)
    line_lengths = [model] * 7 + [hidden_units]
    outs = (
        *([piece_out] * pieces),
        jax.ShapeDtypeStruct((rows, HEADS, width + EXTRA, length), jnp.bfloat16),
        f32(rows, length, model),
        *gradient_outs,
    )
    out_specs = (
        *([pl.BlockSpec((1, local, model), lambda r, i, j, s, k, m: (r, 0, 0))] * pieces),
        pl.BlockSpec(
            (1, HEADS, width + EXTRA, tokens_len),
            lambda r, i, j, s, k, m: (r, 0, 0, i * steps + j),
        ),
        pl.BlockSpec((1, tokens_len, model), lambda r, i, j, s, k, m: (r, i * steps + j, 0)),
        *[whole(a) for a in gradient_outs],
    )

    def context_spec(row):
        def block(r, i, j, s, k, m):
            step = i * steps + j
            return 0, jnp.where(r < row, 0, jnp.where(r > row, pieces * steps - 1, step))

        return pl.BlockSpec((model, tokens_len), block)

    flat_remote = [array for arrays in remote for array in arrays]
    flat_remote_cotangent = [array for arrays in remote_cotangent for array in arrays]
    in_specs = (
        own_spec,
        own_spec,
        *[whole(a) for a in (*flat_remote, *flat_remote_cotangent)],
        *[context_spec(row) for row in range(rows)],
        *[whole(a) for a in weights],
    )
    return pl.pallas_call(
        functools.partial(token_kernel, rows, pieces, steps, width, min(model, hidden_units)),
        out_shape=outs,
        grid_spec=pltpu.PrefetchScalarGridSpec(
            num_scalar_prefetch=3,
            grid=(rows, pieces, steps),
            in_specs=in_specs,
            out_specs=out_specs,
            scratch_shapes=[
                pltpu.VMEM((tokens_len, model), jnp.bfloat16),
                pltpu.VMEM((tokens_len, model), jnp.bfloat16),
                pltpu.VMEM((model, tokens_len), jnp.float32),
                pltpu.VMEM((tokens_len, hidden_units), jnp.bfloat16),
                pltpu.VMEM((tokens_len, hidden_units), jnp.float32),
                pltpu.VMEM((total_rows, model), jnp.float32),
                lines_shape(slots),
                *[pltpu.VMEM((1, n), jnp.float32) for n in line_lengths],
            ],
        ),
        compiler_params=pltpu.CompilerParams(vmem_limit_bytes=60 * MIB),
        cost_estimate=pl.CostEstimate(flops=1, bytes_accessed=1, transcendentals=0),
        name="by_token",
    )(
        row_index,
        keep,
        me,
        tokens,
        cotangent,
        *flat_remote,
        *flat_remote_cotangent,
        *contexts,
        *weights,
    )


def attend_back_kernel(pieces, width, block, last_row, last_part, *refs):
    _, me_ref, refs = *refs[:2], refs[2:]
    token_refs, refs = refs[:pieces], refs[pieces:]
    head_refs, refs = refs[:4], refs[4:]
    grad_tokens_in, query_weight, key_weight, value_weight, totals_in, bias_in = refs[:6]
    refs = refs[6:]
    earlier = 0
    packing = last_row and last_part
    if packing:
        earlier = (len(refs) - (pieces + 2 + 6)) // 2
    earlier_totals, refs = refs[:earlier], refs[earlier:]
    earlier_biases, refs = refs[:earlier], refs[earlier:]
    outs = pieces if last_part else 1
    grad_tokens, refs = refs[:outs], refs[outs:]
    if packing:
        packed_near, packed_far, *refs, lines, totals, bias = refs
    else:
        totals, bias, *refs = refs
    grad_query_scratch, grad_key_scratch, grad_value_scratch = refs
    query_ref, key_ref, value_ref, grad_ref = (ref.at[0] for ref in head_refs)
    heads, _, length = query_ref.shape
    local = length // pieces
    pair_width = 2 * width
    model = query_weight.shape[0]

    def head_pair(pair, carry):
        grad_queries = [[], []]
        for side in range(2):
            head = pair * 2 + side
            key = key_ref[head]
            value = value_ref[head]
            grad_key = 0.0
            grad_value = 0.0
            for start in range(0, length, block):
                span = pl.ds(start, block)
                query = query_ref[head, :, span]
                grad = grad_ref[head, :, span]
                weights = jnp.exp2(dot(query, key, 0, 0))
                grad_weights = dot(grad, value, 0, 0)
                weights_low = weights.astype(jnp.bfloat16)
                grad_scores = (weights * grad_weights).astype(jnp.bfloat16)
                grad_value = grad_value + dot(grad[:width], weights_low, 1, 0)
                grad_key = grad_key + dot(query[:width], grad_scores, 1, 0)
                grad_queries[side].append(dot(grad_scores, key[:width], 1, 1))
            rows = pl.ds(pl.multiple_of(head * width, width), width)
            grad_value_scratch[rows, :] = grad_value.astype(jnp.bfloat16)
            grad_key_scratch[rows, :] = (grad_key * LN2).astype(jnp.bfloat16)
        for index, start in enumerate(range(0, length, block)):
            both = jnp.concatenate([grad_queries[0][index], grad_queries[1][index]], 1)
            grad_query_scratch[pair, pl.ds(start, block)] = (both * width**-0.5).astype(
                jnp.bfloat16
            )
        return carry

    lax.fori_loop(0, heads // 2, head_pair, 0)
    for pair in range(heads // 2):
        columns = pl.ds(pair * pair_width, pair_width)
        bias[:, columns] = bias_in[:, columns] + column_sum(
            grad_query_scratch[pair].astype(jnp.float32)
        )
    for piece in range(pieces):
        span = pl.ds(piece * local, local)
        tokens = token_refs[piece][0]
        grad_query = jnp.concatenate([grad_query_scratch[pair, span] for pair in range(heads // 2)], 1)
        grad_key = grad_key_scratch[:, span]
        grad_value = grad_value_scratch[:, span]
        for position, term in enumerate(
            (
                dot(tokens, grad_query, 0, 0),
                dot(tokens, grad_key, 0, 1),
                dot(tokens, grad_value, 0, 1),
            )
        ):
            part = pl.ds(position * model, model)
            totals[part, :] = (totals_in if piece == 0 else totals)[part, :] + term
        total = (
            grad_tokens_in[0, span]
            + dot(grad_query, query_weight[...], 1, 1)
            + dot(grad_key, key_weight[...], 0, 1)
            + dot(grad_value, value_weight[...], 0, 1)
        )
        if last_part:
            grad_tokens[piece][0] = total.astype(jnp.bfloat16)
        else:
            grad_tokens[0][0, span] = total
    if packing:
        lines[...] = jnp.zeros(lines.shape, lines.dtype)
        first = 0
        for ref in (*earlier_biases, bias):
            set_lines(lines, first, ref[...])
            first += ref.shape[1] // LANES
        pack([*earlier_totals, totals], lines, packed_near, packed_far, me_ref[0])


def attend_back(
    place, row_index, me, tokens, remote, heads, grad_tokens, weights, totals, biases, slots
):
    row, rows, part, parts = place
    last_row, last_part = row == rows - 1, part == parts - 1
    pieces = 1 + len(remote)
    local, model = tokens.shape[1:]
    length = pieces * local
    width = model // HEADS
    columns = model // parts
    whole = lambda array: pl.BlockSpec(array.shape, lambda i, s, m: (0,) * array.ndim)
    own_spec = pl.BlockSpec((1, local, model), lambda i, s, m: (s[0], 0, 0))
    head_spec = lambda array: pl.BlockSpec(
        (1, HEADS // parts, *array.shape[2:]),
        lambda i, s, m: (row if array.shape[0] > 1 else 0, part, 0, 0),
    )
    grad_spec = pl.BlockSpec(
        (1, length, model), lambda i, s, m: (row if grad_tokens.shape[0] > 1 else 0, 0, 0)
    )
    weight_spec = pl.BlockSpec((model, columns), lambda i, s, m: (0, part))
    f32 = lambda *shape: jax.ShapeDtypeStruct(shape, jnp.float32)
    if last_part:
        outs = [jax.ShapeDtypeStruct((1, local, model), jnp.bfloat16)] * pieces
    else:
        outs = [f32(1, length, model)]
    scratch = [
        pltpu.VMEM((HEADS // parts // 2, length, 2 * width), jnp.bfloat16),
        pltpu.VMEM((columns, length), jnp.bfloat16),
        pltpu.VMEM((columns, length), jnp.bfloat16),
    ]
    own_sums = [totals[part], biases[part]]
    others = []
    if last_row and last_part:
        outs += [packed_shape(slots, 3 * model, model)] * 2
        scratch += [lines_shape(slots), *[pltpu.VMEM(a.shape, jnp.float32) for a in own_sums]]
        others = [*totals[:part], *biases[:part]]
    else:
        outs += [f32(*a.shape) for a in own_sums]
    after = [*own_sums, *others]
    return pl.pallas_call(
        functools.partial(
            attend_back_kernel, pieces, width, min(256, length), last_row, last_part
        ),
        out_shape=outs,
        grid_spec=pltpu.PrefetchScalarGridSpec(
            num_scalar_prefetch=2,
            grid=(1,),
            in_specs=[
                own_spec,
                *[whole(a) for a in remote],
                *[head_spec(a) for a in heads],
                grad_spec,
                *[weight_spec] * 3,
                *[whole(a) for a in after],
            ],
            out_specs=[whole(a) for a in outs],
            scratch_shapes=scratch,
        ),
        compiler_params=pltpu.CompilerParams(vmem_limit_bytes=48 * MIB),
        cost_estimate=pl.CostEstimate(flops=4 * 10**9, bytes_accessed=1, transcendentals=0),
        name="attend_back",
    )(row_index, me, tokens, *remote, *heads, grad_tokens, *weights, *after)


def unpack_kernel(moves, line_count, me_ref, near, far, *outs):
    half, size, width = near.shape
    mine = lax.rem(me_ref[0], half)
    for side in range(2):

        @pl.when(me_ref[0] // half == side)
        def _():
            def rows_of(piece, start, rows):
                source = near if piece // half == side else far
                return source[(piece % half) ^ mine, pl.ds(start, rows), :].astype(jnp.float32)

            for piece, start, rows, out, row, column in moves:
                outs[out][pl.ds(row, rows), pl.ds(column, width)] = rows_of(piece, start, rows)
            blocks = outs[-1].shape[1] // width
            for index in range(line_count * blocks):
                line, block = divmod(index, blocks)
                piece, row = divmod(index, LINE_ROWS)
                outs[-1][line : line + 1, pl.ds(block * width, width)] = rows_of(
                    piece, size - EXTRA, EXTRA
                )[row : row + 1]


def unpack(me, near, far, shapes, model, line_count):
    half, size, width = near.shape
    blocks = model // width
    height = (size - EXTRA) // blocks
    squares = [
        (out, row, column)
        for out, shape in enumerate(shapes)
        for row in range(0, shape[0], model)
        for column in range(0, shape[1], model)
    ]
    moves = []
    for piece in range(2 * half):
        done = 0
        while done < height:
            square, inside = divmod(piece * height + done, model)
            rows = min(height - done, model - inside)
            out, row, column = squares[square]
            for block in range(blocks):
                moves.append(
                    (piece, block * height + done, rows, out, row + inside, column + block * width)
                )
            done += rows
    outs = [jax.ShapeDtypeStruct(shape, jnp.float32) for shape in (*shapes, (line_count, model))]
    whole = lambda array: pl.BlockSpec(array.shape, lambda i, m: (0,) * array.ndim)
    return pl.pallas_call(
        functools.partial(unpack_kernel, moves, line_count),
        out_shape=outs,
        grid_spec=pltpu.PrefetchScalarGridSpec(
            num_scalar_prefetch=1,
            grid=(1,),
            in_specs=[whole(near), whole(far)],
            out_specs=[whole(a) for a in outs],
        ),
        compiler_params=pltpu.CompilerParams(vmem_limit_bytes=60 * MIB),
        cost_estimate=pl.CostEstimate(flops=1, bytes_accessed=1, transcendentals=0),
        name="unpack",
    )(me, near, far)


NEAR, MIDDLE, FAR, SEQ = AXES = ("near", "middle", "far", "seq")
STAGES = ((NEAR,), (MIDDLE, SEQ), (FAR,))


def add_up(arrays):
    return functools.reduce(jnp.add, [a.astype(jnp.float32) for a in arrays]).astype(jnp.bfloat16)


def after(arrays, *others):
    return lax.optimization_barrier((arrays, others))[0]


class Sums:
    def __init__(self):
        self.sizes = [lax.axis_size(axes) for axes in STAGES]
        self.devices = math.prod(self.sizes)
        digits = [lax.axis_index(axes) for axes in STAGES]
        self.me = (digits[0] * self.sizes[1] + digits[1]) * self.sizes[2] + digits[2]

    def swap(self, array, stage, turn):
        pairs = [(i, i ^ turn) for i in range(self.sizes[stage])]
        return lax.ppermute(array, STAGES[stage], pairs)

    def meet(self, parts, stage):
        return [parts[0], *[self.swap(parts[t], stage, t) for t in range(1, len(parts))]]

    def add_parts(self, arrays, stage):
        size = self.sizes[stage]
        share = arrays[0].shape[0] // size
        return [
            add_up([array[turn * share : (turn + 1) * share] for array in arrays])
            for turn in range(size)
        ]

    def spread(self, held, stage):
        others = [self.swap(held, stage, turn) for turn in range(1, self.sizes[stage])]
        return jnp.concatenate([held, *others], 0)


def norm_rows(values, gain, shift):
    row_mean = jnp.mean(values, -1, keepdims=True)
    centred = values - row_mean
    variance = jnp.mean(centred * centred, -1, keepdims=True)
    return centred * lax.rsqrt(variance + EPSILON) * gain + shift


def gelu_exact(values):
    return jax.nn.gelu(values, approximate=False)


def plain_dot(left, right):
    return jnp.dot(left, right, preferred_element_type=jnp.float32)


def left_dot(left, right):
    return lax.dot_general(
        left, right, (((0,), (0,)), ((), ())), preferred_element_type=jnp.float32
    )


def right_dot(left, right):
    return lax.dot_general(
        left, right, (((1,), (1,)), ((), ())), preferred_element_type=jnp.float32
    )


def column_sum(values):
    return jnp.sum(values.astype(jnp.float32), 0)


def split_heads(values, piece_len):
    return values.reshape(values.shape[0], piece_len, HEADS, values.shape[2] // HEADS)


def block_length(piece_len, local_len):
    return math.gcd(math.gcd(piece_len, local_len), BLOCK_CAP)


def masked_scores(query_heads, key_heads, query_ids, key_ids, score_scale):
    scores = (
        jnp.einsum("rqhd,rkhd->rhqk", query_heads, key_heads, preferred_element_type=jnp.float32)
        * score_scale
    )
    same_doc = query_ids[:, None, :, None] == key_ids[:, None, None, :]
    return jnp.where(same_doc, scores, NEG_FILL)


def split_attend_back(
    query_heads,
    grad_heads,
    log_total,
    spread,
    query_ids,
    key_heads,
    value_heads,
    key_ids,
    score_scale,
):
    scores = masked_scores(query_heads, key_heads, query_ids, key_ids, score_scale)
    weights = jnp.exp(scores - jnp.transpose(log_total, (0, 2, 1))[..., None])
    grad_value = jnp.einsum(
        "rhqk,rqhd->rkhd",
        weights.astype(jnp.bfloat16),
        grad_heads,
        preferred_element_type=jnp.float32,
    )
    grad_weights = jnp.einsum(
        "rqhd,rkhd->rhqk", grad_heads, value_heads, preferred_element_type=jnp.float32
    )
    grad_scores = (weights * (grad_weights - jnp.transpose(spread, (0, 2, 1))[..., None])).astype(
        jnp.bfloat16
    )
    grad_query = (
        jnp.einsum("rhqk,rkhd->rqhd", grad_scores, key_heads, preferred_element_type=jnp.float32)
        * score_scale
    )
    grad_key = (
        jnp.einsum("rhqk,rqhd->rkhd", grad_scores, query_heads, preferred_element_type=jnp.float32)
        * score_scale
    )
    return (grad_query, grad_key, grad_value)


def add_into(buffer, term, block_start):
    current = lax.dynamic_slice_in_dim(buffer, block_start, term.shape[1], 1)
    return lax.dynamic_update_slice_in_dim(buffer, current + term, block_start, 1)


def split_rows(
    tokens,
    segments,
    keep_flags,
    query_weight,
    query_bias,
    key_weight,
    value_weight,
    value_bias,
    out_weight,
    out_bias,
    first_gain,
    first_shift,
    up_weight,
    up_bias,
    down_weight,
    down_bias,
    second_gain,
    second_shift,
    cotangent,
):
    row_count, local_tokens, model_width = tokens.shape
    head_width = model_width // HEADS
    score_scale = head_width ** (-0.5)
    flat_tokens = tokens.reshape(row_count * local_tokens, model_width)
    row_shape = (row_count, local_tokens, model_width)
    query_low = (
        (plain_dot(flat_tokens, query_weight) + query_bias).astype(jnp.bfloat16).reshape(row_shape)
    )
    key_low = plain_dot(flat_tokens, key_weight).astype(jnp.bfloat16).reshape(row_shape)
    value_low = (
        (plain_dot(flat_tokens, value_weight) + value_bias).astype(jnp.bfloat16).reshape(row_shape)
    )
    query_heads = split_heads(query_low, local_tokens)
    own_start = lax.axis_index("seq") * local_tokens
    own_ids = lax.dynamic_slice_in_dim(segments, own_start, local_tokens, 1)
    initial = (
        jnp.full((row_count, HEADS, local_tokens), NEG_FILL, jnp.float32),
        jnp.zeros((row_count, HEADS, local_tokens), jnp.float32),
        jnp.zeros((row_count, HEADS, local_tokens, head_width), jnp.float32),
    )
    key_piece = lax.all_gather(key_low, "seq", axis=1, tiled=True)
    value_piece = lax.all_gather(value_low, "seq", axis=1, tiled=True)
    block_size = block_length(key_piece.shape[1], local_tokens)

    def key_step(position, inner_state):
        running_max, running_sum, running_acc = inner_state
        block_start = position * block_size
        key_heads = split_heads(
            lax.dynamic_slice_in_dim(key_piece, block_start, block_size, 1), block_size
        )
        value_heads = split_heads(
            lax.dynamic_slice_in_dim(value_piece, block_start, block_size, 1), block_size
        )
        key_ids = lax.dynamic_slice_in_dim(segments, block_start, block_size, 1)
        scores = masked_scores(query_heads, key_heads, own_ids, key_ids, score_scale)
        newest = jnp.maximum(running_max, jnp.max(scores, -1))
        factor = jnp.exp(running_max - newest)
        weights = jnp.exp(scores - newest[..., None])
        running_sum = running_sum * factor + jnp.sum(weights, -1)
        update = jnp.einsum(
            "rhqk,rkhd->rhqd",
            weights.astype(jnp.bfloat16),
            value_heads,
            preferred_element_type=jnp.float32,
        )
        return (newest, running_sum, running_acc * factor[..., None] + update)

    running_max, running_sum, running_acc = lax.fori_loop(
        0, key_piece.shape[1] // block_size, key_step, initial
    )
    context_heads = jnp.transpose(running_acc / running_sum[..., None], (0, 2, 1, 3))
    log_total = jnp.transpose(running_max + jnp.log(running_sum), (0, 2, 1))
    context_low = context_heads.reshape(row_count * local_tokens, model_width).astype(jnp.bfloat16)
    first_sum = flat_tokens.astype(jnp.float32) + (plain_dot(context_low, out_weight) + out_bias)
    hidden, first_back = jax.vjp(norm_rows, first_sum, first_gain, first_shift)
    hidden_low = hidden.astype(jnp.bfloat16)
    pre_act = plain_dot(hidden_low, up_weight) + up_bias
    activated, act_back = jax.vjp(gelu_exact, pre_act)
    act_low = activated.astype(jnp.bfloat16)
    second_sum = hidden + (plain_dot(act_low, down_weight) + down_bias)
    normed, second_back = jax.vjp(norm_rows, second_sum, second_gain, second_shift)
    kept_rows = (keep_flags != 0)[:, None, None]
    layer_out = jnp.where(kept_rows, normed.reshape(row_shape), tokens.astype(jnp.float32)).astype(
        jnp.bfloat16
    )
    grad_out = jnp.where(kept_rows, cotangent.astype(jnp.float32), 0.0).reshape(
        row_count * local_tokens, model_width
    )
    grad_second, grad_second_gain, grad_second_shift = second_back(grad_out)
    grad_branch_low = grad_second.astype(jnp.bfloat16)
    grad_down_bias = column_sum(grad_branch_low)
    grad_down_weight = left_dot(act_low, grad_branch_low)
    (grad_pre,) = act_back(right_dot(grad_branch_low, down_weight))
    grad_pre_low = grad_pre.astype(jnp.bfloat16)
    grad_up_bias = column_sum(grad_pre_low)
    grad_up_weight = left_dot(hidden_low, grad_pre_low)
    grad_hidden = grad_second + right_dot(grad_pre_low, up_weight)
    grad_first, grad_first_gain, grad_first_shift = first_back(grad_hidden)
    grad_attn_low = grad_first.astype(jnp.bfloat16)
    grad_out_bias = column_sum(grad_attn_low)
    grad_out_weight = left_dot(context_low, grad_attn_low)
    late_grads = (
        grad_out_weight,
        grad_out_bias,
        grad_first_gain,
        grad_first_shift,
        grad_up_weight,
        grad_up_bias,
        grad_down_weight,
        grad_down_bias,
        grad_second_gain,
        grad_second_shift,
    )
    grad_context_low = right_dot(grad_attn_low, out_weight).astype(jnp.bfloat16)
    grad_context_rows = grad_context_low.reshape(row_shape)
    grad_heads = split_heads(grad_context_rows, local_tokens)
    spread = jnp.sum(grad_heads.astype(jnp.float32) * context_heads, -1)
    zero_local = jnp.zeros((row_count, local_tokens, HEADS, head_width), jnp.float32)
    zero_whole = jnp.zeros(
        (row_count, local_tokens * lax.axis_size("seq"), HEADS, head_width), jnp.float32
    )
    gathered_total, gathered_spread = (
        lax.all_gather(log_total, "seq", axis=1, tiled=True),
        lax.all_gather(spread, "seq", axis=1, tiled=True),
    )
    key_heads_local = split_heads(key_low, local_tokens)
    value_heads_local = split_heads(value_low, local_tokens)
    query_piece = lax.all_gather(query_low, "seq", axis=1, tiled=True)
    grad_piece = lax.all_gather(grad_context_rows, "seq", axis=1, tiled=True)
    back_block_size = block_length(query_piece.shape[1], local_tokens)

    def query_step(position, inner_state):
        grad_key, grad_value, queries_whole = inner_state
        block_start = position * back_block_size
        part_query, part_key, part_value = split_attend_back(
            split_heads(
                lax.dynamic_slice_in_dim(query_piece, block_start, back_block_size, 1),
                back_block_size,
            ),
            split_heads(
                lax.dynamic_slice_in_dim(grad_piece, block_start, back_block_size, 1),
                back_block_size,
            ),
            lax.dynamic_slice_in_dim(gathered_total, block_start, back_block_size, 1),
            lax.dynamic_slice_in_dim(gathered_spread, block_start, back_block_size, 1),
            lax.dynamic_slice_in_dim(segments, block_start, back_block_size, 1),
            key_heads_local,
            value_heads_local,
            own_ids,
            score_scale,
        )
        return (
            grad_key + part_key,
            grad_value + part_value,
            add_into(queries_whole, part_query, block_start),
        )

    grad_key, grad_value, queries_whole = lax.fori_loop(
        0, query_piece.shape[1] // back_block_size, query_step, (zero_local, zero_local, zero_whole)
    )
    grad_query = lax.psum_scatter(queries_whole, "seq", scatter_dimension=1, tiled=True)
    flat_shape = (row_count * local_tokens, model_width)
    grad_query_low = grad_query.reshape(flat_shape).astype(jnp.bfloat16)
    grad_key_low = grad_key.reshape(flat_shape).astype(jnp.bfloat16)
    grad_value_low = grad_value.reshape(flat_shape).astype(jnp.bfloat16)
    grad_query_bias = column_sum(grad_query_low)
    grad_query_weight = left_dot(flat_tokens, grad_query_low)
    grad_key_weight = left_dot(flat_tokens, grad_key_low)
    grad_value_bias = column_sum(grad_value_low)
    grad_value_weight = left_dot(flat_tokens, grad_value_low)
    grad_flat = (
        grad_first
        + right_dot(grad_query_low, query_weight)
        + right_dot(grad_key_low, key_weight)
        + right_dot(grad_value_low, value_weight)
    )
    tokens_grad = jnp.where(
        kept_rows, grad_flat.reshape(row_shape), cotangent.astype(jnp.float32)
    ).astype(jnp.bfloat16)
    early_grads = (
        grad_query_weight,
        grad_query_bias,
        grad_key_weight,
        grad_value_weight,
        grad_value_bias,
    )
    summed = lax.psum(
        (
            grad_query_weight,
            grad_query_bias,
            grad_key_weight,
            grad_value_weight,
            grad_value_bias,
            grad_out_weight,
            grad_out_bias,
            grad_first_gain,
            grad_first_shift,
            grad_up_weight,
            grad_up_bias,
            grad_down_weight,
            grad_down_bias,
            grad_second_gain,
            grad_second_shift,
        ),
        ("dp", "seq"),
    )
    early_grads = summed[:5]
    late_grads = summed[5:]
    return (
        layer_out,
        tokens_grad,
        early_grads[0],
        early_grads[1],
        early_grads[2],
        early_grads[3],
        early_grads[4],
        late_grads[0],
        late_grads[1],
        late_grads[2],
        late_grads[3],
        late_grads[4],
        late_grads[5],
        late_grads[6],
        late_grads[7],
        late_grads[8],
        late_grads[9],
    )


def deal_rows(
    tokens,
    segments,
    keep_flags,
    query_weight,
    query_bias,
    key_weight,
    value_weight,
    value_bias,
    out_weight,
    out_bias,
    first_gain,
    first_shift,
    up_weight,
    up_bias,
    down_weight,
    down_bias,
    second_gain,
    second_shift,
    cotangent,
):
    row_count, local_tokens, model = tokens.shape
    ring = lax.axis_size("seq")
    me = lax.axis_index("seq")
    rows = row_count // ring
    first_row = me * rows
    turns = [[(i, (i + turn) % ring) for i in range(ring)] for turn in range(ring)]
    back_turns = [[(i, (i - turn) % ring) for i in range(ring)] for turn in range(ring)]

    def fetch(array, row, turn):
        theirs = lax.rem(me + turn, ring) * rows + row
        sent = lax.dynamic_slice_in_dim(array, theirs, 1, 0)
        return lax.ppermute(sent, "seq", turns[turn])

    remote = [[fetch(tokens, row, turn) for turn in range(1, ring)] for row in range(rows)]
    remote_cotangent = [
        [fetch(cotangent, row, turn) for turn in range(1, ring)] for row in range(rows)
    ]
    own_segments = lax.dynamic_slice_in_dim(segments, first_row, rows, 0)
    own_segments = jnp.concatenate(
        [
            lax.dynamic_slice_in_dim(
                own_segments, lax.rem(me - turn + ring, ring) * local_tokens, local_tokens, 1
            )
            for turn in range(ring)
        ],
        1,
    )
    extra_index = jnp.arange(EXTRA, dtype=jnp.int32)[None, :, None]
    same = own_segments[:, None, :] == extra_index
    query_extra = jnp.where(same & (extra_index < 3), 1.0, 0.0)
    key_extra = jnp.where(
        extra_index < 3, jnp.where(same, 0.0, NEG_FILL), jnp.where(extra_index < 6, 1.0, 0.0)
    )
    keep = lax.dynamic_slice_in_dim(keep_flags, first_row, rows, 0)
    line = lambda vector: vector.reshape(1, -1)
    column = lambda vector: vector.reshape(-1, 1)
    forward_weights = (
        query_weight,
        column(query_bias),
        key_weight,
        value_weight,
        column(value_bias),
    )
    token_weights = (
        out_weight,
        line(out_bias),
        line(first_gain),
        line(first_shift),
        up_weight,
        line(up_bias),
        down_weight,
        line(down_bias),
        line(second_gain),
        line(second_shift),
    )
    back_weights = (query_weight, key_weight, value_weight)
    row_index = [(first_row + row).reshape(1) for row in range(rows)]
    sums = Sums()
    number, slots = sums.me.reshape(1), sums.devices
    heads, contexts = [], []
    for row in range(rows):
        if row:
            remote[row] = after(remote[row], contexts[-1])
        query, key, value, context = attend(
            row_index[row], tokens, remote[row], query_extra[row], key_extra[row], forward_weights
        )
        heads.append((query, key, value))
        contexts.append(context)
    remote_cotangent = after(remote_cotangent, contexts[-1])
    results = by_token(
        row_index[0],
        keep,
        number,
        tokens,
        remote,
        cotangent,
        remote_cotangent,
        contexts,
        token_weights,
        slots,
    )
    layer_outs, results = results[:ring], results[ring:]
    grad_heads, grad_first, late_near, late_far = results
    def give_back(parts, *before):
        return [
            part if turn == 0 else lax.ppermute(after(part, *before), "seq", back_turns[turn])
            for turn, part in enumerate(parts)
        ]

    def place(moved):
        by_turn = [jnp.concatenate(parts, 0) for parts in zip(*moved)]
        places = [
            [by_turn[(slot - index) % ring] for slot in range(ring)] for index in range(ring)
        ]
        whole = jnp.concatenate(places[0], 0)
        for index in range(1, ring):
            whole = jnp.where(me == index, jnp.concatenate(places[index], 0), whole)
        return whole

    late = sums.add_parts([late_near, sums.swap(late_far, 0, 1)], 1)
    parts = 2
    totals = [jnp.zeros((3 * model, model // parts), jnp.float32)] * parts
    biases = [jnp.zeros((1, model // parts), jnp.float32)] * parts
    tokens_grads = []
    here = after(number, *late)
    late = sums.meet(late, 1)
    for row in range(rows):
        grad_tokens = grad_first
        for part in range(parts):
            results = attend_back(
                (row, rows, part, parts),
                row_index[row],
                here,
                tokens,
                remote[row],
                (*heads[row], grad_heads),
                grad_tokens,
                back_weights,
                totals,
                biases,
                slots,
            )
            if part == parts - 1:
                tokens_grads.append(give_back(results[:ring]))
                results = results[ring:]
            else:
                grad_tokens, *results = results
            if row < rows - 1 or part < parts - 1:
                totals[part], biases[part] = results
            if row == rows - 1 and part == 0:
                late = add_up(after(late, totals[0]))
                here = after(number, late, layer_outs[0])
        if row == 0:
            late = sums.add_parts(after(late, totals[1]), 2)
            here = after(number, *late)
            layer_outs = [
                give_back([part[row : row + 1] for part in layer_outs], *late)
                for row in range(rows)
            ]
            late = sums.meet(late, 2)
    late = sums.spread(late, 2)
    results = after(results, late, *layer_outs[1:], *tokens_grads[:-1])
    early = sums.add_parts([results[0], sums.swap(results[1], 0, 1)], 1)
    late = sums.spread(after(late, *early), 1)
    early = sums.add_parts(sums.meet(early, 1), 2)
    early = add_up(sums.meet(early, 2))
    early = sums.spread(early, 2)
    layer_out = place(layer_outs)
    late, tokens_grads, early = after((late, tokens_grads, early), early, layer_out)
    tokens_grad = place(tokens_grads)
    early = sums.spread(early, 1)
    late = (late, sums.swap(late, 0, 1))
    hidden_units = up_weight.shape[1]
    lines = 7 + hidden_units // model
    grad_up, grad_down, grad_out_weight, late_lines = unpack(
        number, *late, [(model, hidden_units), (hidden_units, model), (model, model)], model, lines
    )
    early = (early, after(sums.swap(early, 0, 1), late_lines, tokens_grad))
    grad_query, grad_key, grad_value, early_lines = unpack(
        number, *early, [(model, model)] * 3, model, 1
    )

    (
        grad_out_bias,
        grad_first_gain,
        grad_first_shift,
        grad_down_bias,
        grad_second_gain,
        grad_second_shift,
        grad_value_bias,
    ) = [late_lines[i] for i in range(7)]
    grad_up_bias = late_lines[7:].reshape(-1)
    return (
        layer_out,
        tokens_grad,
        grad_query,
        early_lines[0],
        grad_key,
        grad_value,
        grad_value_bias,
        grad_out_weight,
        grad_out_bias,
        grad_first_gain,
        grad_first_shift,
        grad_up,
        grad_up_bias,
        grad_down,
        grad_down_bias,
        grad_second_gain,
        grad_second_shift,
    )


def solution(mesh):
    dp, ring = mesh.shape["dp"], mesh.shape["seq"]

    def placed(function, mesh, rows):
        return jax.shard_map(
            function,
            mesh=mesh,
            in_specs=(
                P(rows, "seq", None),
                P(rows, None),
                P(rows),
                *([P()] * 15),
                P(rows, "seq", None),
            ),
            out_specs=(P(rows, "seq", None), P(rows, "seq", None), *([P()] * 15)),
            check_vma=False,
        )

    def layer(tokens, *others):
        row_count, model = tokens.shape[0] // dp, tokens.shape[2]
        powers = dp & (dp - 1) == 0 and ring & (ring - 1) == 0 and dp >= 4
        if not powers or row_count % ring or model % (16 * dp * ring):
            return placed(split_rows, mesh, "dp")(tokens, *others)
        axes = (FAR, MIDDLE, NEAR)
        finer = jax.sharding.Mesh(mesh.devices.reshape(dp // 4, 2, 2, ring), (*axes, SEQ))
        return placed(deal_rows, finer, axes)(tokens, *others)

    return layer
```

```python
import functools
import math

import jax
import jax.numpy as jnp
from jax import lax
from jax.experimental import pallas as pl
from jax.experimental.pallas import tpu as pltpu
from jax.sharding import PartitionSpec as P

HEADS = 8
EXTRA = 16
LANES = 128
LINE_ROWS = 2
NEG_FILL = -1e30
EPSILON = 1e-05
BLOCK_CAP = 512
LOG2E = 1.4426950408889634
LN2 = 0.6931471805599453
MIB = 1 << 20


def dot(left, right, left_dim, right_dim):
    return lax.dot_general(
        left, right, (((left_dim,), (right_dim,)), ((), ())), preferred_element_type=jnp.float32
    )


def three_parts(values):
    high = values.astype(jnp.bfloat16)
    rest = values - high.astype(jnp.float32)
    middle = rest.astype(jnp.bfloat16)
    low = (rest - middle.astype(jnp.float32)).astype(jnp.bfloat16)
    return high.astype(jnp.float32), middle.astype(jnp.float32), low.astype(jnp.float32)


def extra_rows(base, values, first):
    row = lax.broadcasted_iota(jnp.int32, base.shape, 0)
    for offset, part in enumerate(three_parts(values)):
        base = jnp.where(row == first + offset, part, base)
    return base


def attend_kernel(pieces, width, block, *refs):
    _, refs = refs[0], refs[1:]
    token_refs, refs = refs[:pieces], refs[pieces:]
    (
        query_extra,
        key_extra,
        query_weight,
        query_bias,
        key_weight,
        value_weight,
        value_bias,
        query_out,
        key_out,
        value_out,
        context_out,
        scores_even,
        scores_odd,
        largest_even,
        largest_odd,
    ) = refs
    query_out, key_out, value_out = (ref.at[0] for ref in (query_out, key_out, value_out))
    length = query_out.shape[2]
    local = length // pieces
    for piece in range(pieces):
        span = pl.ds(piece * local, local)
        tokens = token_refs[piece][0]
        query = (dot(query_weight[...], tokens, 0, 1) + query_bias[...]) * (LOG2E * width**-0.5)
        query_out[:, :width, span] = query.astype(jnp.bfloat16).reshape(HEADS, width, local)
        key = dot(key_weight[...], tokens, 0, 1)
        key_out[:, :width, span] = key.astype(jnp.bfloat16).reshape(HEADS, width, local)
        value = dot(value_weight[...], tokens, 0, 1) + value_bias[...]
        value_out[:, :width, span] = value.astype(jnp.bfloat16).reshape(HEADS, width, local)
    row = lax.broadcasted_iota(jnp.int32, (EXTRA, length), 0)
    ones = (row < 3).astype(jnp.bfloat16)
    query_base = query_extra[...]
    for head in range(HEADS):
        query_out[head, width:] = query_base.astype(jnp.bfloat16)
        key_out[head, width:] = key_extra[...].astype(jnp.bfloat16)
        value_out[head, width:] = ones

    def score(head, scores_ref, largest_ref, start):
        span = pl.ds(start, block)
        scores = dot(key_out[head], query_out[head, :, span], 0, 0)
        scores_ref[:, span] = scores
        largest_ref[:, span] = jnp.max(scores, 0, keepdims=True)

    def weigh(head, scores_ref, largest_ref, start):
        span = pl.ds(start, block)
        largest = largest_ref[:, span]
        weights = jnp.exp2(scores_ref[:, span] - largest).astype(jnp.bfloat16)
        update = dot(value_out[head], weights, 1, 0)
        total = update[width : width + 1]
        context_out[pl.ds(pl.multiple_of(head * width, width), width), span] = (
            update[:width] / total
        )
        log_total = largest + jnp.log(total) * LOG2E
        query_out[head, width:, span] = extra_rows(
            query_base[:, start : start + block], -log_total, 3
        ).astype(jnp.bfloat16)

    starts = range(0, length, block)
    for start in starts:
        score(0, scores_even, largest_even, start)

    def head_pair(pair, carry):
        head = pair * 2
        for start in starts:
            score(head + 1, scores_odd, largest_odd, start)
            weigh(head, scores_even, largest_even, start)
        following = jnp.minimum(head + 2, HEADS - 1)
        for start in starts:
            score(following, scores_even, largest_even, start)
            weigh(head + 1, scores_odd, largest_odd, start)
        return carry

    lax.fori_loop(0, HEADS // 2, head_pair, 0)


def attend(row_index, tokens, remote, query_extra, key_extra, weights):
    pieces = 1 + len(remote)
    local, model = tokens.shape[1:]
    length = pieces * local
    width = model // HEADS
    whole = lambda array: pl.BlockSpec(array.shape, lambda i, s: (0,) * array.ndim)
    own_spec = pl.BlockSpec((1, local, model), lambda i, s: (s[0], 0, 0))
    low = jax.ShapeDtypeStruct((1, HEADS, width + EXTRA, length), jnp.bfloat16)
    outs = (low, low, low, jax.ShapeDtypeStruct((model, length), jnp.float32))
    operands = (tokens, *remote, query_extra, key_extra, *weights)
    return pl.pallas_call(
        functools.partial(attend_kernel, pieces, width, min(256, length)),
        out_shape=outs,
        grid_spec=pltpu.PrefetchScalarGridSpec(
            num_scalar_prefetch=1,
            grid=(1,),
            in_specs=[own_spec] + [whole(a) for a in operands[1:]],
            out_specs=[whole(a) for a in outs],
            scratch_shapes=[
                pltpu.VMEM((length, length), jnp.float32),
                pltpu.VMEM((length, length), jnp.float32),
                pltpu.VMEM((1, length), jnp.float32),
                pltpu.VMEM((1, length), jnp.float32),
            ],
        ),
        compiler_params=pltpu.CompilerParams(vmem_limit_bytes=60 * MIB),
        cost_estimate=pl.CostEstimate(
            flops=3 * 10**9, bytes_accessed=1, transcendentals=0
        ),
        name="attend",
    )(row_index, *operands)


def row_mean(values):
    return jnp.mean(values, -1, keepdims=True)


def normalise(values):
    centred = values - row_mean(values)
    scale = lax.rsqrt(row_mean(centred * centred) + EPSILON)
    return centred * scale, scale


def norm_back(grad, gain, normed, scale):
    entering = grad * gain
    return (entering - row_mean(entering) - normed * row_mean(entering * normed)) * scale


def column_sum(values):
    return jnp.sum(values, 0, keepdims=True)


def gelu_parts(values):
    phi = 0.5 + 0.5 * lax.erf(values * 0.5**0.5)
    bell = jnp.exp2(values * values * (-0.5 * LOG2E))
    return values * phi, phi + values * bell * 0.3989422804014327


def token_kernel(rows, pieces, steps, width, chunk, *refs):
    _, keep_ref, me_ref, refs = *refs[:3], refs[3:]
    own_tokens, own_cotangent, refs = *refs[:2], refs[2:]
    remote_count = rows * (pieces - 1)
    remote_tokens, refs = refs[:remote_count], refs[remote_count:]
    remote_cotangents, refs = refs[:remote_count], refs[remote_count:]
    context_refs, refs = refs[:rows], refs[rows:]
    (
        out_weight,
        out_bias,
        first_gain,
        first_shift,
        up_weight,
        up_bias,
        down_weight,
        down_bias,
        second_gain,
        second_shift,
    ) = refs[:10]
    refs = refs[10:]
    layer_outs, refs = refs[: rows * pieces], refs[rows * pieces :]
    (
        grad_out_heads,
        grad_first_out,
        packed_near,
        packed_far,
        tokens_scratch,
        cotangent_scratch,
        context_scratch,
        act_scratch,
        slope_scratch,
        totals,
        lines,
        *line_sums,
    ) = refs
    (
        grad_out_bias,
        grad_first_gain,
        grad_first_shift,
        grad_down_bias,
        grad_second_gain,
        grad_second_shift,
        grad_value_bias,
        grad_up_bias,
    ) = line_sums
    row_index = pl.program_id(0)
    piece_index = pl.program_id(1)
    step_index = pl.program_id(2)
    tokens_len, model = tokens_scratch.shape
    hidden_units = up_weight.shape[1]
    kept = keep_ref[row_index] != 0
    span = pl.ds(pl.multiple_of(step_index * tokens_len, tokens_len), tokens_len)

    @pl.when(piece_index == 0)
    def _():
        tokens_scratch[...] = own_tokens[0, span]
        cotangent_scratch[...] = own_cotangent[0, span]

    for row in range(rows):

        @pl.when(row_index == row)
        def _():
            context_scratch[...] = context_refs[row][...]

        for piece in range(1, pieces):

            @pl.when((row_index == row) & (piece_index == piece))
            def _():
                position = row * (pieces - 1) + piece - 1
                tokens_scratch[...] = remote_tokens[position][0, span]
                cotangent_scratch[...] = remote_cotangents[position][0, span]

    @pl.when((row_index == 0) & (piece_index == 0) & (step_index == 0))
    def _():
        for ref in (totals, lines, *line_sums):
            ref[...] = jnp.zeros(ref.shape, ref.dtype)

    tokens = tokens_scratch[...].astype(jnp.float32)
    context = context_scratch[...]
    context_low = context.astype(jnp.bfloat16)
    first_sum = tokens + (dot(context_low, out_weight[...], 0, 0) + out_bias[...])
    first_normed, first_scale = normalise(first_sum)
    hidden = first_normed * first_gain[...] + first_shift[...]
    hidden_low = hidden.astype(jnp.bfloat16)
    branch = down_bias[...]
    for start in range(0, hidden_units, chunk):
        units = pl.ds(start, chunk)
        pre_act = dot(hidden_low, up_weight[:, units], 1, 0) + up_bias[:, units]
        activated, slope = gelu_parts(pre_act)
        act_low = activated.astype(jnp.bfloat16)
        act_scratch[:, units] = act_low
        slope_scratch[:, units] = slope
        branch = branch + dot(act_low, down_weight[units, :], 1, 0)
    second_normed, second_scale = normalise(hidden + branch)
    result = jnp.where(
        kept, second_normed * second_gain[...] + second_shift[...], tokens
    ).astype(jnp.bfloat16)
    for position, ref in enumerate(layer_outs):

        @pl.when(row_index * pieces + piece_index == position)
        def _():
            ref[0, span] = result

    cotangent = cotangent_scratch[...].astype(jnp.float32)
    grad_out = jnp.where(kept, cotangent, 0.0)
    grad_second_gain[...] += column_sum(grad_out * second_normed)
    grad_second_shift[...] += column_sum(grad_out)
    grad_second = norm_back(grad_out, second_gain[...], second_normed, second_scale)
    grad_branch_low = grad_second.astype(jnp.bfloat16)
    grad_down_bias[...] += column_sum(grad_branch_low.astype(jnp.float32))
    grad_hidden = grad_second
    for start in range(0, hidden_units, chunk):
        units = pl.ds(start, chunk)
        grad_pre = dot(grad_branch_low, down_weight[units, :], 1, 1) * slope_scratch[:, units]
        grad_pre_low = grad_pre.astype(jnp.bfloat16)
        grad_up_bias[:, units] += column_sum(grad_pre_low.astype(jnp.float32))
        totals[units, :] += dot(hidden_low, grad_pre_low, 0, 0)
        totals[pl.ds(hidden_units + start, chunk), :] += dot(
            act_scratch[:, units], grad_branch_low, 0, 0
        )
        grad_hidden = grad_hidden + dot(grad_pre_low, up_weight[:, units], 1, 1)
    grad_first_gain[...] += column_sum(grad_hidden * first_normed)
    grad_first_shift[...] += column_sum(grad_hidden)
    grad_first = norm_back(grad_hidden, first_gain[...], first_normed, first_scale)
    grad_first_out[0] = jnp.where(kept, grad_first, cotangent)
    grad_attn_low = grad_first.astype(jnp.bfloat16)
    grad_out_bias[...] += column_sum(grad_attn_low.astype(jnp.float32))
    totals[pl.ds(2 * hidden_units, model), :] += dot(context_low, grad_attn_low, 1, 0)
    grad_context = dot(out_weight[...], grad_attn_low, 1, 1).astype(jnp.bfloat16)
    grad_context_wide = grad_context.astype(jnp.float32)
    ones = jnp.ones((EXTRA, tokens_len), jnp.bfloat16)
    grad_value_bias[...] += dot(ones, grad_context, 1, 1)[:1]
    product = grad_context_wide * context
    blank = jnp.zeros((EXTRA, tokens_len), jnp.float32)
    for head in range(HEADS):
        columns = slice(head * width, (head + 1) * width)
        grad_out_heads[0, head, :width] = grad_context[columns]
        spread = jnp.sum(product[columns], 0, keepdims=True)
        grad_out_heads[0, head, width:] = extra_rows(blank, -spread, 0).astype(jnp.bfloat16)

    @pl.when((row_index == rows - 1) & (piece_index == pieces - 1) & (step_index == steps - 1))
    def _():
        first = 0
        for ref in line_sums:
            set_lines(lines, first, ref[...])
            first += ref.shape[1] // LANES
        pack([totals], lines, packed_near, packed_far, me_ref[0])


def set_lines(lines, first, values):
    width = lines.shape[2]
    for block in range(values.shape[1] // width):
        slot, row = divmod(first + block, LINE_ROWS)
        lines[slot, row : row + 1] = values[:, block * width : (block + 1) * width]


def pack(parts, lines, near, far, me):
    half, size, width = near.shape
    columns = [(ref, start) for ref in parts for start in range(0, ref.shape[1], width)]
    height = parts[0].shape[0] // (2 * half)

    def one(slot, carry):
        for ref, first in ((near, 0), (far, half)):
            piece = (slot + first) ^ me
            rows = pl.ds(pl.multiple_of(piece * height, EXTRA), height)
            for block, (source, start) in enumerate(columns):
                ref[slot, pl.ds(block * height, height), :] = source[
                    rows, pl.ds(start, width)
                ].astype(jnp.bfloat16)
            ref[slot, pl.ds(len(columns) * height, EXTRA), :] = jnp.concatenate(
                [lines[piece], jnp.zeros_like(lines[piece])], 0
            ).astype(jnp.bfloat16)
        return carry

    lax.fori_loop(0, half, one, 0)


def packed_shape(slots, rows, model):
    return jax.ShapeDtypeStruct(
        (slots // 2, rows * (model // LANES) // slots + EXTRA, LANES), jnp.bfloat16
    )


def lines_shape(slots):
    return pltpu.VMEM((slots, EXTRA // 2, LANES), jnp.float32)


def by_token(
    row_index, keep, me, tokens, remote, cotangent, remote_cotangent, contexts, weights, slots
):
    rows = len(contexts)
    pieces = 1 + len(remote[0])
    local, model = tokens.shape[1:]
    length = pieces * local
    width = model // HEADS
    hidden_units = weights[4].shape[1]
    tokens_len = min(512, local)
    steps = local // tokens_len
    whole = lambda array: pl.BlockSpec(array.shape, lambda r, i, j, s, k, m: (0,) * array.ndim)
    own_spec = pl.BlockSpec((1, local, model), lambda r, i, j, s, k, m: (s[0] + r, 0, 0))
    f32 = lambda *shape: jax.ShapeDtypeStruct(shape, jnp.float32)
    total_rows = 2 * hidden_units + model
    packed = packed_shape(slots, total_rows, model)
    piece_out = jax.ShapeDtypeStruct((1, local, model), jnp.bfloat16)
    gradient_outs = (packed, packed)
    line_lengths = [model] * 7 + [hidden_units]
    outs = (
        *([piece_out] * (rows * pieces)),
        jax.ShapeDtypeStruct((rows, HEADS, width + EXTRA, length), jnp.bfloat16),
        f32(rows, length, model),
        *gradient_outs,
    )
    out_specs = (
        *([whole(piece_out)] * (rows * pieces)),
        pl.BlockSpec(
            (1, HEADS, width + EXTRA, tokens_len),
            lambda r, i, j, s, k, m: (r, 0, 0, i * steps + j),
        ),
        pl.BlockSpec((1, tokens_len, model), lambda r, i, j, s, k, m: (r, i * steps + j, 0)),
        *[whole(a) for a in gradient_outs],
    )

    def context_spec(row):
        def block(r, i, j, s, k, m):
            step = i * steps + j
            return 0, jnp.where(r < row, 0, jnp.where(r > row, pieces * steps - 1, step))

        return pl.BlockSpec((model, tokens_len), block)

    flat_remote = [array for arrays in remote for array in arrays]
    flat_remote_cotangent = [array for arrays in remote_cotangent for array in arrays]
    in_specs = (
        own_spec,
        own_spec,
        *[whole(a) for a in (*flat_remote, *flat_remote_cotangent)],
        *[context_spec(row) for row in range(rows)],
        *[whole(a) for a in weights],
    )
    return pl.pallas_call(
        functools.partial(token_kernel, rows, pieces, steps, width, min(model, hidden_units)),
        out_shape=outs,
        grid_spec=pltpu.PrefetchScalarGridSpec(
            num_scalar_prefetch=3,
            grid=(rows, pieces, steps),
            in_specs=in_specs,
            out_specs=out_specs,
            scratch_shapes=[
                pltpu.VMEM((tokens_len, model), jnp.bfloat16),
                pltpu.VMEM((tokens_len, model), jnp.bfloat16),
                pltpu.VMEM((model, tokens_len), jnp.float32),
                pltpu.VMEM((tokens_len, hidden_units), jnp.bfloat16),
                pltpu.VMEM((tokens_len, hidden_units), jnp.float32),
                pltpu.VMEM((total_rows, model), jnp.float32),
                lines_shape(slots),
                *[pltpu.VMEM((1, n), jnp.float32) for n in line_lengths],
            ],
        ),
        compiler_params=pltpu.CompilerParams(vmem_limit_bytes=60 * MIB),
        cost_estimate=pl.CostEstimate(flops=1, bytes_accessed=1, transcendentals=0),
        name="by_token",
    )(
        row_index,
        keep,
        me,
        tokens,
        cotangent,
        *flat_remote,
        *flat_remote_cotangent,
        *contexts,
        *weights,
    )


def attend_back_kernel(pieces, width, block, place, *refs):
    row, rows, part, parts = place
    first_row, last_part = row == 0, part == parts - 1
    packing = row == rows - 1 and last_part
    row_ref, me_ref, refs = *refs[:2], refs[2:]
    token_refs, refs = refs[:pieces], refs[pieces:]
    head_refs, refs = refs[:4], refs[4:]
    grad_tokens_in, *weight_refs, refs = *refs[:4], refs[4:]
    if not first_row:
        totals_in, bias_in, refs = *refs[:2], refs[2:]
    earlier = part if packing else 0
    earlier_totals, refs = refs[:earlier], refs[earlier:]
    earlier_biases, refs = refs[:earlier], refs[earlier:]
    outs = pieces if last_part else 1
    grad_tokens, refs = refs[:outs], refs[outs:]
    if packing:
        packed_near, packed_far, *refs = refs
    else:
        totals_out, bias, *refs = refs
    (
        grad_query_scratch,
        grad_key_scratch,
        grad_value_scratch,
        tokens_scratch,
        grad_scratch,
        weights_scratch,
        totals,
        sems,
        *refs,
    ) = refs
    if packing:
        lines, bias, *earlier_scratch = refs
    query_ref, key_ref, value_ref, grad_ref = (ref.at[0] for ref in head_refs)
    pair = pl.program_id(0)
    pairs = pl.num_programs(0)
    length = query_ref.shape[2]
    local = length // pieces
    model, columns = weights_scratch.shape[1:]
    pair_width = 2 * width
    share = pl.ds(part * columns, columns)
    incoming = [(token_refs[0].at[row_ref[0]], tokens_scratch.at[0])]
    incoming += [(ref.at[0], tokens_scratch.at[i + 1]) for i, ref in enumerate(token_refs[1:])]
    incoming.append((grad_tokens_in.at[row if part == 0 else 0], grad_scratch))
    incoming += [(ref.at[:, share], weights_scratch.at[i]) for i, ref in enumerate(weight_refs)]
    if not first_row:
        incoming.append((totals_in, totals))
    if packing:
        incoming += list(zip(earlier_totals, earlier_scratch))
    incoming = [
        pltpu.make_async_copy(source, target, sems.at[i])
        for i, (source, target) in enumerate(incoming)
    ]

    @pl.when(pair == 0)
    def _():
        for copy in incoming:
            copy.start()

    grad_queries = [[], []]
    for side in range(2):
        key = key_ref[side]
        value = value_ref[side]
        grad_key = 0.0
        grad_value = 0.0
        for start in range(0, length, block):
            span = pl.ds(start, block)
            query = query_ref[side, :, span]
            grad = grad_ref[side, :, span]
            weights = jnp.exp2(dot(query, key, 0, 0))
            grad_weights = dot(grad, value, 0, 0)
            weights_low = weights.astype(jnp.bfloat16)
            grad_scores = (weights * grad_weights).astype(jnp.bfloat16)
            grad_value = grad_value + dot(grad[:width], weights_low, 1, 0)
            grad_key = grad_key + dot(query[:width], grad_scores, 1, 0)
            grad_queries[side].append(dot(grad_scores, key[:width], 1, 1))
        head = pl.ds(pl.multiple_of(pair * pair_width + side * width, width), width)
        grad_value_scratch[head, :] = grad_value.astype(jnp.bfloat16)
        grad_key_scratch[head, :] = (grad_key * LN2).astype(jnp.bfloat16)
    for index, start in enumerate(range(0, length, block)):
        both = jnp.concatenate([grad_queries[0][index], grad_queries[1][index]], 1)
        grad_query_scratch[pair, pl.ds(start, block)] = (both * width**-0.5).astype(jnp.bfloat16)

    @pl.when(pair == pairs - 1)
    def _():
        for copy in incoming:
            copy.wait()
        count = grad_query_scratch.shape[0]
        for index in range(count):
            lanes = pl.ds(index * pair_width, pair_width)
            total = column_sum(grad_query_scratch[index].astype(jnp.float32))
            bias[:, lanes] = total if first_row else bias_in[:, lanes] + total
        grad_query = jnp.concatenate([grad_query_scratch[index] for index in range(count)], 1)
        outgoing = []
        for position in range(3):
            lines_of = pl.ds(position * model, model)
            term = 0.0
            for piece in range(pieces):
                span = slice(piece * local, (piece + 1) * local)
                tokens = tokens_scratch[piece]
                if position == 0:
                    term = term + dot(tokens, grad_query[span], 0, 0)
                else:
                    source = grad_key_scratch if position == 1 else grad_value_scratch
                    term = term + dot(tokens, source[:, span], 0, 1)
            totals[lines_of, :] = term if first_row else totals[lines_of, :] + term
        if not packing:
            outgoing.append(pltpu.make_async_copy(totals, totals_out, sems.at[0]))
            outgoing[0].start()
        for piece in range(pieces):
            span = pl.ds(piece * local, local)
            total = (
                grad_scratch[span]
                + dot(grad_query[piece * local : (piece + 1) * local], weights_scratch[0], 1, 1)
                + dot(grad_key_scratch[:, span], weights_scratch[1], 0, 1)
                + dot(grad_value_scratch[:, span], weights_scratch[2], 0, 1)
            )
            if last_part:
                grad_tokens[piece][0] = total.astype(jnp.bfloat16)
            else:
                grad_scratch[span] = total
                outgoing.append(
                    pltpu.make_async_copy(
                        grad_scratch.at[span], grad_tokens[0].at[0, span], sems.at[1 + piece]
                    )
                )
                outgoing[-1].start()
        if packing:
            lines[...] = jnp.zeros(lines.shape, lines.dtype)
            first = 0
            for ref in (*earlier_biases, bias):
                set_lines(lines, first, ref[...])
                first += ref.shape[1] // LANES
            pack([*earlier_scratch, totals], lines, packed_near, packed_far, me_ref[0])
        for copy in outgoing:
            copy.wait()


def attend_back(
    place, row_index, me, tokens, remote, heads, grad_tokens, weights, totals, biases, slots, gflops
):
    row, rows, part, parts = place
    last_part = part == parts - 1
    packing = row == rows - 1 and last_part
    pieces = 1 + len(remote)
    local, model = tokens.shape[1:]
    length = pieces * local
    width = model // HEADS
    columns = model // parts
    pairs = HEADS // parts // 2
    anywhere = pl.BlockSpec(memory_space=pl.ANY)
    whole = lambda array: pl.BlockSpec(array.shape, lambda i, s, m: (0,) * array.ndim)
    head_spec = lambda array: pl.BlockSpec(
        (1, 2, *array.shape[2:]),
        lambda i, s, m: (row if array.shape[0] > 1 else 0, part * pairs + i, 0, 0),
    )
    f32 = lambda *shape: jax.ShapeDtypeStruct(shape, jnp.float32)
    if last_part:
        outs = [jax.ShapeDtypeStruct((1, local, model), jnp.bfloat16)] * pieces
        out_specs = [whole(a) for a in outs]
    else:
        outs, out_specs = [f32(1, length, model)], [anywhere]
    total, bias = f32(3 * model, columns), f32(1, columns)
    in_specs = [anywhere] * pieces + [head_spec(a) for a in heads] + [anywhere] * 4
    operands = [tokens, *remote, *heads, grad_tokens, *weights]
    if row:
        operands += [totals[part], biases[part]]
        in_specs += [anywhere, whole(bias)]
    scratch = [
        pltpu.VMEM((pairs, length, 2 * width), jnp.bfloat16),
        pltpu.VMEM((columns, length), jnp.bfloat16),
        pltpu.VMEM((columns, length), jnp.bfloat16),
        pltpu.VMEM((pieces, local, model), jnp.bfloat16),
        pltpu.VMEM((length, model), jnp.float32),
        pltpu.VMEM((3, model, columns), jnp.bfloat16),
        pltpu.VMEM(total.shape, jnp.float32),
        pltpu.SemaphoreType.DMA((pieces + 5 + parts,)),
    ]
    if packing:
        operands += [*totals[:part], *biases[:part]]
        in_specs += [anywhere] * part + [whole(bias)] * part
        packed = packed_shape(slots, 3 * model, model)
        outs += [packed] * 2
        out_specs += [whole(packed)] * 2
        scratch += [lines_shape(slots), pltpu.VMEM(bias.shape, jnp.float32)]
        scratch += [pltpu.VMEM(total.shape, jnp.float32)] * part
    else:
        outs += [total, bias]
        out_specs += [anywhere, whole(bias)]
    return pl.pallas_call(
        functools.partial(attend_back_kernel, pieces, width, min(256, length), place),
        out_shape=outs,
        grid_spec=pltpu.PrefetchScalarGridSpec(
            num_scalar_prefetch=2,
            grid=(pairs,),
            in_specs=in_specs,
            out_specs=out_specs,
            scratch_shapes=scratch,
        ),
        compiler_params=pltpu.CompilerParams(vmem_limit_bytes=60 * MIB),
        cost_estimate=pl.CostEstimate(
            flops=gflops * 10**9, bytes_accessed=1, transcendentals=0
        ),
        name="attend_back",
    )(row_index, me, *operands)


def unpack_kernel(moves, line_count, count, me_ref, *refs):
    sources, refs = refs[:count], refs[count:]
    *outs, slots, in_sems, out_sems = refs
    outs, blocks_out = outs[: len(outs) // 2], outs[len(outs) // 2 :]
    _, size, width = slots.shape
    me = me_ref[0]
    share = slots.shape[0] // count
    copies = [
        pltpu.make_async_copy(source, slots.at[pl.ds(index * share, share)], in_sems.at[index])
        for index, source in enumerate(sources)
    ]
    for copy in copies:
        copy.start()
    for copy in copies:
        copy.wait()
    lines = blocks_out[-1]
    blocks = lines.shape[1] // width
    for index in range(line_count * blocks):
        line, block = divmod(index, blocks)
        piece, row = divmod(index, LINE_ROWS)
        extra = slots[piece ^ me, pl.ds(size - EXTRA, EXTRA), :].astype(jnp.float32)
        lines[line : line + 1, pl.ds(block * width, width)] = extra[row : row + 1]
    copies = [pltpu.make_async_copy(lines, outs[-1], out_sems.at[0])]
    copies[0].start()
    for square, (out, row, column, pieces) in enumerate(moves):
        for piece, start, rows, inside, offset in pieces:
            blocks_out[out][pl.ds(row + inside, rows), pl.ds(column + offset, width)] = slots[
                piece ^ me, pl.ds(start, rows), :
            ].astype(jnp.float32)
        model = lines.shape[1]
        part = pl.ds(row, model), pl.ds(column, model)
        copies.append(
            pltpu.make_async_copy(
                blocks_out[out].at[part], outs[out].at[part], out_sems.at[square + 1]
            )
        )
        copies[-1].start()
    for copy in copies:
        copy.wait()


def unpack(me, arrays, shapes, model, line_count):
    share, size, width = arrays[0].shape
    slots = share * len(arrays)
    blocks = model // width
    height = (size - EXTRA) // blocks
    moves = [
        (out, row, column, [])
        for out, shape in enumerate(shapes)
        for row in range(0, shape[0], model)
        for column in range(0, shape[1], model)
    ]
    for piece in range(slots):
        done = 0
        while done < height:
            square, inside = divmod(piece * height + done, model)
            rows = min(height - done, model - inside)
            for block in range(blocks):
                moves[square][3].append(
                    (piece, block * height + done, rows, inside, block * width)
                )
            done += rows
    outs = [jax.ShapeDtypeStruct(shape, jnp.float32) for shape in (*shapes, (line_count, model))]
    anywhere = pl.BlockSpec(memory_space=pl.ANY)
    return pl.pallas_call(
        functools.partial(unpack_kernel, moves, line_count, len(arrays)),
        out_shape=outs,
        grid_spec=pltpu.PrefetchScalarGridSpec(
            num_scalar_prefetch=1,
            grid=(1,),
            in_specs=[anywhere] * len(arrays),
            out_specs=[anywhere] * len(outs),
            scratch_shapes=[
                *[pltpu.VMEM(a.shape, jnp.float32) for a in outs],
                pltpu.VMEM((slots, size, width), jnp.bfloat16),
                pltpu.SemaphoreType.DMA((len(arrays),)),
                pltpu.SemaphoreType.DMA((len(moves) + 1,)),
            ],
        ),
        compiler_params=pltpu.CompilerParams(vmem_limit_bytes=60 * MIB),
        cost_estimate=pl.CostEstimate(
            flops=2 * 10**10, bytes_accessed=1, transcendentals=0
        ),
        name="unpack",
    )(me, *arrays)


NEAR, MIDDLE, FAR, SEQ = AXES = ("near", "middle", "far", "seq")
STAGES = ((NEAR,), (MIDDLE, SEQ), (FAR,))


def add_up(arrays):
    arrays = [a.astype(jnp.float32) for a in arrays]
    while len(arrays) > 1:
        arrays = [first + second for first, second in zip(arrays[::2], arrays[1::2], strict=True)]
    return arrays[0].astype(jnp.bfloat16)


def after(arrays, *others):
    return lax.optimization_barrier((arrays, others))[0]


class Sums:
    def __init__(self):
        self.sizes = [lax.axis_size(axes) for axes in STAGES]
        self.devices = math.prod(self.sizes)
        digits = [lax.axis_index(axes) for axes in STAGES]
        self.me = (digits[0] * self.sizes[1] + digits[1]) * self.sizes[2] + digits[2]
        self.me_near = self.me - digits[2]

    def swap(self, array, stage, turn):
        pairs = [(i, i ^ turn) for i in range(self.sizes[stage])]
        return lax.ppermute(array, STAGES[stage], pairs)

    def meet(self, parts, stage):
        return [parts[0], *[self.swap(parts[t], stage, t) for t in range(1, len(parts))]]

    def add_parts(self, arrays, stage):
        size = self.sizes[stage]
        share = arrays[0].shape[0] // size
        return [
            add_up([array[turn * share : (turn + 1) * share] for array in arrays])
            for turn in range(size)
        ]

    def others(self, held, stage):
        return [self.swap(held, stage, turn) for turn in range(1, self.sizes[stage])]


def norm_rows(values, gain, shift):
    row_mean = jnp.mean(values, -1, keepdims=True)
    centred = values - row_mean
    variance = jnp.mean(centred * centred, -1, keepdims=True)
    return centred * lax.rsqrt(variance + EPSILON) * gain + shift


def gelu_exact(values):
    return jax.nn.gelu(values, approximate=False)


def plain_dot(left, right):
    return jnp.dot(left, right, preferred_element_type=jnp.float32)


def left_dot(left, right):
    return lax.dot_general(
        left, right, (((0,), (0,)), ((), ())), preferred_element_type=jnp.float32
    )


def right_dot(left, right):
    return lax.dot_general(
        left, right, (((1,), (1,)), ((), ())), preferred_element_type=jnp.float32
    )


def token_sum(values):
    return jnp.sum(values.astype(jnp.float32), 0)


def split_heads(values, piece_len):
    return values.reshape(values.shape[0], piece_len, HEADS, values.shape[2] // HEADS)


def block_length(piece_len, local_len):
    return math.gcd(math.gcd(piece_len, local_len), BLOCK_CAP)


def masked_scores(query_heads, key_heads, query_ids, key_ids, score_scale):
    scores = (
        jnp.einsum("rqhd,rkhd->rhqk", query_heads, key_heads, preferred_element_type=jnp.float32)
        * score_scale
    )
    same_doc = query_ids[:, None, :, None] == key_ids[:, None, None, :]
    return jnp.where(same_doc, scores, NEG_FILL)


def split_attend_back(
    query_heads,
    grad_heads,
    log_total,
    spread,
    query_ids,
    key_heads,
    value_heads,
    key_ids,
    score_scale,
):
    scores = masked_scores(query_heads, key_heads, query_ids, key_ids, score_scale)
    weights = jnp.exp(scores - jnp.transpose(log_total, (0, 2, 1))[..., None])
    grad_value = jnp.einsum(
        "rhqk,rqhd->rkhd",
        weights.astype(jnp.bfloat16),
        grad_heads,
        preferred_element_type=jnp.float32,
    )
    grad_weights = jnp.einsum(
        "rqhd,rkhd->rhqk", grad_heads, value_heads, preferred_element_type=jnp.float32
    )
    grad_scores = (weights * (grad_weights - jnp.transpose(spread, (0, 2, 1))[..., None])).astype(
        jnp.bfloat16
    )
    grad_query = (
        jnp.einsum("rhqk,rkhd->rqhd", grad_scores, key_heads, preferred_element_type=jnp.float32)
        * score_scale
    )
    grad_key = (
        jnp.einsum("rhqk,rqhd->rkhd", grad_scores, query_heads, preferred_element_type=jnp.float32)
        * score_scale
    )
    return (grad_query, grad_key, grad_value)


def add_into(buffer, term, block_start):
    current = lax.dynamic_slice_in_dim(buffer, block_start, term.shape[1], 1)
    return lax.dynamic_update_slice_in_dim(buffer, current + term, block_start, 1)


def split_rows(
    tokens,
    segments,
    keep_flags,
    query_weight,
    query_bias,
    key_weight,
    value_weight,
    value_bias,
    out_weight,
    out_bias,
    first_gain,
    first_shift,
    up_weight,
    up_bias,
    down_weight,
    down_bias,
    second_gain,
    second_shift,
    cotangent,
):
    row_count, local_tokens, model_width = tokens.shape
    head_width = model_width // HEADS
    score_scale = head_width ** (-0.5)
    flat_tokens = tokens.reshape(row_count * local_tokens, model_width)
    row_shape = (row_count, local_tokens, model_width)
    query_low = (
        (plain_dot(flat_tokens, query_weight) + query_bias).astype(jnp.bfloat16).reshape(row_shape)
    )
    key_low = plain_dot(flat_tokens, key_weight).astype(jnp.bfloat16).reshape(row_shape)
    value_low = (
        (plain_dot(flat_tokens, value_weight) + value_bias).astype(jnp.bfloat16).reshape(row_shape)
    )
    query_heads = split_heads(query_low, local_tokens)
    own_start = lax.axis_index("seq") * local_tokens
    own_ids = lax.dynamic_slice_in_dim(segments, own_start, local_tokens, 1)
    initial = (
        jnp.full((row_count, HEADS, local_tokens), NEG_FILL, jnp.float32),
        jnp.zeros((row_count, HEADS, local_tokens), jnp.float32),
        jnp.zeros((row_count, HEADS, local_tokens, head_width), jnp.float32),
    )
    key_piece = lax.all_gather(key_low, "seq", axis=1, tiled=True)
    value_piece = lax.all_gather(value_low, "seq", axis=1, tiled=True)
    block_size = block_length(key_piece.shape[1], local_tokens)

    def key_step(position, inner_state):
        running_max, running_sum, running_acc = inner_state
        block_start = position * block_size
        key_heads = split_heads(
            lax.dynamic_slice_in_dim(key_piece, block_start, block_size, 1), block_size
        )
        value_heads = split_heads(
            lax.dynamic_slice_in_dim(value_piece, block_start, block_size, 1), block_size
        )
        key_ids = lax.dynamic_slice_in_dim(segments, block_start, block_size, 1)
        scores = masked_scores(query_heads, key_heads, own_ids, key_ids, score_scale)
        newest = jnp.maximum(running_max, jnp.max(scores, -1))
        factor = jnp.exp(running_max - newest)
        weights = jnp.exp(scores - newest[..., None])
        running_sum = running_sum * factor + jnp.sum(weights, -1)
        update = jnp.einsum(
            "rhqk,rkhd->rhqd",
            weights.astype(jnp.bfloat16),
            value_heads,
            preferred_element_type=jnp.float32,
        )
        return (newest, running_sum, running_acc * factor[..., None] + update)

    running_max, running_sum, running_acc = lax.fori_loop(
        0, key_piece.shape[1] // block_size, key_step, initial
    )
    context_heads = jnp.transpose(running_acc / running_sum[..., None], (0, 2, 1, 3))
    log_total = jnp.transpose(running_max + jnp.log(running_sum), (0, 2, 1))
    context_low = context_heads.reshape(row_count * local_tokens, model_width).astype(jnp.bfloat16)
    first_sum = flat_tokens.astype(jnp.float32) + (plain_dot(context_low, out_weight) + out_bias)
    hidden, first_back = jax.vjp(norm_rows, first_sum, first_gain, first_shift)
    hidden_low = hidden.astype(jnp.bfloat16)
    pre_act = plain_dot(hidden_low, up_weight) + up_bias
    activated, act_back = jax.vjp(gelu_exact, pre_act)
    act_low = activated.astype(jnp.bfloat16)
    second_sum = hidden + (plain_dot(act_low, down_weight) + down_bias)
    normed, second_back = jax.vjp(norm_rows, second_sum, second_gain, second_shift)
    kept_rows = (keep_flags != 0)[:, None, None]
    layer_out = jnp.where(kept_rows, normed.reshape(row_shape), tokens.astype(jnp.float32)).astype(
        jnp.bfloat16
    )
    grad_out = jnp.where(kept_rows, cotangent.astype(jnp.float32), 0.0).reshape(
        row_count * local_tokens, model_width
    )
    grad_second, grad_second_gain, grad_second_shift = second_back(grad_out)
    grad_branch_low = grad_second.astype(jnp.bfloat16)
    grad_down_bias = token_sum(grad_branch_low)
    grad_down_weight = left_dot(act_low, grad_branch_low)
    (grad_pre,) = act_back(right_dot(grad_branch_low, down_weight))
    grad_pre_low = grad_pre.astype(jnp.bfloat16)
    grad_up_bias = token_sum(grad_pre_low)
    grad_up_weight = left_dot(hidden_low, grad_pre_low)
    grad_hidden = grad_second + right_dot(grad_pre_low, up_weight)
    grad_first, grad_first_gain, grad_first_shift = first_back(grad_hidden)
    grad_attn_low = grad_first.astype(jnp.bfloat16)
    grad_out_bias = token_sum(grad_attn_low)
    grad_out_weight = left_dot(context_low, grad_attn_low)
    late_grads = (
        grad_out_weight,
        grad_out_bias,
        grad_first_gain,
        grad_first_shift,
        grad_up_weight,
        grad_up_bias,
        grad_down_weight,
        grad_down_bias,
        grad_second_gain,
        grad_second_shift,
    )
    grad_context_low = right_dot(grad_attn_low, out_weight).astype(jnp.bfloat16)
    grad_context_rows = grad_context_low.reshape(row_shape)
    grad_heads = split_heads(grad_context_rows, local_tokens)
    spread = jnp.sum(grad_heads.astype(jnp.float32) * context_heads, -1)
    zero_local = jnp.zeros((row_count, local_tokens, HEADS, head_width), jnp.float32)
    zero_whole = jnp.zeros(
        (row_count, local_tokens * lax.axis_size("seq"), HEADS, head_width), jnp.float32
    )
    gathered_total, gathered_spread = (
        lax.all_gather(log_total, "seq", axis=1, tiled=True),
        lax.all_gather(spread, "seq", axis=1, tiled=True),
    )
    key_heads_local = split_heads(key_low, local_tokens)
    value_heads_local = split_heads(value_low, local_tokens)
    query_piece = lax.all_gather(query_low, "seq", axis=1, tiled=True)
    grad_piece = lax.all_gather(grad_context_rows, "seq", axis=1, tiled=True)
    back_block_size = block_length(query_piece.shape[1], local_tokens)

    def query_step(position, inner_state):
        grad_key, grad_value, queries_whole = inner_state
        block_start = position * back_block_size
        part_query, part_key, part_value = split_attend_back(
            split_heads(
                lax.dynamic_slice_in_dim(query_piece, block_start, back_block_size, 1),
                back_block_size,
            ),
            split_heads(
                lax.dynamic_slice_in_dim(grad_piece, block_start, back_block_size, 1),
                back_block_size,
            ),
            lax.dynamic_slice_in_dim(gathered_total, block_start, back_block_size, 1),
            lax.dynamic_slice_in_dim(gathered_spread, block_start, back_block_size, 1),
            lax.dynamic_slice_in_dim(segments, block_start, back_block_size, 1),
            key_heads_local,
            value_heads_local,
            own_ids,
            score_scale,
        )
        return (
            grad_key + part_key,
            grad_value + part_value,
            add_into(queries_whole, part_query, block_start),
        )

    grad_key, grad_value, queries_whole = lax.fori_loop(
        0, query_piece.shape[1] // back_block_size, query_step, (zero_local, zero_local, zero_whole)
    )
    grad_query = lax.psum_scatter(queries_whole, "seq", scatter_dimension=1, tiled=True)
    flat_shape = (row_count * local_tokens, model_width)
    grad_query_low = grad_query.reshape(flat_shape).astype(jnp.bfloat16)
    grad_key_low = grad_key.reshape(flat_shape).astype(jnp.bfloat16)
    grad_value_low = grad_value.reshape(flat_shape).astype(jnp.bfloat16)
    grad_query_bias = token_sum(grad_query_low)
    grad_query_weight = left_dot(flat_tokens, grad_query_low)
    grad_key_weight = left_dot(flat_tokens, grad_key_low)
    grad_value_bias = token_sum(grad_value_low)
    grad_value_weight = left_dot(flat_tokens, grad_value_low)
    grad_flat = (
        grad_first
        + right_dot(grad_query_low, query_weight)
        + right_dot(grad_key_low, key_weight)
        + right_dot(grad_value_low, value_weight)
    )
    tokens_grad = jnp.where(
        kept_rows, grad_flat.reshape(row_shape), cotangent.astype(jnp.float32)
    ).astype(jnp.bfloat16)
    early_grads = (
        grad_query_weight,
        grad_query_bias,
        grad_key_weight,
        grad_value_weight,
        grad_value_bias,
    )
    summed = lax.psum(
        (
            grad_query_weight,
            grad_query_bias,
            grad_key_weight,
            grad_value_weight,
            grad_value_bias,
            grad_out_weight,
            grad_out_bias,
            grad_first_gain,
            grad_first_shift,
            grad_up_weight,
            grad_up_bias,
            grad_down_weight,
            grad_down_bias,
            grad_second_gain,
            grad_second_shift,
        ),
        ("dp", "seq"),
    )
    early_grads = summed[:5]
    late_grads = summed[5:]
    return (
        layer_out,
        tokens_grad,
        early_grads[0],
        early_grads[1],
        early_grads[2],
        early_grads[3],
        early_grads[4],
        late_grads[0],
        late_grads[1],
        late_grads[2],
        late_grads[3],
        late_grads[4],
        late_grads[5],
        late_grads[6],
        late_grads[7],
        late_grads[8],
        late_grads[9],
    )


def deal_rows(
    tokens,
    segments,
    keep_flags,
    query_weight,
    query_bias,
    key_weight,
    value_weight,
    value_bias,
    out_weight,
    out_bias,
    first_gain,
    first_shift,
    up_weight,
    up_bias,
    down_weight,
    down_bias,
    second_gain,
    second_shift,
    cotangent,
):
    row_count, local_tokens, model = tokens.shape
    ring = lax.axis_size("seq")
    me = lax.axis_index("seq")
    rows = row_count // ring
    first_row = me * rows
    turns = [[(i, (i + turn) % ring) for i in range(ring)] for turn in range(ring)]
    back_turns = [[(i, (i - turn) % ring) for i in range(ring)] for turn in range(ring)]

    def fetch(array, row, turn, before):
        theirs = lax.rem(me + turn, ring) * rows + row
        sent = after(lax.dynamic_slice_in_dim(array, theirs, 1, 0), before)
        return lax.ppermute(sent, "seq", turns[turn])

    remote, remote_cotangent, arrived = [], [], ()
    for row in range(rows):
        for array, fetched in ((tokens, remote), (cotangent, remote_cotangent)):
            fetched.append([fetch(array, row, turn, arrived) for turn in range(1, ring)])
            arrived = arrived or remote[row]
        arrived = remote[row]
    own_segments = lax.dynamic_slice_in_dim(segments, first_row, rows, 0)
    own_segments = jnp.concatenate(
        [
            lax.dynamic_slice_in_dim(
                own_segments, lax.rem(me - turn + ring, ring) * local_tokens, local_tokens, 1
            )
            for turn in range(ring)
        ],
        1,
    )
    extra_index = jnp.arange(EXTRA, dtype=jnp.int32)[None, :, None]
    same = own_segments[:, None, :] == extra_index
    query_extra = jnp.where(same & (extra_index < 3), 1.0, 0.0)
    key_extra = jnp.where(
        extra_index < 3, jnp.where(same, 0.0, NEG_FILL), jnp.where(extra_index < 6, 1.0, 0.0)
    )
    keep = lax.dynamic_slice_in_dim(keep_flags, first_row, rows, 0)
    line = lambda vector: vector.reshape(1, -1)
    column = lambda vector: vector.reshape(-1, 1)
    forward_weights = (
        query_weight,
        column(query_bias),
        key_weight,
        value_weight,
        column(value_bias),
    )
    token_weights = (
        out_weight,
        line(out_bias),
        line(first_gain),
        line(first_shift),
        up_weight,
        line(up_bias),
        down_weight,
        line(down_bias),
        line(second_gain),
        line(second_shift),
    )
    back_weights = (query_weight, key_weight, value_weight)
    row_index = [(first_row + row).reshape(1) for row in range(rows)]
    sums = Sums()
    number, slots = sums.me.reshape(1), sums.devices
    early_number = sums.me_near.reshape(1)
    heads, contexts = [], []
    remote[0] = after(remote[0], query_extra, key_extra, forward_weights, token_weights, number)
    for row in range(rows):
        if row:
            remote[row] = after(remote[row], contexts[-1])
        query, key, value, context = attend(
            row_index[row], tokens, remote[row], query_extra[row], key_extra[row], forward_weights
        )
        heads.append((query, key, value))
        contexts.append(context)
    remote_cotangent = after(remote_cotangent, contexts[-1])
    results = by_token(
        row_index[0],
        keep,
        number,
        tokens,
        remote,
        cotangent,
        remote_cotangent,
        contexts,
        token_weights,
        slots,
    )
    layer_outs = [results[row * ring : (row + 1) * ring] for row in range(rows)]
    results = results[rows * ring :]
    grad_heads, grad_first, late_near, late_far = results
    def give_back(parts, *before):
        return [
            part if turn == 0 else lax.ppermute(after(part, *before), "seq", back_turns[turn])
            for turn, part in enumerate(parts)
        ]

    def place(moved):
        by_turn = [jnp.concatenate(parts, 0) for parts in zip(*moved)]
        places = [
            [by_turn[(slot - index) % ring] for slot in range(ring)] for index in range(ring)
        ]
        whole = jnp.concatenate(places[0], 0)
        for index in range(1, ring):
            whole = jnp.where(me == index, jnp.concatenate(places[index], 0), whole)
        return whole

    late = sums.add_parts([late_near, sums.swap(late_far, 0, 1)], 1)
    parts = 2
    totals, biases = [None] * parts, [None] * parts
    tokens_grads = []
    here = after(early_number, *late)
    late = sums.meet(late, 1)
    for row in range(rows):
        grad_tokens = grad_first
        for part in range(parts):
            results = attend_back(
                (row, rows, part, parts),
                row_index[row],
                here,
                tokens,
                remote[row],
                (*heads[row], grad_heads),
                grad_tokens,
                back_weights,
                totals,
                biases,
                slots,
                1 if row == 0 and part else 200,
            )
            if part == parts - 1:
                tokens_grads.append(
                    results[:ring] if row == rows - 1 else give_back(results[:ring])
                )
                results = results[ring:]
            else:
                grad_tokens, *results = results
            if row < rows - 1 or part < parts - 1:
                totals[part], biases[part] = results
            if row == rows - 1 and part == 0:
                late = add_up(after(late, totals[0]))
                here = after(early_number, late, layer_outs[0])
        if row == 0:
            late = sums.add_parts(after(late, totals[1]), 2)
            here = after(early_number, *late)
            layer_outs = [give_back(parts, *late) for parts in layer_outs]
            late = sums.meet(late, 2)
    late = [late, *sums.others(late, 2)]
    late, layer_outs, tokens_grads[:-1] = after((late, layer_outs, tokens_grads[:-1]), results[0])
    early_near, early_far = after(results, late, layer_outs, tokens_grads[:-1])
    early = sums.add_parts([early_near, sums.swap(early_far, 0, 1)], 1)
    late = jnp.concatenate(late, 0)
    early = add_up(sums.meet(early, 1))
    late = after(late, early)
    late = [late, *sums.others(late, 1)]
    layer_out = place(layer_outs)
    early = add_up(after([early, *sums.others(early, 2)], late, layer_out))
    late = after(late, early)
    late = [*late, *[sums.swap(array, 0, 1) for array in late]]
    early = [early, *sums.others(early, 1)]
    hidden_units = up_weight.shape[1]
    lines = 7 + hidden_units // model
    tokens_grads[-1] = give_back(tokens_grads[-1], late)
    grad_up, grad_down, grad_out_weight, late_lines = unpack(
        number, late, [(model, hidden_units), (hidden_units, model), (model, model)], model, lines
    )
    early = after(early, late_lines)
    early = [*early, *[sums.swap(array, 0, 1) for array in early]]
    tokens_grad = place(after(tokens_grads, late_lines))
    late_vectors = [late_lines[i] for i in range(7)] + [late_lines[7:].reshape(-1)]
    early = after(early, late_vectors)
    grad_query, grad_key, grad_value, early_lines = unpack(
        early_number, early, [(model, model)] * 3, model, 1
    )
    (
        grad_out_bias,
        grad_first_gain,
        grad_first_shift,
        grad_down_bias,
        grad_second_gain,
        grad_second_shift,
        grad_value_bias,
        grad_up_bias,
    ) = late_vectors
    return (
        layer_out,
        tokens_grad,
        grad_query,
        early_lines[0],
        grad_key,
        grad_value,
        grad_value_bias,
        grad_out_weight,
        grad_out_bias,
        grad_first_gain,
        grad_first_shift,
        grad_up,
        grad_up_bias,
        grad_down,
        grad_down_bias,
        grad_second_gain,
        grad_second_shift,
    )


def solution(mesh):
    dp, ring = mesh.shape["dp"], mesh.shape["seq"]

    def placed(function, mesh, rows):
        return jax.shard_map(
            function,
            mesh=mesh,
            in_specs=(
                P(rows, "seq", None),
                P(rows, None),
                P(rows),
                *([P()] * 15),
                P(rows, "seq", None),
            ),
            out_specs=(P(rows, "seq", None), P(rows, "seq", None), *([P()] * 15)),
            check_vma=False,
        )

    def layer(tokens, *others):
        row_count, model = tokens.shape[0] // dp, tokens.shape[2]
        powers = dp & (dp - 1) == 0 and ring & (ring - 1) == 0 and dp >= 4
        if not powers or row_count % ring or model % (16 * dp * ring):
            return placed(split_rows, mesh, "dp")(tokens, *others)
        axes = (FAR, MIDDLE, NEAR)
        finer = jax.sharding.Mesh(mesh.devices.reshape(dp // 4, 2, 2, ring), (*axes, SEQ))
        return placed(deal_rows, finer, axes)(tokens, *others)

    return layer
```

```python
import functools
import math

import jax
import jax.numpy as jnp
from jax import lax
from jax.experimental import pallas as pl
from jax.experimental.pallas import tpu as pltpu
from jax.sharding import PartitionSpec as P

HEADS = 8
EXTRA = 16
LANES = 128
LINE_ROWS = 2
NEG_FILL = -1e30
EPSILON = 1e-05
BLOCK_CAP = 512
LOG2E = 1.4426950408889634
LN2 = 0.6931471805599453
MIB = 1 << 20


def dot(left, right, left_dim, right_dim):
    return lax.dot_general(
        left, right, (((left_dim,), (right_dim,)), ((), ())), preferred_element_type=jnp.float32
    )


def three_parts(values):
    high = values.astype(jnp.bfloat16)
    rest = values - high.astype(jnp.float32)
    middle = rest.astype(jnp.bfloat16)
    low = (rest - middle.astype(jnp.float32)).astype(jnp.bfloat16)
    return high.astype(jnp.float32), middle.astype(jnp.float32), low.astype(jnp.float32)


def extra_rows(base, values, first):
    row = lax.broadcasted_iota(jnp.int32, base.shape, 0)
    for offset, part in enumerate(three_parts(values)):
        base = jnp.where(row == first + offset, part, base)
    return base


def attend_kernel(pieces, width, block, *refs):
    row_ref, refs = refs[0], refs[1:]
    token_refs, refs = refs[:pieces], refs[pieces:]
    (
        query_extra,
        key_extra,
        query_weight,
        query_bias,
        key_weight,
        value_weight,
        value_bias,
        query_out,
        key_out,
        value_out,
        context_out,
        tokens_scratch,
        weights_scratch,
        query_scratch,
        key_scratch,
        value_scratch,
        context_scratch,
        scores_even,
        scores_odd,
        largest_even,
        largest_odd,
        in_sems,
        out_sems,
        query_sems,
        context_sems,
    ) = refs
    length = query_scratch.shape[2]
    local = length // pieces
    incoming = [
        (query_weight, weights_scratch.at[0]),
        (token_refs[0].at[row_ref[0]], tokens_scratch.at[0]),
        (key_weight, weights_scratch.at[1]),
        (value_weight, weights_scratch.at[2]),
        *[(ref.at[0], tokens_scratch.at[i + 1]) for i, ref in enumerate(token_refs[1:])],
    ]
    incoming = [
        pltpu.make_async_copy(source, target, in_sems.at[i])
        for i, (source, target) in enumerate(incoming)
    ]
    for copy in incoming:
        copy.start()
    row = lax.broadcasted_iota(jnp.int32, (EXTRA, length), 0)
    ones = (row < 3).astype(jnp.bfloat16)
    query_base = query_extra[...]
    for head in range(HEADS):
        query_scratch[head, width:] = query_base.astype(jnp.bfloat16)
        key_scratch[head, width:] = key_extra[...].astype(jnp.bfloat16)
        value_scratch[head, width:] = ones

    def upright(line):
        return jnp.broadcast_to(line, (8, line.shape[1])).T[:, :1]

    query_column, value_column = upright(query_bias[...]), upright(value_bias[...])
    shape = HEADS, width, local
    for piece in range(pieces):
        span = pl.ds(piece * local, local)
        if piece == 0:
            incoming[0].wait()
            incoming[1].wait()
        else:
            incoming[3 + piece].wait()
        tokens = tokens_scratch[piece]
        query = (dot(weights_scratch[0], tokens, 0, 1) + query_column) * (LOG2E * width**-0.5)
        query_scratch[:, :width, span] = query.astype(jnp.bfloat16).reshape(shape)
        if piece == 0:
            incoming[2].wait()
        key = dot(weights_scratch[1], tokens, 0, 1)
        key_scratch[:, :width, span] = key.astype(jnp.bfloat16).reshape(shape)
        if piece == 0:
            incoming[3].wait()
        value = dot(weights_scratch[2], tokens, 0, 1) + value_column
        value_scratch[:, :width, span] = value.astype(jnp.bfloat16).reshape(shape)
    outgoing = [
        pltpu.make_async_copy(key_scratch, key_out.at[0], out_sems.at[0]),
        pltpu.make_async_copy(value_scratch, value_out.at[0], out_sems.at[1]),
    ]
    for copy in outgoing:
        copy.start()

    def pair_copies(pair):
        heads = pl.ds(pair * 2, 2)
        rows = pl.ds(pl.multiple_of(pair * 2 * width, 2 * width), 2 * width)
        return (
            pltpu.make_async_copy(
                query_scratch.at[heads], query_out.at[0, heads], query_sems.at[pair]
            ),
            pltpu.make_async_copy(
                context_scratch.at[rows], context_out.at[rows], context_sems.at[pair]
            ),
        )

    def score(head, scores_ref, largest_ref, start):
        span = pl.ds(start, block)
        scores = dot(key_scratch[head], query_scratch[head, :, span], 0, 0)
        scores_ref[:, span] = scores
        largest_ref[:, span] = jnp.max(scores, 0, keepdims=True)

    def weigh(head, scores_ref, largest_ref, start):
        span = pl.ds(start, block)
        largest = largest_ref[:, span]
        weights = jnp.exp2(scores_ref[:, span] - largest).astype(jnp.bfloat16)
        update = dot(value_scratch[head], weights, 1, 0)
        total = update[width : width + 1]
        context_scratch[pl.ds(pl.multiple_of(head * width, width), width), span] = (
            update[:width] / total
        )
        log_total = largest + jnp.log(total) * LOG2E
        query_scratch[head, width:, span] = extra_rows(
            query_base[:, start : start + block], -log_total, 3
        ).astype(jnp.bfloat16)

    starts = range(0, length, block)
    for start in starts:
        score(0, scores_even, largest_even, start)

    def head_pair(pair, carry):
        head = pair * 2
        for start in starts:
            score(head + 1, scores_odd, largest_odd, start)
            weigh(head, scores_even, largest_even, start)
        following = jnp.minimum(head + 2, HEADS - 1)
        for start in starts:
            score(following, scores_even, largest_even, start)
            weigh(head + 1, scores_odd, largest_odd, start)
        for copy in pair_copies(pair):
            copy.start()
        return carry

    lax.fori_loop(0, HEADS // 2, head_pair, 0)
    for pair in range(HEADS // 2):
        outgoing.extend(pair_copies(pair))
    for copy in outgoing:
        copy.wait()


def attend(row_index, tokens, remote, query_extra, key_extra, weights):
    pieces = 1 + len(remote)
    local, model = tokens.shape[1:]
    length = pieces * local
    width = model // HEADS
    whole = lambda array: pl.BlockSpec(array.shape, lambda i, s: (0,) * array.ndim)
    anywhere = pl.BlockSpec(memory_space=pl.ANY)
    low = jax.ShapeDtypeStruct((1, HEADS, width + EXTRA, length), jnp.bfloat16)
    outs = (low, low, low, jax.ShapeDtypeStruct((model, length), jnp.float32))
    query_weight, query_bias, key_weight, value_weight, value_bias = weights
    head_scratch = pltpu.VMEM(low.shape[1:], jnp.bfloat16)
    return pl.pallas_call(
        functools.partial(attend_kernel, pieces, width, min(256, length)),
        out_shape=outs,
        grid_spec=pltpu.PrefetchScalarGridSpec(
            num_scalar_prefetch=1,
            grid=(1,),
            in_specs=[
                *[anywhere] * pieces,
                whole(query_extra),
                whole(key_extra),
                anywhere,
                whole(query_bias),
                anywhere,
                anywhere,
                whole(value_bias),
            ],
            out_specs=[anywhere] * 4,
            scratch_shapes=[
                pltpu.VMEM((pieces, local, model), jnp.bfloat16),
                pltpu.VMEM((3, model, model), jnp.bfloat16),
                head_scratch,
                head_scratch,
                head_scratch,
                pltpu.VMEM((model, length), jnp.float32),
                pltpu.VMEM((length, length), jnp.float32),
                pltpu.VMEM((length, length), jnp.float32),
                pltpu.VMEM((1, length), jnp.float32),
                pltpu.VMEM((1, length), jnp.float32),
                pltpu.SemaphoreType.DMA((3 + pieces,)),
                pltpu.SemaphoreType.DMA((2,)),
                pltpu.SemaphoreType.DMA((HEADS // 2,)),
                pltpu.SemaphoreType.DMA((HEADS // 2,)),
            ],
        ),
        compiler_params=pltpu.CompilerParams(vmem_limit_bytes=60 * MIB),
        cost_estimate=pl.CostEstimate(
            flops=3 * 10**9, bytes_accessed=1, transcendentals=0
        ),
        name="attend",
    )(row_index, tokens, *remote, query_extra, key_extra, *weights)


def row_mean(values):
    return jnp.mean(values, -1, keepdims=True)


def normalise(values):
    centred = values - row_mean(values)
    scale = lax.rsqrt(row_mean(centred * centred) + EPSILON)
    return centred * scale, scale


def norm_back(grad, gain, normed, scale):
    entering = grad * gain
    return (entering - row_mean(entering) - normed * row_mean(entering * normed)) * scale


def column_sum(values):
    return jnp.sum(values, 0, keepdims=True)


def gelu_parts(values):
    phi = 0.5 + 0.5 * lax.erf(values * 0.5**0.5)
    bell = jnp.exp2(values * values * (-0.5 * LOG2E))
    return values * phi, phi + values * bell * 0.3989422804014327


def token_kernel(rows, pieces, steps, width, *refs):
    _, keep_ref, me_ref, refs = *refs[:3], refs[3:]
    own_tokens, own_cotangent, refs = *refs[:2], refs[2:]
    remote_count = rows * (pieces - 1)
    remote_tokens, refs = refs[:remote_count], refs[remote_count:]
    remote_cotangents, refs = refs[:remote_count], refs[remote_count:]
    context_refs, refs = refs[:rows], refs[rows:]
    (
        out_weight,
        out_bias,
        first_gain,
        first_shift,
        up_weight,
        up_bias,
        down_weight,
        down_bias,
        second_gain,
        second_shift,
    ) = refs[:10]
    refs = refs[10:]
    layer_outs, refs = refs[: rows * pieces], refs[rows * pieces :]
    (
        grad_out_heads,
        grad_first_out,
        near_out,
        far_out,
        up_scratch,
        down_scratch,
        result_scratch,
        packed_near,
        packed_far,
        sems,
        tokens_scratch,
        cotangent_scratch,
        context_scratch,
        act_scratch,
        slope_scratch,
        totals,
        lines,
        *line_sums,
    ) = refs
    (
        grad_out_bias,
        grad_first_gain,
        grad_first_shift,
        grad_down_bias,
        grad_second_gain,
        grad_second_shift,
        grad_value_bias,
        grad_up_bias,
    ) = line_sums
    row_index = pl.program_id(0)
    piece_index = pl.program_id(1)
    step_index = pl.program_id(2)
    tokens_len, model = tokens_scratch.shape
    hidden_units = up_weight.shape[1]
    kept = keep_ref[row_index] != 0
    span = pl.ds(pl.multiple_of(step_index * tokens_len, tokens_len), tokens_len)

    @pl.when(piece_index == 0)
    def _():
        tokens_scratch[...] = own_tokens[0, span]
        cotangent_scratch[...] = own_cotangent[0, span]

    first_step = (row_index == 0) & (piece_index == 0) & (step_index == 0)
    last_step = (row_index == rows - 1) & (piece_index == pieces - 1) & (step_index == steps - 1)
    fetches = [
        pltpu.make_async_copy(up_weight, up_scratch, sems.at[0]),
        pltpu.make_async_copy(down_weight, down_scratch, sems.at[1]),
    ]

    @pl.when(first_step)
    def _():
        for copy in fetches:
            copy.start()

    for row in range(rows):

        @pl.when(row_index == row)
        def _():
            context_scratch[...] = context_refs[row][...]

        for piece in range(1, pieces):

            @pl.when((row_index == row) & (piece_index == piece))
            def _():
                position = row * (pieces - 1) + piece - 1
                tokens_scratch[...] = remote_tokens[position][0, span]
                cotangent_scratch[...] = remote_cotangents[position][0, span]

    @pl.when(first_step)
    def _():
        for ref in (totals, lines, *line_sums):
            ref[...] = jnp.zeros(ref.shape, ref.dtype)

    tokens = tokens_scratch[...].astype(jnp.float32)
    context = context_scratch[...]
    context_low = context.astype(jnp.bfloat16)
    first_sum = tokens + (dot(context_low, out_weight[...], 0, 0) + out_bias[...])
    first_normed, first_scale = normalise(first_sum)
    hidden = first_normed * first_gain[...] + first_shift[...]
    hidden_low = hidden.astype(jnp.bfloat16)

    @pl.when(first_step)
    def _():
        for copy in fetches:
            copy.wait()

    pre_act = dot(hidden_low, up_scratch[...], 1, 0) + up_bias[...]
    activated, slope = gelu_parts(pre_act)
    act_low = activated.astype(jnp.bfloat16)
    act_scratch[...] = act_low
    slope_scratch[...] = slope
    branch = dot(act_low, down_scratch[...], 1, 0) + down_bias[...]
    second_normed, second_scale = normalise(hidden + branch)
    result = jnp.where(
        kept, second_normed * second_gain[...] + second_shift[...], tokens
    ).astype(jnp.bfloat16)
    gives = [
        pltpu.make_async_copy(result_scratch, ref.at[0, span], sems.at[2]) for ref in layer_outs
    ]

    @pl.when(jnp.logical_not(first_step))
    def _():
        gives[0].wait()

    result_scratch[...] = result
    for position, copy in enumerate(gives):

        @pl.when(row_index * pieces + piece_index == position)
        def _():
            copy.start()

    cotangent = cotangent_scratch[...].astype(jnp.float32)
    grad_out = jnp.where(kept, cotangent, 0.0)
    grad_second_gain[...] += column_sum(grad_out * second_normed)
    grad_second_shift[...] += column_sum(grad_out)
    grad_second = norm_back(grad_out, second_gain[...], second_normed, second_scale)
    grad_branch_low = grad_second.astype(jnp.bfloat16)
    grad_down_bias[...] += column_sum(grad_branch_low.astype(jnp.float32))
    grad_act = dot(grad_branch_low, down_scratch[...], 1, 1)
    grad_pre_low = (grad_act * slope_scratch[...]).astype(jnp.bfloat16)
    grad_hidden = grad_second + dot(grad_pre_low, up_scratch[...], 1, 1)
    totals[pl.ds(hidden_units, hidden_units), :] += dot(act_scratch[...], grad_branch_low, 0, 0)
    for start in range(0, hidden_units, model):
        totals[pl.ds(start, model), :] += dot(
            hidden_low, grad_pre_low[:, start : start + model], 0, 0
        )
    grad_up_bias[...] += column_sum(grad_pre_low.astype(jnp.float32))
    grad_first_gain[...] += column_sum(grad_hidden * first_normed)
    grad_first_shift[...] += column_sum(grad_hidden)
    grad_first = norm_back(grad_hidden, first_gain[...], first_normed, first_scale)
    grad_first_out[0] = jnp.where(kept, grad_first, cotangent)
    grad_attn_low = grad_first.astype(jnp.bfloat16)
    grad_out_bias[...] += column_sum(grad_attn_low.astype(jnp.float32))
    totals[pl.ds(2 * hidden_units, model), :] += dot(context_low, grad_attn_low, 1, 0)
    grad_context = dot(out_weight[...], grad_attn_low, 1, 1).astype(jnp.bfloat16)
    grad_context_wide = grad_context.astype(jnp.float32)
    ones = jnp.ones((EXTRA, tokens_len), jnp.bfloat16)
    grad_value_bias[...] += dot(ones, grad_context, 1, 1)[:1]
    product = grad_context_wide * context
    blank = jnp.zeros((EXTRA, tokens_len), jnp.float32)
    for head in range(HEADS):
        columns = slice(head * width, (head + 1) * width)
        grad_out_heads[0, head, :width] = grad_context[columns]
        spread = jnp.sum(product[columns], 0, keepdims=True)
        grad_out_heads[0, head, width:] = extra_rows(blank, -spread, 0).astype(jnp.bfloat16)

    @pl.when(last_step)
    def _():
        first = 0
        for ref in line_sums:
            set_lines(lines, first, ref[...])
            first += ref.shape[1] // LANES
        copies = [gives[0]]
        for half, out, sem in ((packed_far, far_out, 0), (packed_near, near_out, 1)):
            pack([totals], lines, *((None, half) if sem == 0 else (half, None)), me_ref[0])
            copies.append(pltpu.make_async_copy(half, out, sems.at[sem]))
            copies[-1].start()
        for copy in copies:
            copy.wait()


def set_lines(lines, first, values):
    width = lines.shape[2]
    for block in range(values.shape[1] // width):
        slot, row = divmod(first + block, LINE_ROWS)
        lines[slot, row : row + 1] = values[:, block * width : (block + 1) * width]


def pack(parts, lines, near, far, me):
    half, size, width = (near if far is None else far).shape
    columns = [(ref, start) for ref in parts for start in range(0, ref.shape[1], width)]
    height = parts[0].shape[0] // (2 * half)

    def one(slot, carry):
        for ref, first in ((near, 0), (far, half)):
            if ref is None:
                continue
            piece = (slot + first) ^ me
            rows = pl.ds(pl.multiple_of(piece * height, EXTRA), height)
            for block, (source, start) in enumerate(columns):
                ref[slot, pl.ds(block * height, height), :] = source[
                    rows, pl.ds(start, width)
                ].astype(jnp.bfloat16)
            ref[slot, pl.ds(len(columns) * height, EXTRA), :] = jnp.concatenate(
                [lines[piece], jnp.zeros_like(lines[piece])], 0
            ).astype(jnp.bfloat16)
        return carry

    lax.fori_loop(0, half, one, 0)


def packed_shape(slots, rows, model):
    return jax.ShapeDtypeStruct(
        (slots // 2, rows * (model // LANES) // slots + EXTRA, LANES), jnp.bfloat16
    )


def lines_shape(slots):
    return pltpu.VMEM((slots, EXTRA // 2, LANES), jnp.float32)


def by_token(
    row_index, keep, me, tokens, remote, cotangent, remote_cotangent, contexts, weights, slots
):
    rows = len(contexts)
    pieces = 1 + len(remote[0])
    local, model = tokens.shape[1:]
    length = pieces * local
    width = model // HEADS
    hidden_units = weights[4].shape[1]
    tokens_len = min(512, local)
    steps = local // tokens_len
    whole = lambda array: pl.BlockSpec(array.shape, lambda r, i, j, s, k, m: (0,) * array.ndim)
    own_spec = pl.BlockSpec((1, local, model), lambda r, i, j, s, k, m: (s[0] + r, 0, 0))
    f32 = lambda *shape: jax.ShapeDtypeStruct(shape, jnp.float32)
    anywhere = pl.BlockSpec(memory_space=pl.ANY)
    total_rows = 2 * hidden_units + model
    packed = packed_shape(slots, total_rows, model)
    piece_out = jax.ShapeDtypeStruct((1, local, model), jnp.bfloat16)
    gradient_outs = (packed, packed)
    line_lengths = [model] * 7 + [hidden_units]
    outs = (
        *([piece_out] * (rows * pieces)),
        jax.ShapeDtypeStruct((rows, HEADS, width + EXTRA, length), jnp.bfloat16),
        f32(rows, length, model),
        *gradient_outs,
    )
    out_specs = (
        *([anywhere] * (rows * pieces)),
        pl.BlockSpec(
            (1, HEADS, width + EXTRA, tokens_len),
            lambda r, i, j, s, k, m: (r, 0, 0, i * steps + j),
        ),
        pl.BlockSpec((1, tokens_len, model), lambda r, i, j, s, k, m: (r, i * steps + j, 0)),
        anywhere,
        anywhere,
    )

    def context_spec(row):
        def block(r, i, j, s, k, m):
            step = i * steps + j
            return 0, jnp.where(r < row, 0, jnp.where(r > row, pieces * steps - 1, step))

        return pl.BlockSpec((model, tokens_len), block)

    flat_remote = [array for arrays in remote for array in arrays]
    flat_remote_cotangent = [array for arrays in remote_cotangent for array in arrays]
    in_specs = (
        own_spec,
        own_spec,
        *[whole(a) for a in (*flat_remote, *flat_remote_cotangent)],
        *[context_spec(row) for row in range(rows)],
        *[anywhere if a.shape[0] * a.shape[1] > model * model else whole(a) for a in weights],
    )
    return pl.pallas_call(
        functools.partial(token_kernel, rows, pieces, steps, width),
        out_shape=outs,
        grid_spec=pltpu.PrefetchScalarGridSpec(
            num_scalar_prefetch=3,
            grid=(rows, pieces, steps),
            in_specs=in_specs,
            out_specs=out_specs,
            scratch_shapes=[
                pltpu.VMEM((model, hidden_units), jnp.bfloat16),
                pltpu.VMEM((hidden_units, model), jnp.bfloat16),
                pltpu.VMEM((tokens_len, model), jnp.bfloat16),
                pltpu.VMEM(packed.shape, jnp.bfloat16),
                pltpu.VMEM(packed.shape, jnp.bfloat16),
                pltpu.SemaphoreType.DMA((3,)),
                pltpu.VMEM((tokens_len, model), jnp.bfloat16),
                pltpu.VMEM((tokens_len, model), jnp.bfloat16),
                pltpu.VMEM((model, tokens_len), jnp.float32),
                pltpu.VMEM((tokens_len, hidden_units), jnp.bfloat16),
                pltpu.VMEM((tokens_len, hidden_units), jnp.float32),
                pltpu.VMEM((total_rows, model), jnp.float32),
                lines_shape(slots),
                *[pltpu.VMEM((1, n), jnp.float32) for n in line_lengths],
            ],
        ),
        compiler_params=pltpu.CompilerParams(vmem_limit_bytes=60 * MIB),
        cost_estimate=pl.CostEstimate(flops=1, bytes_accessed=1, transcendentals=0),
        name="by_token",
    )(
        row_index,
        keep,
        me,
        tokens,
        cotangent,
        *flat_remote,
        *flat_remote_cotangent,
        *contexts,
        *weights,
    )


def attend_back_kernel(pieces, width, block, place, *refs):
    row, rows, part, parts = place
    first_row, last_part = row == 0, part == parts - 1
    packing = row == rows - 1 and last_part
    row_ref, me_ref, refs = *refs[:2], refs[2:]
    token_refs, refs = refs[:pieces], refs[pieces:]
    head_refs, refs = refs[:4], refs[4:]
    grad_tokens_in, *weight_refs, refs = *refs[:4], refs[4:]
    if not first_row:
        totals_in, bias_in, refs = *refs[:2], refs[2:]
    earlier = part if packing else 0
    earlier_totals, refs = refs[:earlier], refs[earlier:]
    earlier_biases, refs = refs[:earlier], refs[earlier:]
    outs = pieces if last_part else 1
    grad_tokens, refs = refs[:outs], refs[outs:]
    if packing:
        packed_near, packed_far, *refs = refs
    else:
        totals_out, bias, *refs = refs
    (
        grad_query_scratch,
        grad_key_scratch,
        grad_value_scratch,
        tokens_scratch,
        grad_scratch,
        weights_scratch,
        totals,
        sems,
        *refs,
    ) = refs
    if packing:
        lines, bias, *earlier_scratch = refs
    query_ref, key_ref, value_ref, grad_ref = (ref.at[0] for ref in head_refs)
    pair = pl.program_id(0)
    pairs = pl.num_programs(0)
    length = query_ref.shape[2]
    local = length // pieces
    model, columns = weights_scratch.shape[1:]
    pair_width = 2 * width
    share = pl.ds(part * columns, columns)
    incoming = [(token_refs[0].at[row_ref[0]], tokens_scratch.at[0])]
    incoming += [(ref.at[0], tokens_scratch.at[i + 1]) for i, ref in enumerate(token_refs[1:])]
    incoming.append((grad_tokens_in.at[row if part == 0 else 0], grad_scratch))
    incoming += [(ref.at[:, share], weights_scratch.at[i]) for i, ref in enumerate(weight_refs)]
    if not first_row:
        incoming.append((totals_in, totals))
    if packing:
        incoming += list(zip(earlier_totals, earlier_scratch))
    incoming = [
        pltpu.make_async_copy(source, target, sems.at[i])
        for i, (source, target) in enumerate(incoming)
    ]

    @pl.when(pair == 0)
    def _():
        for copy in incoming:
            copy.start()

    grad_queries = [[], []]
    for side in range(2):
        key = key_ref[side]
        value = value_ref[side]
        grad_key = 0.0
        grad_value = 0.0
        for start in range(0, length, block):
            span = pl.ds(start, block)
            query = query_ref[side, :, span]
            grad = grad_ref[side, :, span]
            weights = jnp.exp2(dot(query, key, 0, 0))
            grad_weights = dot(grad, value, 0, 0)
            weights_low = weights.astype(jnp.bfloat16)
            grad_scores = (weights * grad_weights).astype(jnp.bfloat16)
            grad_value = grad_value + dot(grad[:width], weights_low, 1, 0)
            grad_key = grad_key + dot(query[:width], grad_scores, 1, 0)
            grad_queries[side].append(dot(grad_scores, key[:width], 1, 1))
        head = pl.ds(pl.multiple_of(pair * pair_width + side * width, width), width)
        grad_value_scratch[head, :] = grad_value.astype(jnp.bfloat16)
        grad_key_scratch[head, :] = (grad_key * LN2).astype(jnp.bfloat16)
    for index, start in enumerate(range(0, length, block)):
        both = jnp.concatenate([grad_queries[0][index], grad_queries[1][index]], 1)
        grad_query_scratch[pair, pl.ds(start, block)] = (both * width**-0.5).astype(jnp.bfloat16)

    @pl.when(pair == pairs - 1)
    def _():
        for copy in incoming:
            copy.wait()
        count = grad_query_scratch.shape[0]
        for index in range(count):
            lanes = pl.ds(index * pair_width, pair_width)
            total = column_sum(grad_query_scratch[index].astype(jnp.float32))
            bias[:, lanes] = total if first_row else bias_in[:, lanes] + total
        grad_query = jnp.concatenate([grad_query_scratch[index] for index in range(count)], 1)
        outgoing = []
        for position in range(3):
            lines_of = pl.ds(position * model, model)
            term = 0.0
            for piece in range(pieces):
                span = slice(piece * local, (piece + 1) * local)
                tokens = tokens_scratch[piece]
                if position == 0:
                    term = term + dot(tokens, grad_query[span], 0, 0)
                else:
                    source = grad_key_scratch if position == 1 else grad_value_scratch
                    term = term + dot(tokens, source[:, span], 0, 1)
            totals[lines_of, :] = term if first_row else totals[lines_of, :] + term
        if not packing:
            outgoing.append(pltpu.make_async_copy(totals, totals_out, sems.at[0]))
            outgoing[0].start()
        for piece in range(pieces):
            span = pl.ds(piece * local, local)
            total = (
                grad_scratch[span]
                + dot(grad_query[piece * local : (piece + 1) * local], weights_scratch[0], 1, 1)
                + dot(grad_key_scratch[:, span], weights_scratch[1], 0, 1)
                + dot(grad_value_scratch[:, span], weights_scratch[2], 0, 1)
            )
            if last_part:
                grad_tokens[piece][0] = total.astype(jnp.bfloat16)
            else:
                grad_scratch[span] = total
                outgoing.append(
                    pltpu.make_async_copy(
                        grad_scratch.at[span], grad_tokens[0].at[0, span], sems.at[1 + piece]
                    )
                )
                outgoing[-1].start()
        if packing:
            lines[...] = jnp.zeros(lines.shape, lines.dtype)
            first = 0
            for ref in (*earlier_biases, bias):
                set_lines(lines, first, ref[...])
                first += ref.shape[1] // LANES
            pack([*earlier_scratch, totals], lines, packed_near, packed_far, me_ref[0])
        for copy in outgoing:
            copy.wait()


def attend_back(
    place, row_index, me, tokens, remote, heads, grad_tokens, weights, totals, biases, slots, gflops
):
    row, rows, part, parts = place
    last_part = part == parts - 1
    packing = row == rows - 1 and last_part
    pieces = 1 + len(remote)
    local, model = tokens.shape[1:]
    length = pieces * local
    width = model // HEADS
    columns = model // parts
    pairs = HEADS // parts // 2
    anywhere = pl.BlockSpec(memory_space=pl.ANY)
    whole = lambda array: pl.BlockSpec(array.shape, lambda i, s, m: (0,) * array.ndim)
    head_spec = lambda array: pl.BlockSpec(
        (1, 2, *array.shape[2:]),
        lambda i, s, m: (row if array.shape[0] > 1 else 0, part * pairs + i, 0, 0),
    )
    f32 = lambda *shape: jax.ShapeDtypeStruct(shape, jnp.float32)
    if last_part:
        outs = [jax.ShapeDtypeStruct((1, local, model), jnp.bfloat16)] * pieces
        out_specs = [whole(a) for a in outs]
    else:
        outs, out_specs = [f32(1, length, model)], [anywhere]
    total, bias = f32(3 * model, columns), f32(1, columns)
    in_specs = [anywhere] * pieces + [head_spec(a) for a in heads] + [anywhere] * 4
    operands = [tokens, *remote, *heads, grad_tokens, *weights]
    if row:
        operands += [totals[part], biases[part]]
        in_specs += [anywhere, whole(bias)]
    scratch = [
        pltpu.VMEM((pairs, length, 2 * width), jnp.bfloat16),
        pltpu.VMEM((columns, length), jnp.bfloat16),
        pltpu.VMEM((columns, length), jnp.bfloat16),
        pltpu.VMEM((pieces, local, model), jnp.bfloat16),
        pltpu.VMEM((length, model), jnp.float32),
        pltpu.VMEM((3, model, columns), jnp.bfloat16),
        pltpu.VMEM(total.shape, jnp.float32),
        pltpu.SemaphoreType.DMA((pieces + 5 + parts,)),
    ]
    if packing:
        operands += [*totals[:part], *biases[:part]]
        in_specs += [anywhere] * part + [whole(bias)] * part
        packed = packed_shape(slots, 3 * model, model)
        outs += [packed] * 2
        out_specs += [whole(packed)] * 2
        scratch += [lines_shape(slots), pltpu.VMEM(bias.shape, jnp.float32)]
        scratch += [pltpu.VMEM(total.shape, jnp.float32)] * part
    else:
        outs += [total, bias]
        out_specs += [anywhere, whole(bias)]
    return pl.pallas_call(
        functools.partial(attend_back_kernel, pieces, width, min(256, length), place),
        out_shape=outs,
        grid_spec=pltpu.PrefetchScalarGridSpec(
            num_scalar_prefetch=2,
            grid=(pairs,),
            in_specs=in_specs,
            out_specs=out_specs,
            scratch_shapes=scratch,
        ),
        compiler_params=pltpu.CompilerParams(vmem_limit_bytes=60 * MIB),
        cost_estimate=pl.CostEstimate(
            flops=gflops * 10**9, bytes_accessed=1, transcendentals=0
        ),
        name="attend_back",
    )(row_index, me, *operands)


def unpack_kernel(moves, model, counts, me_ref, *refs):
    sources, refs = refs[: counts[0]], refs[counts[0] :]
    outs, refs = refs[: counts[1]], refs[counts[1] :]
    lines, refs = refs[: counts[2]], refs[counts[2] :]
    *blocks_out, slots, in_sems, out_sems = refs
    count = counts[0]
    _, size, width = slots.shape
    me = me_ref[0]
    share = slots.shape[0] // count
    copies = [
        pltpu.make_async_copy(source, slots.at[pl.ds(index * share, share)], in_sems.at[index])
        for index, source in enumerate(sources)
    ]
    for copy in copies:
        copy.start()
    for copy in copies:
        copy.wait()
    index = 0
    for line in lines:
        for block in range(line.shape[1] // width):
            piece, row = divmod(index, LINE_ROWS)
            extra = slots[piece ^ me, pl.ds(size - EXTRA, EXTRA), :].astype(jnp.float32)
            line[:, pl.ds(block * width, width)] = extra[row : row + 1]
            index += 1
    copies = []
    for square, (out, row, column, pieces) in enumerate(moves):
        for piece, start, rows, inside, offset in pieces:
            blocks_out[out][pl.ds(row + inside, rows), pl.ds(column + offset, width)] = slots[
                piece ^ me, pl.ds(start, rows), :
            ].astype(jnp.float32)
        part = pl.ds(row, model), pl.ds(column, model)
        copies.append(
            pltpu.make_async_copy(
                blocks_out[out].at[part], outs[out].at[part], out_sems.at[square]
            )
        )
        copies[-1].start()
    for copy in copies:
        copy.wait()


def unpack(me, arrays, shapes, model, lengths):
    share, size, width = arrays[0].shape
    slots = share * len(arrays)
    blocks = model // width
    height = (size - EXTRA) // blocks
    moves = [
        (out, row, column, [])
        for out, shape in enumerate(shapes)
        for row in range(0, shape[0], model)
        for column in range(0, shape[1], model)
    ]
    for piece in range(slots):
        done = 0
        while done < height:
            square, inside = divmod(piece * height + done, model)
            rows = min(height - done, model - inside)
            for block in range(blocks):
                moves[square][3].append(
                    (piece, block * height + done, rows, inside, block * width)
                )
            done += rows
    outs = [jax.ShapeDtypeStruct(shape, jnp.float32) for shape in shapes]
    lines = [jax.ShapeDtypeStruct((1, n), jnp.float32) for n in lengths]
    anywhere = pl.BlockSpec(memory_space=pl.ANY)
    return pl.pallas_call(
        functools.partial(unpack_kernel, moves, model, (len(arrays), len(outs), len(lines))),
        out_shape=[*outs, *lines],
        grid_spec=pltpu.PrefetchScalarGridSpec(
            num_scalar_prefetch=1,
            grid=(1,),
            in_specs=[anywhere] * len(arrays),
            out_specs=[
                *[anywhere] * len(outs),
                *[pl.BlockSpec(a.shape, lambda i, m: (0, 0)) for a in lines],
            ],
            scratch_shapes=[
                *[pltpu.VMEM(a.shape, jnp.float32) for a in outs],
                pltpu.VMEM((slots, size, width), jnp.bfloat16),
                pltpu.SemaphoreType.DMA((len(arrays),)),
                pltpu.SemaphoreType.DMA((len(moves),)),
            ],
        ),
        compiler_params=pltpu.CompilerParams(vmem_limit_bytes=60 * MIB),
        cost_estimate=pl.CostEstimate(
            flops=2 * 10**10, bytes_accessed=1, transcendentals=0
        ),
        name="unpack",
    )(me, *arrays)


NEAR, MIDDLE, FAR, SEQ = AXES = ("near", "middle", "far", "seq")
STAGES = ((NEAR,), (MIDDLE, SEQ), (FAR,))


def add_up(arrays):
    arrays = [a.astype(jnp.float32) for a in arrays]
    while len(arrays) > 1:
        arrays = [first + second for first, second in zip(arrays[::2], arrays[1::2], strict=True)]
    return arrays[0].astype(jnp.bfloat16)


def after(arrays, *others):
    return lax.optimization_barrier((arrays, others))[0]


class Sums:
    def __init__(self):
        self.sizes = [lax.axis_size(axes) for axes in STAGES]
        self.devices = math.prod(self.sizes)
        digits = [lax.axis_index(axes) for axes in STAGES]
        self.me = (digits[0] * self.sizes[1] + digits[1]) * self.sizes[2] + digits[2]
        self.me_near = self.me - digits[2]

    def swap(self, array, stage, turn):
        pairs = [(i, i ^ turn) for i in range(self.sizes[stage])]
        return lax.ppermute(array, STAGES[stage], pairs)

    def meet(self, parts, stage):
        return [parts[0], *[self.swap(parts[t], stage, t) for t in range(1, len(parts))]]

    def add_parts(self, arrays, stage):
        size = self.sizes[stage]
        share = arrays[0].shape[0] // size
        return [
            add_up([array[turn * share : (turn + 1) * share] for array in arrays])
            for turn in range(size)
        ]

    def others(self, held, stage):
        return [self.swap(held, stage, turn) for turn in range(1, self.sizes[stage])]


def norm_rows(values, gain, shift):
    row_mean = jnp.mean(values, -1, keepdims=True)
    centred = values - row_mean
    variance = jnp.mean(centred * centred, -1, keepdims=True)
    return centred * lax.rsqrt(variance + EPSILON) * gain + shift


def gelu_exact(values):
    return jax.nn.gelu(values, approximate=False)


def plain_dot(left, right):
    return jnp.dot(left, right, preferred_element_type=jnp.float32)


def left_dot(left, right):
    return lax.dot_general(
        left, right, (((0,), (0,)), ((), ())), preferred_element_type=jnp.float32
    )


def right_dot(left, right):
    return lax.dot_general(
        left, right, (((1,), (1,)), ((), ())), preferred_element_type=jnp.float32
    )


def token_sum(values):
    return jnp.sum(values.astype(jnp.float32), 0)


def split_heads(values, piece_len):
    return values.reshape(values.shape[0], piece_len, HEADS, values.shape[2] // HEADS)


def block_length(piece_len, local_len):
    return math.gcd(math.gcd(piece_len, local_len), BLOCK_CAP)


def masked_scores(query_heads, key_heads, query_ids, key_ids, score_scale):
    scores = (
        jnp.einsum("rqhd,rkhd->rhqk", query_heads, key_heads, preferred_element_type=jnp.float32)
        * score_scale
    )
    same_doc = query_ids[:, None, :, None] == key_ids[:, None, None, :]
    return jnp.where(same_doc, scores, NEG_FILL)


def split_attend_back(
    query_heads,
    grad_heads,
    log_total,
    spread,
    query_ids,
    key_heads,
    value_heads,
    key_ids,
    score_scale,
):
    scores = masked_scores(query_heads, key_heads, query_ids, key_ids, score_scale)
    weights = jnp.exp(scores - jnp.transpose(log_total, (0, 2, 1))[..., None])
    grad_value = jnp.einsum(
        "rhqk,rqhd->rkhd",
        weights.astype(jnp.bfloat16),
        grad_heads,
        preferred_element_type=jnp.float32,
    )
    grad_weights = jnp.einsum(
        "rqhd,rkhd->rhqk", grad_heads, value_heads, preferred_element_type=jnp.float32
    )
    grad_scores = (weights * (grad_weights - jnp.transpose(spread, (0, 2, 1))[..., None])).astype(
        jnp.bfloat16
    )
    grad_query = (
        jnp.einsum("rhqk,rkhd->rqhd", grad_scores, key_heads, preferred_element_type=jnp.float32)
        * score_scale
    )
    grad_key = (
        jnp.einsum("rhqk,rqhd->rkhd", grad_scores, query_heads, preferred_element_type=jnp.float32)
        * score_scale
    )
    return (grad_query, grad_key, grad_value)


def add_into(buffer, term, block_start):
    current = lax.dynamic_slice_in_dim(buffer, block_start, term.shape[1], 1)
    return lax.dynamic_update_slice_in_dim(buffer, current + term, block_start, 1)


def split_rows(
    tokens,
    segments,
    keep_flags,
    query_weight,
    query_bias,
    key_weight,
    value_weight,
    value_bias,
    out_weight,
    out_bias,
    first_gain,
    first_shift,
    up_weight,
    up_bias,
    down_weight,
    down_bias,
    second_gain,
    second_shift,
    cotangent,
):
    row_count, local_tokens, model_width = tokens.shape
    head_width = model_width // HEADS
    score_scale = head_width ** (-0.5)
    flat_tokens = tokens.reshape(row_count * local_tokens, model_width)
    row_shape = (row_count, local_tokens, model_width)
    query_low = (
        (plain_dot(flat_tokens, query_weight) + query_bias).astype(jnp.bfloat16).reshape(row_shape)
    )
    key_low = plain_dot(flat_tokens, key_weight).astype(jnp.bfloat16).reshape(row_shape)
    value_low = (
        (plain_dot(flat_tokens, value_weight) + value_bias).astype(jnp.bfloat16).reshape(row_shape)
    )
    query_heads = split_heads(query_low, local_tokens)
    own_start = lax.axis_index("seq") * local_tokens
    own_ids = lax.dynamic_slice_in_dim(segments, own_start, local_tokens, 1)
    initial = (
        jnp.full((row_count, HEADS, local_tokens), NEG_FILL, jnp.float32),
        jnp.zeros((row_count, HEADS, local_tokens), jnp.float32),
        jnp.zeros((row_count, HEADS, local_tokens, head_width), jnp.float32),
    )
    key_piece = lax.all_gather(key_low, "seq", axis=1, tiled=True)
    value_piece = lax.all_gather(value_low, "seq", axis=1, tiled=True)
    block_size = block_length(key_piece.shape[1], local_tokens)

    def key_step(position, inner_state):
        running_max, running_sum, running_acc = inner_state
        block_start = position * block_size
        key_heads = split_heads(
            lax.dynamic_slice_in_dim(key_piece, block_start, block_size, 1), block_size
        )
        value_heads = split_heads(
            lax.dynamic_slice_in_dim(value_piece, block_start, block_size, 1), block_size
        )
        key_ids = lax.dynamic_slice_in_dim(segments, block_start, block_size, 1)
        scores = masked_scores(query_heads, key_heads, own_ids, key_ids, score_scale)
        newest = jnp.maximum(running_max, jnp.max(scores, -1))
        factor = jnp.exp(running_max - newest)
        weights = jnp.exp(scores - newest[..., None])
        running_sum = running_sum * factor + jnp.sum(weights, -1)
        update = jnp.einsum(
            "rhqk,rkhd->rhqd",
            weights.astype(jnp.bfloat16),
            value_heads,
            preferred_element_type=jnp.float32,
        )
        return (newest, running_sum, running_acc * factor[..., None] + update)

    running_max, running_sum, running_acc = lax.fori_loop(
        0, key_piece.shape[1] // block_size, key_step, initial
    )
    context_heads = jnp.transpose(running_acc / running_sum[..., None], (0, 2, 1, 3))
    log_total = jnp.transpose(running_max + jnp.log(running_sum), (0, 2, 1))
    context_low = context_heads.reshape(row_count * local_tokens, model_width).astype(jnp.bfloat16)
    first_sum = flat_tokens.astype(jnp.float32) + (plain_dot(context_low, out_weight) + out_bias)
    hidden, first_back = jax.vjp(norm_rows, first_sum, first_gain, first_shift)
    hidden_low = hidden.astype(jnp.bfloat16)
    pre_act = plain_dot(hidden_low, up_weight) + up_bias
    activated, act_back = jax.vjp(gelu_exact, pre_act)
    act_low = activated.astype(jnp.bfloat16)
    second_sum = hidden + (plain_dot(act_low, down_weight) + down_bias)
    normed, second_back = jax.vjp(norm_rows, second_sum, second_gain, second_shift)
    kept_rows = (keep_flags != 0)[:, None, None]
    layer_out = jnp.where(kept_rows, normed.reshape(row_shape), tokens.astype(jnp.float32)).astype(
        jnp.bfloat16
    )
    grad_out = jnp.where(kept_rows, cotangent.astype(jnp.float32), 0.0).reshape(
        row_count * local_tokens, model_width
    )
    grad_second, grad_second_gain, grad_second_shift = second_back(grad_out)
    grad_branch_low = grad_second.astype(jnp.bfloat16)
    grad_down_bias = token_sum(grad_branch_low)
    grad_down_weight = left_dot(act_low, grad_branch_low)
    (grad_pre,) = act_back(right_dot(grad_branch_low, down_weight))
    grad_pre_low = grad_pre.astype(jnp.bfloat16)
    grad_up_bias = token_sum(grad_pre_low)
    grad_up_weight = left_dot(hidden_low, grad_pre_low)
    grad_hidden = grad_second + right_dot(grad_pre_low, up_weight)
    grad_first, grad_first_gain, grad_first_shift = first_back(grad_hidden)
    grad_attn_low = grad_first.astype(jnp.bfloat16)
    grad_out_bias = token_sum(grad_attn_low)
    grad_out_weight = left_dot(context_low, grad_attn_low)
    late_grads = (
        grad_out_weight,
        grad_out_bias,
        grad_first_gain,
        grad_first_shift,
        grad_up_weight,
        grad_up_bias,
        grad_down_weight,
        grad_down_bias,
        grad_second_gain,
        grad_second_shift,
    )
    grad_context_low = right_dot(grad_attn_low, out_weight).astype(jnp.bfloat16)
    grad_context_rows = grad_context_low.reshape(row_shape)
    grad_heads = split_heads(grad_context_rows, local_tokens)
    spread = jnp.sum(grad_heads.astype(jnp.float32) * context_heads, -1)
    zero_local = jnp.zeros((row_count, local_tokens, HEADS, head_width), jnp.float32)
    zero_whole = jnp.zeros(
        (row_count, local_tokens * lax.axis_size("seq"), HEADS, head_width), jnp.float32
    )
    gathered_total, gathered_spread = (
        lax.all_gather(log_total, "seq", axis=1, tiled=True),
        lax.all_gather(spread, "seq", axis=1, tiled=True),
    )
    key_heads_local = split_heads(key_low, local_tokens)
    value_heads_local = split_heads(value_low, local_tokens)
    query_piece = lax.all_gather(query_low, "seq", axis=1, tiled=True)
    grad_piece = lax.all_gather(grad_context_rows, "seq", axis=1, tiled=True)
    back_block_size = block_length(query_piece.shape[1], local_tokens)

    def query_step(position, inner_state):
        grad_key, grad_value, queries_whole = inner_state
        block_start = position * back_block_size
        part_query, part_key, part_value = split_attend_back(
            split_heads(
                lax.dynamic_slice_in_dim(query_piece, block_start, back_block_size, 1),
                back_block_size,
            ),
            split_heads(
                lax.dynamic_slice_in_dim(grad_piece, block_start, back_block_size, 1),
                back_block_size,
            ),
            lax.dynamic_slice_in_dim(gathered_total, block_start, back_block_size, 1),
            lax.dynamic_slice_in_dim(gathered_spread, block_start, back_block_size, 1),
            lax.dynamic_slice_in_dim(segments, block_start, back_block_size, 1),
            key_heads_local,
            value_heads_local,
            own_ids,
            score_scale,
        )
        return (
            grad_key + part_key,
            grad_value + part_value,
            add_into(queries_whole, part_query, block_start),
        )

    grad_key, grad_value, queries_whole = lax.fori_loop(
        0, query_piece.shape[1] // back_block_size, query_step, (zero_local, zero_local, zero_whole)
    )
    grad_query = lax.psum_scatter(queries_whole, "seq", scatter_dimension=1, tiled=True)
    flat_shape = (row_count * local_tokens, model_width)
    grad_query_low = grad_query.reshape(flat_shape).astype(jnp.bfloat16)
    grad_key_low = grad_key.reshape(flat_shape).astype(jnp.bfloat16)
    grad_value_low = grad_value.reshape(flat_shape).astype(jnp.bfloat16)
    grad_query_bias = token_sum(grad_query_low)
    grad_query_weight = left_dot(flat_tokens, grad_query_low)
    grad_key_weight = left_dot(flat_tokens, grad_key_low)
    grad_value_bias = token_sum(grad_value_low)
    grad_value_weight = left_dot(flat_tokens, grad_value_low)
    grad_flat = (
        grad_first
        + right_dot(grad_query_low, query_weight)
        + right_dot(grad_key_low, key_weight)
        + right_dot(grad_value_low, value_weight)
    )
    tokens_grad = jnp.where(
        kept_rows, grad_flat.reshape(row_shape), cotangent.astype(jnp.float32)
    ).astype(jnp.bfloat16)
    early_grads = (
        grad_query_weight,
        grad_query_bias,
        grad_key_weight,
        grad_value_weight,
        grad_value_bias,
    )
    summed = lax.psum(
        (
            grad_query_weight,
            grad_query_bias,
            grad_key_weight,
            grad_value_weight,
            grad_value_bias,
            grad_out_weight,
            grad_out_bias,
            grad_first_gain,
            grad_first_shift,
            grad_up_weight,
            grad_up_bias,
            grad_down_weight,
            grad_down_bias,
            grad_second_gain,
            grad_second_shift,
        ),
        ("dp", "seq"),
    )
    early_grads = summed[:5]
    late_grads = summed[5:]
    return (
        layer_out,
        tokens_grad,
        early_grads[0],
        early_grads[1],
        early_grads[2],
        early_grads[3],
        early_grads[4],
        late_grads[0],
        late_grads[1],
        late_grads[2],
        late_grads[3],
        late_grads[4],
        late_grads[5],
        late_grads[6],
        late_grads[7],
        late_grads[8],
        late_grads[9],
    )


def deal_rows(
    tokens,
    segments,
    keep_flags,
    query_weight,
    query_bias,
    key_weight,
    value_weight,
    value_bias,
    out_weight,
    out_bias,
    first_gain,
    first_shift,
    up_weight,
    up_bias,
    down_weight,
    down_bias,
    second_gain,
    second_shift,
    cotangent,
):
    row_count, local_tokens, model = tokens.shape
    ring = lax.axis_size("seq")
    me = lax.axis_index("seq")
    rows = row_count // ring
    first_row = me * rows
    turns = [[(i, (i + turn) % ring) for i in range(ring)] for turn in range(ring)]
    back_turns = [[(i, (i - turn) % ring) for i in range(ring)] for turn in range(ring)]

    def fetch(array, row, turn, before):
        theirs = lax.rem(me + turn, ring) * rows + row
        sent = after(lax.dynamic_slice_in_dim(array, theirs, 1, 0), before)
        return lax.ppermute(sent, "seq", turns[turn])

    remote, remote_cotangent, arrived = [], [], ()
    for row in range(rows):
        for array, fetched in ((tokens, remote), (cotangent, remote_cotangent)):
            fetched.append([fetch(array, row, turn, arrived) for turn in range(1, ring)])
            arrived = arrived or remote[row]
        arrived = remote[row]
    own_segments = lax.dynamic_slice_in_dim(segments, first_row, rows, 0)
    own_segments = jnp.concatenate(
        [
            lax.dynamic_slice_in_dim(
                own_segments, lax.rem(me - turn + ring, ring) * local_tokens, local_tokens, 1
            )
            for turn in range(ring)
        ],
        1,
    )
    extra_index = jnp.arange(EXTRA, dtype=jnp.int32)[None, :, None]
    same = own_segments[:, None, :] == extra_index
    query_extra = jnp.where(same & (extra_index < 3), 1.0, 0.0)
    key_extra = jnp.where(
        extra_index < 3, jnp.where(same, 0.0, NEG_FILL), jnp.where(extra_index < 6, 1.0, 0.0)
    )
    keep = lax.dynamic_slice_in_dim(keep_flags, first_row, rows, 0)
    line = lambda vector: vector.reshape(1, -1)
    forward_weights = (
        query_weight,
        line(query_bias),
        key_weight,
        value_weight,
        line(value_bias),
    )
    token_weights = (
        out_weight,
        line(out_bias),
        line(first_gain),
        line(first_shift),
        up_weight,
        line(up_bias),
        down_weight,
        line(down_bias),
        line(second_gain),
        line(second_shift),
    )
    back_weights = (query_weight, key_weight, value_weight)
    row_index = [(first_row + row).reshape(1) for row in range(rows)]
    sums = Sums()
    number, slots = sums.me.reshape(1), sums.devices
    early_number = sums.me_near.reshape(1)
    heads, contexts = [], []
    remote[0] = after(remote[0], query_extra, key_extra, keep, number, early_number)
    for row in range(rows):
        if row:
            remote[row] = after(remote[row], contexts[-1])
        query, key, value, context = attend(
            row_index[row], tokens, remote[row], query_extra[row], key_extra[row], forward_weights
        )
        heads.append((query, key, value))
        contexts.append(context)
    remote_cotangent = after(remote_cotangent, contexts[-1])
    results = by_token(
        row_index[0],
        keep,
        number,
        tokens,
        remote,
        cotangent,
        remote_cotangent,
        contexts,
        token_weights,
        slots,
    )
    layer_outs = [results[row * ring : (row + 1) * ring] for row in range(rows)]
    results = results[rows * ring :]
    grad_heads, grad_first, late_near, late_far = results
    def give_back(parts, *before):
        return [
            part if turn == 0 else lax.ppermute(after(part, *before), "seq", back_turns[turn])
            for turn, part in enumerate(parts)
        ]

    def place(moved):
        by_turn = [jnp.concatenate(parts, 0) for parts in zip(*moved)]
        places = [
            [by_turn[(slot - index) % ring] for slot in range(ring)] for index in range(ring)
        ]
        whole = jnp.concatenate(places[0], 0)
        for index in range(1, ring):
            whole = jnp.where(me == index, jnp.concatenate(places[index], 0), whole)
        return whole

    parts = 2
    last = rows * parts - 1
    totals, biases = [None] * parts, [None] * parts
    tokens_grads = []
    here = early_number
    late = [late_near, sums.swap(late_far, 0, 1)]
    layer_outs = [give_back(parts_) for parts_ in layer_outs]
    for call in range(rows * parts):
        row, part = divmod(call, parts)
        if part == 0:
            grad_tokens = grad_first
        results = attend_back(
            (row, rows, part, parts),
            row_index[row],
            here,
            tokens,
            remote[row],
            (*heads[row], grad_heads),
            grad_tokens,
            back_weights,
            totals,
            biases,
            slots,
            1 if 1 < call < last else 200,
        )
        if part == parts - 1:
            tokens_grads.append(give_back(results[:ring]))
            results = results[ring:]
        else:
            grad_tokens, *results = results
        if call < last:
            totals[part], biases[part] = results
        if call == 0:
            late, layer_outs[0] = after((late, layer_outs[0]), results[0])
            late = sums.add_parts(after(late, layer_outs[0]), 1)
            here = after(early_number, *late)
            late = sums.meet(late, 1)
        if call == last - 1:
            late, layer_outs = after((late, layer_outs), results[0])
            late = sums.add_parts(after(late, layer_outs), 2)
            here = after(early_number, *late)
            late = sums.meet(late, 2)
    late, tokens_grads[:-1] = after((late, tokens_grads[:-1]), results[0])
    early_near, early_far = after(results, late, tokens_grads[:-1])
    early = sums.add_parts([early_near, sums.swap(early_far, 0, 1)], 1)
    late = add_up(late)
    late = [late, *sums.others(late, 2)]
    early, tokens_grads[-1] = after((sums.meet(early, 1), tokens_grads[-1]), late, tokens_grads[-1])
    early = add_up(early)
    late = jnp.concatenate(late, 0)
    late = after(late, early)
    late = [late, *sums.others(late, 1)]
    layer_out, tokens_grad = place(layer_outs), place(tokens_grads)
    early = add_up(after([early, *sums.others(early, 2)], late, layer_out, tokens_grad))
    late = after(late, early)
    late = [*late, *[sums.swap(array, 0, 1) for array in late]]
    early = [early, *sums.others(early, 1)]
    hidden_units = up_weight.shape[1]
    grad_up, grad_down, grad_out_weight, *late_lines = unpack(
        number,
        late,
        [(model, hidden_units), (hidden_units, model), (model, model)],
        model,
        [model] * 7 + [hidden_units],
    )
    early = after(early, late_lines)
    early = [*early, *[sums.swap(array, 0, 1) for array in early]]
    late_vectors = [line.reshape(-1) for line in late_lines]
    early = after(early, late_vectors)
    grad_query, grad_key, grad_value, query_bias_grad = unpack(
        early_number, early, [(model, model)] * 3, model, [model]
    )
    (
        grad_out_bias,
        grad_first_gain,
        grad_first_shift,
        grad_down_bias,
        grad_second_gain,
        grad_second_shift,
        grad_value_bias,
        grad_up_bias,
    ) = late_vectors
    return (
        layer_out,
        tokens_grad,
        grad_query,
        query_bias_grad.reshape(-1),
        grad_key,
        grad_value,
        grad_value_bias,
        grad_out_weight,
        grad_out_bias,
        grad_first_gain,
        grad_first_shift,
        grad_up,
        grad_up_bias,
        grad_down,
        grad_down_bias,
        grad_second_gain,
        grad_second_shift,
    )


def solution(mesh):
    dp, ring = mesh.shape["dp"], mesh.shape["seq"]

    def placed(function, mesh, rows):
        return jax.shard_map(
            function,
            mesh=mesh,
            in_specs=(
                P(rows, "seq", None),
                P(rows, None),
                P(rows),
                *([P()] * 15),
                P(rows, "seq", None),
            ),
            out_specs=(P(rows, "seq", None), P(rows, "seq", None), *([P()] * 15)),
            check_vma=False,
        )

    def layer(tokens, *others):
        row_count, model = tokens.shape[0] // dp, tokens.shape[2]
        powers = dp & (dp - 1) == 0 and ring & (ring - 1) == 0 and dp >= 4
        if not powers or row_count % ring or model % (16 * dp * ring):
            return placed(split_rows, mesh, "dp")(tokens, *others)
        axes = (FAR, MIDDLE, NEAR)
        finer = jax.sharding.Mesh(mesh.devices.reshape(dp // 4, 2, 2, ring), (*axes, SEQ))
        return placed(deal_rows, finer, axes)(tokens, *others)

    return layer
```

```python
import functools
import math

import jax
import jax.numpy as jnp
from jax import lax
from jax.experimental import pallas as pl
from jax.experimental.pallas import tpu as pltpu
from jax.sharding import PartitionSpec as P

HEADS = 8
EXTRA = 16
LANES = 128
LINE_ROWS = 2
NEG_FILL = -1e30
EPSILON = 1e-05
BLOCK_CAP = 512
LOG2E = 1.4426950408889634
LN2 = 0.6931471805599453
MIB = 1 << 20


def dot(left, right, left_dim, right_dim):
    return lax.dot_general(
        left, right, (((left_dim,), (right_dim,)), ((), ())), preferred_element_type=jnp.float32
    )


def three_parts(values):
    high = values.astype(jnp.bfloat16)
    rest = values - high.astype(jnp.float32)
    middle = rest.astype(jnp.bfloat16)
    low = (rest - middle.astype(jnp.float32)).astype(jnp.bfloat16)
    return high.astype(jnp.float32), middle.astype(jnp.float32), low.astype(jnp.float32)


def extra_rows(base, values, first):
    row = lax.broadcasted_iota(jnp.int32, base.shape, 0)
    for offset, part in enumerate(three_parts(values)):
        base = jnp.where(row == first + offset, part, base)
    return base


def upright(line):
    return jnp.broadcast_to(line, (8, line.shape[1])).T[:, :1]


def project(tokens, weights, query_column, value_column, width):
    shape = HEADS, width, tokens.shape[0]
    query = (dot(weights[0], tokens, 0, 1) + query_column) * (LOG2E * width**-0.5)
    yield query.astype(jnp.bfloat16).reshape(shape)
    yield dot(weights[1], tokens, 0, 1).astype(jnp.bfloat16).reshape(shape)
    yield (dot(weights[2], tokens, 0, 1) + value_column).astype(jnp.bfloat16).reshape(shape)


def prepare_kernel(rows, turns, width, firsts_ref, *refs):
    tokens_ref, cotangent_ref, *refs = refs
    weight_refs, refs = refs[:3], refs[3:]
    query_bias, value_bias, *refs = refs
    sends, refs = refs[: turns * (2 * rows - 1)], refs[turns * (2 * rows - 1) :]
    *projected, tokens_scratch, weights_scratch, sems = refs
    copies = [(ref, weights_scratch.at[i]) for i, ref in enumerate(weight_refs)]
    copies += [(tokens_ref.at[firsts_ref[0] + row], tokens_scratch.at[row]) for row in range(rows)]
    needed = len(copies)
    places = [(tokens_ref, row) for row in range(1, rows)]
    places += [(cotangent_ref, row) for row in range(rows)]
    for turn in range(turns):
        for index, (ref, row) in enumerate(places):
            source = ref.at[pl.ds(firsts_ref[1 + turn] + row, 1)]
            copies.append((source, sends[turn * len(places) + index]))
    copies = [
        pltpu.make_async_copy(source, target, sems.at[i])
        for i, (source, target) in enumerate(copies)
    ]
    for copy in copies:
        copy.start()
    for copy in copies[:needed]:
        copy.wait()
    weights = [weights_scratch[i] for i in range(3)]
    columns = upright(query_bias[...]), upright(value_bias[...])
    for row in range(rows):
        results = project(tokens_scratch[row], weights, *columns, width)
        for ref, result in zip(projected, results):
            ref[row] = result
    for copy in copies[needed:]:
        copy.wait()


def prepare(firsts, rows, tokens, cotangent, weights):
    turns = firsts.shape[0] - 1
    local, model = tokens.shape[1:]
    width = model // HEADS
    query_weight, query_bias, key_weight, value_weight, value_bias = weights
    anywhere = pl.BlockSpec(memory_space=pl.ANY)
    whole = lambda array: pl.BlockSpec(array.shape, lambda i, s: (0,) * array.ndim)
    low = lambda *shape: jax.ShapeDtypeStruct(shape, jnp.bfloat16)
    outs = [low(1, local, model)] * (turns * (2 * rows - 1))
    outs += [low(rows, HEADS, width, local)] * 3
    results = pl.pallas_call(
        functools.partial(prepare_kernel, rows, turns, width),
        out_shape=outs,
        grid_spec=pltpu.PrefetchScalarGridSpec(
            num_scalar_prefetch=1,
            grid=(1,),
            in_specs=[*[anywhere] * 5, whole(query_bias), whole(value_bias)],
            out_specs=[whole(a) for a in outs],
            scratch_shapes=[
                pltpu.VMEM((rows, local, model), jnp.bfloat16),
                pltpu.VMEM((3, model, model), jnp.bfloat16),
                pltpu.SemaphoreType.DMA((3 + rows + turns * (2 * rows - 1),)),
            ],
        ),
        compiler_params=pltpu.CompilerParams(vmem_limit_bytes=60 * MIB),
        cost_estimate=pl.CostEstimate(
            flops=2 * 10**10, bytes_accessed=1, transcendentals=0
        ),
        name="prepare",
    )(firsts, tokens, cotangent, query_weight, key_weight, value_weight, query_bias, value_bias)
    count = 2 * rows - 1
    return [results[turn * count : (turn + 1) * count] for turn in range(turns)], results[-3:]


def attend_kernel(row, pieces, width, block, *refs):
    token_refs, refs = refs[: pieces - 1], refs[pieces - 1 :]
    projected, refs = refs[:3], refs[3:]
    (
        query_extra,
        key_extra,
        query_weight,
        query_bias,
        key_weight,
        value_weight,
        value_bias,
        query_out,
        key_out,
        value_out,
        context_out,
        tokens_scratch,
        weights_scratch,
        query_scratch,
        key_scratch,
        value_scratch,
        context_scratch,
        scores_even,
        scores_odd,
        largest_even,
        largest_odd,
        in_sems,
        out_sems,
        query_sems,
        context_sems,
    ) = refs
    length = query_scratch.shape[2]
    local = length // pieces
    scratches = query_scratch, key_scratch, value_scratch
    incoming = [(ref.at[0], tokens_scratch.at[i]) for i, ref in enumerate(token_refs)]
    weight_refs = query_weight, key_weight, value_weight
    incoming += [(ref, weights_scratch.at[i]) for i, ref in enumerate(weight_refs)]
    incoming += [
        (ref.at[row], scratch.at[:, pl.ds(0, width), pl.ds(0, local)])
        for ref, scratch in zip(projected, scratches)
    ]
    incoming = [
        pltpu.make_async_copy(source, target, in_sems.at[i])
        for i, (source, target) in enumerate(incoming)
    ]
    for copy in incoming:
        copy.start()
    row = lax.broadcasted_iota(jnp.int32, (EXTRA, length), 0)
    ones = (row < 3).astype(jnp.bfloat16)
    query_base = query_extra[...]
    for head in range(HEADS):
        query_scratch[head, width:] = query_base.astype(jnp.bfloat16)
        key_scratch[head, width:] = key_extra[...].astype(jnp.bfloat16)
        value_scratch[head, width:] = ones
    columns = upright(query_bias[...]), upright(value_bias[...])
    for copy in incoming:
        copy.wait()
    weights = [weights_scratch[i] for i in range(3)]
    for piece in range(1, pieces):
        span = pl.ds(piece * local, local)
        results = project(tokens_scratch[piece - 1], weights, *columns, width)
        for scratch, result in zip(scratches, results):
            scratch[:, :width, span] = result
    outgoing = [
        pltpu.make_async_copy(key_scratch, key_out.at[0], out_sems.at[0]),
        pltpu.make_async_copy(value_scratch, value_out.at[0], out_sems.at[1]),
    ]
    for copy in outgoing:
        copy.start()

    def pair_copies(pair):
        heads = pl.ds(pair * 2, 2)
        rows = pl.ds(pl.multiple_of(pair * 2 * width, 2 * width), 2 * width)
        return (
            pltpu.make_async_copy(
                query_scratch.at[heads], query_out.at[0, heads], query_sems.at[pair]
            ),
            pltpu.make_async_copy(
                context_scratch.at[rows], context_out.at[rows], context_sems.at[pair]
            ),
        )

    def score(head, scores_ref, largest_ref, start):
        span = pl.ds(start, block)
        scores = dot(key_scratch[head], query_scratch[head, :, span], 0, 0)
        scores_ref[:, span] = scores
        largest_ref[:, span] = jnp.max(scores, 0, keepdims=True)

    def weigh(head, scores_ref, largest_ref, start):
        span = pl.ds(start, block)
        largest = largest_ref[:, span]
        weights = jnp.exp2(scores_ref[:, span] - largest).astype(jnp.bfloat16)
        update = dot(value_scratch[head], weights, 1, 0)
        total = update[width : width + 1]
        context_scratch[pl.ds(pl.multiple_of(head * width, width), width), span] = (
            update[:width] / total
        )
        log_total = largest + jnp.log(total) * LOG2E
        query_scratch[head, width:, span] = extra_rows(
            query_base[:, start : start + block], -log_total, 3
        ).astype(jnp.bfloat16)

    starts = range(0, length, block)
    for start in starts:
        score(0, scores_even, largest_even, start)

    def head_pair(pair, carry):
        head = pair * 2
        for start in starts:
            score(head + 1, scores_odd, largest_odd, start)
            weigh(head, scores_even, largest_even, start)
        following = jnp.minimum(head + 2, HEADS - 1)
        for start in starts:
            score(following, scores_even, largest_even, start)
            weigh(head + 1, scores_odd, largest_odd, start)
        for copy in pair_copies(pair):
            copy.start()
        return carry

    lax.fori_loop(0, HEADS // 2, head_pair, 0)
    for pair in range(HEADS // 2):
        outgoing.extend(pair_copies(pair))
    for copy in outgoing:
        copy.wait()


def attend(row, projected, remote, query_extra, key_extra, weights):
    pieces = 1 + len(remote)
    _, heads, width, local = projected[0].shape
    model = heads * width
    length = pieces * local
    whole = lambda array: pl.BlockSpec(array.shape, lambda i: (0,) * array.ndim)
    anywhere = pl.BlockSpec(memory_space=pl.ANY)
    low = jax.ShapeDtypeStruct((1, HEADS, width + EXTRA, length), jnp.bfloat16)
    outs = (low, low, low, jax.ShapeDtypeStruct((model, length), jnp.float32))
    query_weight, query_bias, key_weight, value_weight, value_bias = weights
    head_scratch = pltpu.VMEM(low.shape[1:], jnp.bfloat16)
    return pl.pallas_call(
        functools.partial(attend_kernel, row, pieces, width, min(256, length)),
        out_shape=outs,
        grid_spec=pltpu.PrefetchScalarGridSpec(
            num_scalar_prefetch=0,
            grid=(1,),
            in_specs=[
                *[anywhere] * (pieces + 2),
                whole(query_extra),
                whole(key_extra),
                anywhere,
                whole(query_bias),
                anywhere,
                anywhere,
                whole(value_bias),
            ],
            out_specs=[anywhere] * 4,
            scratch_shapes=[
                pltpu.VMEM((max(pieces - 1, 1), local, model), jnp.bfloat16),
                pltpu.VMEM((3, model, model), jnp.bfloat16),
                head_scratch,
                head_scratch,
                head_scratch,
                pltpu.VMEM((model, length), jnp.float32),
                pltpu.VMEM((length, length), jnp.float32),
                pltpu.VMEM((length, length), jnp.float32),
                pltpu.VMEM((1, length), jnp.float32),
                pltpu.VMEM((1, length), jnp.float32),
                pltpu.SemaphoreType.DMA((5 + pieces,)),
                pltpu.SemaphoreType.DMA((2,)),
                pltpu.SemaphoreType.DMA((HEADS // 2,)),
                pltpu.SemaphoreType.DMA((HEADS // 2,)),
            ],
        ),
        compiler_params=pltpu.CompilerParams(vmem_limit_bytes=60 * MIB),
        cost_estimate=pl.CostEstimate(
            flops=3 * 10**9, bytes_accessed=1, transcendentals=0
        ),
        name="attend",
    )(*remote, *projected, query_extra, key_extra, *weights)


def row_mean(values):
    return jnp.mean(values, -1, keepdims=True)


def normalise(values):
    centred = values - row_mean(values)
    scale = lax.rsqrt(row_mean(centred * centred) + EPSILON)
    return centred * scale, scale


def norm_back(grad, gain, normed, scale):
    entering = grad * gain
    return (entering - row_mean(entering) - normed * row_mean(entering * normed)) * scale


def column_sum(values):
    return jnp.sum(values, 0, keepdims=True)


def gelu_parts(values):
    phi = 0.5 + 0.5 * lax.erf(values * 0.5**0.5)
    bell = jnp.exp2(values * values * (-0.5 * LOG2E))
    return values * phi, phi + values * bell * 0.3989422804014327


def token_kernel(rows, pieces, steps, width, *refs):
    _, keep_ref, me_ref, refs = *refs[:3], refs[3:]
    own_tokens, own_cotangent, refs = *refs[:2], refs[2:]
    remote_count = rows * (pieces - 1)
    remote_tokens, refs = refs[:remote_count], refs[remote_count:]
    remote_cotangents, refs = refs[:remote_count], refs[remote_count:]
    context_refs, refs = refs[:rows], refs[rows:]
    (
        out_weight,
        out_bias,
        first_gain,
        first_shift,
        up_weight,
        up_bias,
        down_weight,
        down_bias,
        second_gain,
        second_shift,
    ) = refs[:10]
    refs = refs[10:]
    layer_outs, refs = refs[: rows * pieces], refs[rows * pieces :]
    (
        grad_out_heads,
        grad_first_out,
        near_out,
        far_out,
        up_scratch,
        down_scratch,
        result_scratch,
        packed_near,
        packed_far,
        sems,
        tokens_scratch,
        cotangent_scratch,
        context_scratch,
        act_scratch,
        slope_scratch,
        totals,
        lines,
        *line_sums,
    ) = refs
    (
        grad_out_bias,
        grad_first_gain,
        grad_first_shift,
        grad_down_bias,
        grad_second_gain,
        grad_second_shift,
        grad_value_bias,
        grad_up_bias,
    ) = line_sums
    row_index = pl.program_id(0)
    piece_index = pl.program_id(1)
    step_index = pl.program_id(2)
    tokens_len, model = tokens_scratch.shape
    hidden_units = up_weight.shape[1]
    kept = keep_ref[row_index] != 0
    span = pl.ds(pl.multiple_of(step_index * tokens_len, tokens_len), tokens_len)

    @pl.when(piece_index == 0)
    def _():
        tokens_scratch[...] = own_tokens[0, span]
        cotangent_scratch[...] = own_cotangent[0, span]

    first_step = (row_index == 0) & (piece_index == 0) & (step_index == 0)
    last_step = (row_index == rows - 1) & (piece_index == pieces - 1) & (step_index == steps - 1)
    fetches = [
        pltpu.make_async_copy(up_weight, up_scratch, sems.at[0]),
        pltpu.make_async_copy(down_weight, down_scratch, sems.at[1]),
    ]

    @pl.when(first_step)
    def _():
        for copy in fetches:
            copy.start()

    for row in range(rows):

        @pl.when(row_index == row)
        def _():
            context_scratch[...] = context_refs[row][...]

        for piece in range(1, pieces):

            @pl.when((row_index == row) & (piece_index == piece))
            def _():
                position = row * (pieces - 1) + piece - 1
                tokens_scratch[...] = remote_tokens[position][0, span]
                cotangent_scratch[...] = remote_cotangents[position][0, span]

    @pl.when(first_step)
    def _():
        for ref in (totals, lines, *line_sums):
            ref[...] = jnp.zeros(ref.shape, ref.dtype)

    tokens = tokens_scratch[...].astype(jnp.float32)
    context = context_scratch[...]
    context_low = context.astype(jnp.bfloat16)
    first_sum = tokens + (dot(context_low, out_weight[...], 0, 0) + out_bias[...])
    first_normed, first_scale = normalise(first_sum)
    hidden = first_normed * first_gain[...] + first_shift[...]
    hidden_low = hidden.astype(jnp.bfloat16)

    @pl.when(first_step)
    def _():
        for copy in fetches:
            copy.wait()

    pre_act = dot(hidden_low, up_scratch[...], 1, 0) + up_bias[...]
    activated, slope = gelu_parts(pre_act)
    act_low = activated.astype(jnp.bfloat16)
    act_scratch[...] = act_low
    slope_scratch[...] = slope
    branch = dot(act_low, down_scratch[...], 1, 0) + down_bias[...]
    second_normed, second_scale = normalise(hidden + branch)
    result = jnp.where(
        kept, second_normed * second_gain[...] + second_shift[...], tokens
    ).astype(jnp.bfloat16)
    gives = [
        pltpu.make_async_copy(result_scratch, ref.at[0, span], sems.at[2]) for ref in layer_outs
    ]

    @pl.when(jnp.logical_not(first_step))
    def _():
        gives[0].wait()

    result_scratch[...] = result
    for position, copy in enumerate(gives):

        @pl.when(row_index * pieces + piece_index == position)
        def _():
            copy.start()

    cotangent = cotangent_scratch[...].astype(jnp.float32)
    grad_out = jnp.where(kept, cotangent, 0.0)
    grad_second_gain[...] += column_sum(grad_out * second_normed)
    grad_second_shift[...] += column_sum(grad_out)
    grad_second = norm_back(grad_out, second_gain[...], second_normed, second_scale)
    grad_branch_low = grad_second.astype(jnp.bfloat16)
    grad_down_bias[...] += column_sum(grad_branch_low.astype(jnp.float32))
    grad_act = dot(grad_branch_low, down_scratch[...], 1, 1)
    grad_pre_low = (grad_act * slope_scratch[...]).astype(jnp.bfloat16)
    grad_hidden = grad_second + dot(grad_pre_low, up_scratch[...], 1, 1)
    totals[pl.ds(hidden_units, hidden_units), :] += dot(act_scratch[...], grad_branch_low, 0, 0)
    for start in range(0, hidden_units, model):
        totals[pl.ds(start, model), :] += dot(
            hidden_low, grad_pre_low[:, start : start + model], 0, 0
        )
    grad_up_bias[...] += column_sum(grad_pre_low.astype(jnp.float32))
    grad_first_gain[...] += column_sum(grad_hidden * first_normed)
    grad_first_shift[...] += column_sum(grad_hidden)
    grad_first = norm_back(grad_hidden, first_gain[...], first_normed, first_scale)
    grad_first_out[0] = jnp.where(kept, grad_first, cotangent)
    grad_attn_low = grad_first.astype(jnp.bfloat16)
    grad_out_bias[...] += column_sum(grad_attn_low.astype(jnp.float32))
    totals[pl.ds(2 * hidden_units, model), :] += dot(context_low, grad_attn_low, 1, 0)
    grad_context = dot(out_weight[...], grad_attn_low, 1, 1).astype(jnp.bfloat16)
    grad_context_wide = grad_context.astype(jnp.float32)
    ones = jnp.ones((EXTRA, tokens_len), jnp.bfloat16)
    grad_value_bias[...] += dot(ones, grad_context, 1, 1)[:1]
    product = grad_context_wide * context
    blank = jnp.zeros((EXTRA, tokens_len), jnp.float32)
    for head in range(HEADS):
        columns = slice(head * width, (head + 1) * width)
        grad_out_heads[0, head, :width] = grad_context[columns]
        spread = jnp.sum(product[columns], 0, keepdims=True)
        grad_out_heads[0, head, width:] = extra_rows(blank, -spread, 0).astype(jnp.bfloat16)

    @pl.when(last_step)
    def _():
        first = 0
        for ref in line_sums:
            set_lines(lines, first, ref[...])
            first += ref.shape[1] // LANES
        copies = [gives[0]]
        for half, out, sem in ((packed_far, far_out, 0), (packed_near, near_out, 1)):
            pack([totals], lines, *((None, half) if sem == 0 else (half, None)), me_ref[0])
            copies.append(pltpu.make_async_copy(half, out, sems.at[sem]))
            copies[-1].start()
        for copy in copies:
            copy.wait()


def set_lines(lines, first, values):
    width = lines.shape[2]
    for block in range(values.shape[1] // width):
        slot, row = divmod(first + block, LINE_ROWS)
        lines[slot, row : row + 1] = values[:, block * width : (block + 1) * width]


def pack(parts, lines, near, far, me):
    half, size, width = (near if far is None else far).shape
    columns = [(ref, start) for ref in parts for start in range(0, ref.shape[1], width)]
    height = parts[0].shape[0] // (2 * half)

    def one(slot, carry):
        for ref, first in ((near, 0), (far, half)):
            if ref is None:
                continue
            piece = (slot + first) ^ me
            rows = pl.ds(pl.multiple_of(piece * height, EXTRA), height)
            for block, (source, start) in enumerate(columns):
                ref[slot, pl.ds(block * height, height), :] = source[
                    rows, pl.ds(start, width)
                ].astype(jnp.bfloat16)
            ref[slot, pl.ds(len(columns) * height, EXTRA), :] = jnp.concatenate(
                [lines[piece], jnp.zeros_like(lines[piece])], 0
            ).astype(jnp.bfloat16)
        return carry

    lax.fori_loop(0, half, one, 0)


def packed_shape(slots, rows, model):
    return jax.ShapeDtypeStruct(
        (slots // 2, rows * (model // LANES) // slots + EXTRA, LANES), jnp.bfloat16
    )


def lines_shape(slots):
    return pltpu.VMEM((slots, EXTRA // 2, LANES), jnp.float32)


def by_token(
    row_index, keep, me, tokens, remote, cotangent, remote_cotangent, contexts, weights, slots
):
    rows = len(contexts)
    pieces = 1 + len(remote[0])
    local, model = tokens.shape[1:]
    length = pieces * local
    width = model // HEADS
    hidden_units = weights[4].shape[1]
    tokens_len = min(512, local)
    steps = local // tokens_len
    whole = lambda array: pl.BlockSpec(array.shape, lambda r, i, j, s, k, m: (0,) * array.ndim)
    own_spec = pl.BlockSpec((1, local, model), lambda r, i, j, s, k, m: (s[0] + r, 0, 0))
    f32 = lambda *shape: jax.ShapeDtypeStruct(shape, jnp.float32)
    anywhere = pl.BlockSpec(memory_space=pl.ANY)
    total_rows = 2 * hidden_units + model
    packed = packed_shape(slots, total_rows, model)
    piece_out = jax.ShapeDtypeStruct((1, local, model), jnp.bfloat16)
    gradient_outs = (packed, packed)
    line_lengths = [model] * 7 + [hidden_units]
    outs = (
        *([piece_out] * (rows * pieces)),
        jax.ShapeDtypeStruct((rows, HEADS, width + EXTRA, length), jnp.bfloat16),
        f32(rows, length, model),
        *gradient_outs,
    )
    out_specs = (
        *([anywhere] * (rows * pieces)),
        pl.BlockSpec(
            (1, HEADS, width + EXTRA, tokens_len),
            lambda r, i, j, s, k, m: (r, 0, 0, i * steps + j),
        ),
        pl.BlockSpec((1, tokens_len, model), lambda r, i, j, s, k, m: (r, i * steps + j, 0)),
        anywhere,
        anywhere,
    )

    def context_spec(row):
        def block(r, i, j, s, k, m):
            step = i * steps + j
            return 0, jnp.where(r < row, 0, jnp.where(r > row, pieces * steps - 1, step))

        return pl.BlockSpec((model, tokens_len), block)

    flat_remote = [array for arrays in remote for array in arrays]
    flat_remote_cotangent = [array for arrays in remote_cotangent for array in arrays]
    in_specs = (
        own_spec,
        own_spec,
        *[whole(a) for a in (*flat_remote, *flat_remote_cotangent)],
        *[context_spec(row) for row in range(rows)],
        *[anywhere if a.shape[0] * a.shape[1] > model * model else whole(a) for a in weights],
    )
    return pl.pallas_call(
        functools.partial(token_kernel, rows, pieces, steps, width),
        out_shape=outs,
        grid_spec=pltpu.PrefetchScalarGridSpec(
            num_scalar_prefetch=3,
            grid=(rows, pieces, steps),
            in_specs=in_specs,
            out_specs=out_specs,
            scratch_shapes=[
                pltpu.VMEM((model, hidden_units), jnp.bfloat16),
                pltpu.VMEM((hidden_units, model), jnp.bfloat16),
                pltpu.VMEM((tokens_len, model), jnp.bfloat16),
                pltpu.VMEM(packed.shape, jnp.bfloat16),
                pltpu.VMEM(packed.shape, jnp.bfloat16),
                pltpu.SemaphoreType.DMA((3,)),
                pltpu.VMEM((tokens_len, model), jnp.bfloat16),
                pltpu.VMEM((tokens_len, model), jnp.bfloat16),
                pltpu.VMEM((model, tokens_len), jnp.float32),
                pltpu.VMEM((tokens_len, hidden_units), jnp.bfloat16),
                pltpu.VMEM((tokens_len, hidden_units), jnp.float32),
                pltpu.VMEM((total_rows, model), jnp.float32),
                lines_shape(slots),
                *[pltpu.VMEM((1, n), jnp.float32) for n in line_lengths],
            ],
        ),
        compiler_params=pltpu.CompilerParams(vmem_limit_bytes=60 * MIB),
        cost_estimate=pl.CostEstimate(flops=1, bytes_accessed=1, transcendentals=0),
        name="by_token",
    )(
        row_index,
        keep,
        me,
        tokens,
        cotangent,
        *flat_remote,
        *flat_remote_cotangent,
        *contexts,
        *weights,
    )


def attend_back_kernel(pieces, width, block, place, *refs):
    row, rows, part, parts = place
    first_row, last_part = row == 0, part == parts - 1
    packing = row == rows - 1 and last_part
    row_ref, me_ref, refs = *refs[:2], refs[2:]
    token_refs, refs = refs[:pieces], refs[pieces:]
    head_refs, refs = refs[:4], refs[4:]
    grad_tokens_in, *weight_refs, refs = *refs[:4], refs[4:]
    if not first_row:
        totals_in, bias_in, refs = *refs[:2], refs[2:]
    earlier = part if packing else 0
    earlier_totals, refs = refs[:earlier], refs[earlier:]
    earlier_biases, refs = refs[:earlier], refs[earlier:]
    outs = pieces if last_part else 1
    grad_tokens, refs = refs[:outs], refs[outs:]
    if packing:
        packed_near, packed_far, *refs = refs
    else:
        totals_out, bias, *refs = refs
    (
        grad_query_scratch,
        grad_key_scratch,
        grad_value_scratch,
        tokens_scratch,
        grad_scratch,
        weights_scratch,
        totals,
        sems,
        *refs,
    ) = refs
    if packing:
        lines, bias, *earlier_scratch = refs
    query_ref, key_ref, value_ref, grad_ref = (ref.at[0] for ref in head_refs)
    pair = pl.program_id(0)
    pairs = pl.num_programs(0)
    length = query_ref.shape[2]
    local = length // pieces
    model, columns = weights_scratch.shape[1:]
    pair_width = 2 * width
    share = pl.ds(part * columns, columns)
    incoming = [(token_refs[0].at[row_ref[0]], tokens_scratch.at[0])]
    incoming += [(ref.at[0], tokens_scratch.at[i + 1]) for i, ref in enumerate(token_refs[1:])]
    incoming.append((grad_tokens_in.at[row if part == 0 else 0], grad_scratch))
    incoming += [(ref.at[:, share], weights_scratch.at[i]) for i, ref in enumerate(weight_refs)]
    if not first_row:
        incoming.append((totals_in, totals))
    if packing:
        incoming += list(zip(earlier_totals, earlier_scratch))
    incoming = [
        pltpu.make_async_copy(source, target, sems.at[i])
        for i, (source, target) in enumerate(incoming)
    ]

    @pl.when(pair == 0)
    def _():
        for copy in incoming:
            copy.start()

    grad_queries = [[], []]
    for side in range(2):
        key = key_ref[side]
        value = value_ref[side]
        grad_key = 0.0
        grad_value = 0.0
        for start in range(0, length, block):
            span = pl.ds(start, block)
            query = query_ref[side, :, span]
            grad = grad_ref[side, :, span]
            weights = jnp.exp2(dot(query, key, 0, 0))
            grad_weights = dot(grad, value, 0, 0)
            weights_low = weights.astype(jnp.bfloat16)
            grad_scores = (weights * grad_weights).astype(jnp.bfloat16)
            grad_value = grad_value + dot(grad[:width], weights_low, 1, 0)
            grad_key = grad_key + dot(query[:width], grad_scores, 1, 0)
            grad_queries[side].append(dot(grad_scores, key[:width], 1, 1))
        head = pl.ds(pl.multiple_of(pair * pair_width + side * width, width), width)
        grad_value_scratch[head, :] = grad_value.astype(jnp.bfloat16)
        grad_key_scratch[head, :] = (grad_key * LN2).astype(jnp.bfloat16)
    for index, start in enumerate(range(0, length, block)):
        both = jnp.concatenate([grad_queries[0][index], grad_queries[1][index]], 1)
        grad_query_scratch[pair, pl.ds(start, block)] = (both * width**-0.5).astype(jnp.bfloat16)

    @pl.when(pair == pairs - 1)
    def _():
        for copy in incoming:
            copy.wait()
        count = grad_query_scratch.shape[0]
        for index in range(count):
            lanes = pl.ds(index * pair_width, pair_width)
            total = column_sum(grad_query_scratch[index].astype(jnp.float32))
            bias[:, lanes] = total if first_row else bias_in[:, lanes] + total
        grad_query = jnp.concatenate([grad_query_scratch[index] for index in range(count)], 1)
        outgoing = []
        for position in range(3):
            lines_of = pl.ds(position * model, model)
            term = 0.0
            for piece in range(pieces):
                span = slice(piece * local, (piece + 1) * local)
                tokens = tokens_scratch[piece]
                if position == 0:
                    term = term + dot(tokens, grad_query[span], 0, 0)
                else:
                    source = grad_key_scratch if position == 1 else grad_value_scratch
                    term = term + dot(tokens, source[:, span], 0, 1)
            totals[lines_of, :] = term if first_row else totals[lines_of, :] + term
        if not packing:
            outgoing.append(pltpu.make_async_copy(totals, totals_out, sems.at[0]))
            outgoing[0].start()
        for piece in range(pieces):
            span = pl.ds(piece * local, local)
            total = (
                grad_scratch[span]
                + dot(grad_query[piece * local : (piece + 1) * local], weights_scratch[0], 1, 1)
                + dot(grad_key_scratch[:, span], weights_scratch[1], 0, 1)
                + dot(grad_value_scratch[:, span], weights_scratch[2], 0, 1)
            )
            if last_part:
                grad_tokens[piece][0] = total.astype(jnp.bfloat16)
            else:
                grad_scratch[span] = total
                outgoing.append(
                    pltpu.make_async_copy(
                        grad_scratch.at[span], grad_tokens[0].at[0, span], sems.at[1 + piece]
                    )
                )
                outgoing[-1].start()
        if packing:
            lines[...] = jnp.zeros(lines.shape, lines.dtype)
            first = 0
            for ref in (*earlier_biases, bias):
                set_lines(lines, first, ref[...])
                first += ref.shape[1] // LANES
            pack([*earlier_scratch, totals], lines, packed_near, packed_far, me_ref[0])
        for copy in outgoing:
            copy.wait()


def attend_back(
    place, row_index, me, tokens, remote, heads, grad_tokens, weights, totals, biases, slots, gflops
):
    row, rows, part, parts = place
    last_part = part == parts - 1
    packing = row == rows - 1 and last_part
    pieces = 1 + len(remote)
    local, model = tokens.shape[1:]
    length = pieces * local
    width = model // HEADS
    columns = model // parts
    pairs = HEADS // parts // 2
    anywhere = pl.BlockSpec(memory_space=pl.ANY)
    whole = lambda array: pl.BlockSpec(array.shape, lambda i, s, m: (0,) * array.ndim)
    head_spec = lambda array: pl.BlockSpec(
        (1, 2, *array.shape[2:]),
        lambda i, s, m: (row if array.shape[0] > 1 else 0, part * pairs + i, 0, 0),
    )
    f32 = lambda *shape: jax.ShapeDtypeStruct(shape, jnp.float32)
    if last_part:
        outs = [jax.ShapeDtypeStruct((1, local, model), jnp.bfloat16)] * pieces
        out_specs = [whole(a) for a in outs]
    else:
        outs, out_specs = [f32(1, length, model)], [anywhere]
    total, bias = f32(3 * model, columns), f32(1, columns)
    in_specs = [anywhere] * pieces + [head_spec(a) for a in heads] + [anywhere] * 4
    operands = [tokens, *remote, *heads, grad_tokens, *weights]
    if row:
        operands += [totals[part], biases[part]]
        in_specs += [anywhere, whole(bias)]
    scratch = [
        pltpu.VMEM((pairs, length, 2 * width), jnp.bfloat16),
        pltpu.VMEM((columns, length), jnp.bfloat16),
        pltpu.VMEM((columns, length), jnp.bfloat16),
        pltpu.VMEM((pieces, local, model), jnp.bfloat16),
        pltpu.VMEM((length, model), jnp.float32),
        pltpu.VMEM((3, model, columns), jnp.bfloat16),
        pltpu.VMEM(total.shape, jnp.float32),
        pltpu.SemaphoreType.DMA((pieces + 5 + parts,)),
    ]
    if packing:
        operands += [*totals[:part], *biases[:part]]
        in_specs += [anywhere] * part + [whole(bias)] * part
        packed = packed_shape(slots, 3 * model, model)
        outs += [packed] * 2
        out_specs += [whole(packed)] * 2
        scratch += [lines_shape(slots), pltpu.VMEM(bias.shape, jnp.float32)]
        scratch += [pltpu.VMEM(total.shape, jnp.float32)] * part
    else:
        outs += [total, bias]
        out_specs += [anywhere, whole(bias)]
    return pl.pallas_call(
        functools.partial(attend_back_kernel, pieces, width, min(256, length), place),
        out_shape=outs,
        grid_spec=pltpu.PrefetchScalarGridSpec(
            num_scalar_prefetch=2,
            grid=(pairs,),
            in_specs=in_specs,
            out_specs=out_specs,
            scratch_shapes=scratch,
        ),
        compiler_params=pltpu.CompilerParams(vmem_limit_bytes=60 * MIB),
        cost_estimate=pl.CostEstimate(
            flops=gflops * 10**9, bytes_accessed=1, transcendentals=0
        ),
        name="attend_back",
    )(row_index, me, *operands)


def unpack_kernel(moves, model, counts, me_ref, *refs):
    sources, refs = refs[: counts[0]], refs[counts[0] :]
    outs, refs = refs[: counts[1]], refs[counts[1] :]
    lines, refs = refs[: counts[2]], refs[counts[2] :]
    *blocks_out, slots, in_sems, out_sems = refs
    count = counts[0]
    _, size, width = slots.shape
    me = me_ref[0]
    share = slots.shape[0] // count
    copies = [
        pltpu.make_async_copy(source, slots.at[pl.ds(index * share, share)], in_sems.at[index])
        for index, source in enumerate(sources)
    ]
    for copy in copies:
        copy.start()
    for copy in copies:
        copy.wait()
    index = 0
    for line in lines:
        for block in range(line.shape[1] // width):
            piece, row = divmod(index, LINE_ROWS)
            extra = slots[piece ^ me, pl.ds(size - EXTRA, EXTRA), :].astype(jnp.float32)
            line[:, pl.ds(block * width, width)] = extra[row : row + 1]
            index += 1
    copies = []
    for square, (out, row, column, pieces) in enumerate(moves):
        for piece, start, rows, inside, offset in pieces:
            blocks_out[out][pl.ds(row + inside, rows), pl.ds(column + offset, width)] = slots[
                piece ^ me, pl.ds(start, rows), :
            ].astype(jnp.float32)
        part = pl.ds(row, model), pl.ds(column, model)
        copies.append(
            pltpu.make_async_copy(
                blocks_out[out].at[part], outs[out].at[part], out_sems.at[square]
            )
        )
        copies[-1].start()
    for copy in copies:
        copy.wait()


def unpack(me, arrays, shapes, model, lengths):
    share, size, width = arrays[0].shape
    slots = share * len(arrays)
    blocks = model // width
    height = (size - EXTRA) // blocks
    moves = [
        (out, row, column, [])
        for out, shape in enumerate(shapes)
        for row in range(0, shape[0], model)
        for column in range(0, shape[1], model)
    ]
    for piece in range(slots):
        done = 0
        while done < height:
            square, inside = divmod(piece * height + done, model)
            rows = min(height - done, model - inside)
            for block in range(blocks):
                moves[square][3].append(
                    (piece, block * height + done, rows, inside, block * width)
                )
            done += rows
    outs = [jax.ShapeDtypeStruct(shape, jnp.float32) for shape in shapes]
    lines = [jax.ShapeDtypeStruct((1, n), jnp.float32) for n in lengths]
    anywhere = pl.BlockSpec(memory_space=pl.ANY)
    return pl.pallas_call(
        functools.partial(unpack_kernel, moves, model, (len(arrays), len(outs), len(lines))),
        out_shape=[*outs, *lines],
        grid_spec=pltpu.PrefetchScalarGridSpec(
            num_scalar_prefetch=1,
            grid=(1,),
            in_specs=[anywhere] * len(arrays),
            out_specs=[
                *[anywhere] * len(outs),
                *[pl.BlockSpec(a.shape, lambda i, m: (0, 0)) for a in lines],
            ],
            scratch_shapes=[
                *[pltpu.VMEM(a.shape, jnp.float32) for a in outs],
                pltpu.VMEM((slots, size, width), jnp.bfloat16),
                pltpu.SemaphoreType.DMA((len(arrays),)),
                pltpu.SemaphoreType.DMA((len(moves),)),
            ],
        ),
        compiler_params=pltpu.CompilerParams(vmem_limit_bytes=60 * MIB),
        cost_estimate=pl.CostEstimate(
            flops=2 * 10**10, bytes_accessed=1, transcendentals=0
        ),
        name="unpack",
    )(me, *arrays)


NEAR, MIDDLE, FAR, SEQ = AXES = ("near", "middle", "far", "seq")
STAGES = ((NEAR,), (MIDDLE, SEQ), (FAR,))


def add_up(arrays):
    arrays = [a.astype(jnp.float32) for a in arrays]
    while len(arrays) > 1:
        arrays = [first + second for first, second in zip(arrays[::2], arrays[1::2], strict=True)]
    return arrays[0].astype(jnp.bfloat16)


def after(arrays, *others):
    return lax.optimization_barrier((arrays, others))[0]


class Sums:
    def __init__(self):
        self.sizes = [lax.axis_size(axes) for axes in STAGES]
        self.devices = math.prod(self.sizes)
        digits = [lax.axis_index(axes) for axes in STAGES]
        self.me = (digits[0] * self.sizes[1] + digits[1]) * self.sizes[2] + digits[2]
        self.me_near = self.me - digits[2]

    def swap(self, array, stage, turn):
        pairs = [(i, i ^ turn) for i in range(self.sizes[stage])]
        return lax.ppermute(array, STAGES[stage], pairs)

    def meet(self, parts, stage):
        return [parts[0], *[self.swap(parts[t], stage, t) for t in range(1, len(parts))]]

    def add_parts(self, arrays, stage):
        size = self.sizes[stage]
        share = arrays[0].shape[0] // size
        return [
            add_up([array[turn * share : (turn + 1) * share] for array in arrays])
            for turn in range(size)
        ]

    def others(self, held, stage):
        return [self.swap(held, stage, turn) for turn in range(1, self.sizes[stage])]


def norm_rows(values, gain, shift):
    row_mean = jnp.mean(values, -1, keepdims=True)
    centred = values - row_mean
    variance = jnp.mean(centred * centred, -1, keepdims=True)
    return centred * lax.rsqrt(variance + EPSILON) * gain + shift


def gelu_exact(values):
    return jax.nn.gelu(values, approximate=False)


def plain_dot(left, right):
    return jnp.dot(left, right, preferred_element_type=jnp.float32)


def left_dot(left, right):
    return lax.dot_general(
        left, right, (((0,), (0,)), ((), ())), preferred_element_type=jnp.float32
    )


def right_dot(left, right):
    return lax.dot_general(
        left, right, (((1,), (1,)), ((), ())), preferred_element_type=jnp.float32
    )


def token_sum(values):
    return jnp.sum(values.astype(jnp.float32), 0)


def split_heads(values, piece_len):
    return values.reshape(values.shape[0], piece_len, HEADS, values.shape[2] // HEADS)


def block_length(piece_len, local_len):
    return math.gcd(math.gcd(piece_len, local_len), BLOCK_CAP)


def masked_scores(query_heads, key_heads, query_ids, key_ids, score_scale):
    scores = (
        jnp.einsum("rqhd,rkhd->rhqk", query_heads, key_heads, preferred_element_type=jnp.float32)
        * score_scale
    )
    same_doc = query_ids[:, None, :, None] == key_ids[:, None, None, :]
    return jnp.where(same_doc, scores, NEG_FILL)


def split_attend_back(
    query_heads,
    grad_heads,
    log_total,
    spread,
    query_ids,
    key_heads,
    value_heads,
    key_ids,
    score_scale,
):
    scores = masked_scores(query_heads, key_heads, query_ids, key_ids, score_scale)
    weights = jnp.exp(scores - jnp.transpose(log_total, (0, 2, 1))[..., None])
    grad_value = jnp.einsum(
        "rhqk,rqhd->rkhd",
        weights.astype(jnp.bfloat16),
        grad_heads,
        preferred_element_type=jnp.float32,
    )
    grad_weights = jnp.einsum(
        "rqhd,rkhd->rhqk", grad_heads, value_heads, preferred_element_type=jnp.float32
    )
    grad_scores = (weights * (grad_weights - jnp.transpose(spread, (0, 2, 1))[..., None])).astype(
        jnp.bfloat16
    )
    grad_query = (
        jnp.einsum("rhqk,rkhd->rqhd", grad_scores, key_heads, preferred_element_type=jnp.float32)
        * score_scale
    )
    grad_key = (
        jnp.einsum("rhqk,rqhd->rkhd", grad_scores, query_heads, preferred_element_type=jnp.float32)
        * score_scale
    )
    return (grad_query, grad_key, grad_value)


def add_into(buffer, term, block_start):
    current = lax.dynamic_slice_in_dim(buffer, block_start, term.shape[1], 1)
    return lax.dynamic_update_slice_in_dim(buffer, current + term, block_start, 1)


def split_rows(
    tokens,
    segments,
    keep_flags,
    query_weight,
    query_bias,
    key_weight,
    value_weight,
    value_bias,
    out_weight,
    out_bias,
    first_gain,
    first_shift,
    up_weight,
    up_bias,
    down_weight,
    down_bias,
    second_gain,
    second_shift,
    cotangent,
):
    row_count, local_tokens, model_width = tokens.shape
    head_width = model_width // HEADS
    score_scale = head_width ** (-0.5)
    flat_tokens = tokens.reshape(row_count * local_tokens, model_width)
    row_shape = (row_count, local_tokens, model_width)
    query_low = (
        (plain_dot(flat_tokens, query_weight) + query_bias).astype(jnp.bfloat16).reshape(row_shape)
    )
    key_low = plain_dot(flat_tokens, key_weight).astype(jnp.bfloat16).reshape(row_shape)
    value_low = (
        (plain_dot(flat_tokens, value_weight) + value_bias).astype(jnp.bfloat16).reshape(row_shape)
    )
    query_heads = split_heads(query_low, local_tokens)
    own_start = lax.axis_index("seq") * local_tokens
    own_ids = lax.dynamic_slice_in_dim(segments, own_start, local_tokens, 1)
    initial = (
        jnp.full((row_count, HEADS, local_tokens), NEG_FILL, jnp.float32),
        jnp.zeros((row_count, HEADS, local_tokens), jnp.float32),
        jnp.zeros((row_count, HEADS, local_tokens, head_width), jnp.float32),
    )
    key_piece = lax.all_gather(key_low, "seq", axis=1, tiled=True)
    value_piece = lax.all_gather(value_low, "seq", axis=1, tiled=True)
    block_size = block_length(key_piece.shape[1], local_tokens)

    def key_step(position, inner_state):
        running_max, running_sum, running_acc = inner_state
        block_start = position * block_size
        key_heads = split_heads(
            lax.dynamic_slice_in_dim(key_piece, block_start, block_size, 1), block_size
        )
        value_heads = split_heads(
            lax.dynamic_slice_in_dim(value_piece, block_start, block_size, 1), block_size
        )
        key_ids = lax.dynamic_slice_in_dim(segments, block_start, block_size, 1)
        scores = masked_scores(query_heads, key_heads, own_ids, key_ids, score_scale)
        newest = jnp.maximum(running_max, jnp.max(scores, -1))
        factor = jnp.exp(running_max - newest)
        weights = jnp.exp(scores - newest[..., None])
        running_sum = running_sum * factor + jnp.sum(weights, -1)
        update = jnp.einsum(
            "rhqk,rkhd->rhqd",
            weights.astype(jnp.bfloat16),
            value_heads,
            preferred_element_type=jnp.float32,
        )
        return (newest, running_sum, running_acc * factor[..., None] + update)

    running_max, running_sum, running_acc = lax.fori_loop(
        0, key_piece.shape[1] // block_size, key_step, initial
    )
    context_heads = jnp.transpose(running_acc / running_sum[..., None], (0, 2, 1, 3))
    log_total = jnp.transpose(running_max + jnp.log(running_sum), (0, 2, 1))
    context_low = context_heads.reshape(row_count * local_tokens, model_width).astype(jnp.bfloat16)
    first_sum = flat_tokens.astype(jnp.float32) + (plain_dot(context_low, out_weight) + out_bias)
    hidden, first_back = jax.vjp(norm_rows, first_sum, first_gain, first_shift)
    hidden_low = hidden.astype(jnp.bfloat16)
    pre_act = plain_dot(hidden_low, up_weight) + up_bias
    activated, act_back = jax.vjp(gelu_exact, pre_act)
    act_low = activated.astype(jnp.bfloat16)
    second_sum = hidden + (plain_dot(act_low, down_weight) + down_bias)
    normed, second_back = jax.vjp(norm_rows, second_sum, second_gain, second_shift)
    kept_rows = (keep_flags != 0)[:, None, None]
    layer_out = jnp.where(kept_rows, normed.reshape(row_shape), tokens.astype(jnp.float32)).astype(
        jnp.bfloat16
    )
    grad_out = jnp.where(kept_rows, cotangent.astype(jnp.float32), 0.0).reshape(
        row_count * local_tokens, model_width
    )
    grad_second, grad_second_gain, grad_second_shift = second_back(grad_out)
    grad_branch_low = grad_second.astype(jnp.bfloat16)
    grad_down_bias = token_sum(grad_branch_low)
    grad_down_weight = left_dot(act_low, grad_branch_low)
    (grad_pre,) = act_back(right_dot(grad_branch_low, down_weight))
    grad_pre_low = grad_pre.astype(jnp.bfloat16)
    grad_up_bias = token_sum(grad_pre_low)
    grad_up_weight = left_dot(hidden_low, grad_pre_low)
    grad_hidden = grad_second + right_dot(grad_pre_low, up_weight)
    grad_first, grad_first_gain, grad_first_shift = first_back(grad_hidden)
    grad_attn_low = grad_first.astype(jnp.bfloat16)
    grad_out_bias = token_sum(grad_attn_low)
    grad_out_weight = left_dot(context_low, grad_attn_low)
    late_grads = (
        grad_out_weight,
        grad_out_bias,
        grad_first_gain,
        grad_first_shift,
        grad_up_weight,
        grad_up_bias,
        grad_down_weight,
        grad_down_bias,
        grad_second_gain,
        grad_second_shift,
    )
    grad_context_low = right_dot(grad_attn_low, out_weight).astype(jnp.bfloat16)
    grad_context_rows = grad_context_low.reshape(row_shape)
    grad_heads = split_heads(grad_context_rows, local_tokens)
    spread = jnp.sum(grad_heads.astype(jnp.float32) * context_heads, -1)
    zero_local = jnp.zeros((row_count, local_tokens, HEADS, head_width), jnp.float32)
    zero_whole = jnp.zeros(
        (row_count, local_tokens * lax.axis_size("seq"), HEADS, head_width), jnp.float32
    )
    gathered_total, gathered_spread = (
        lax.all_gather(log_total, "seq", axis=1, tiled=True),
        lax.all_gather(spread, "seq", axis=1, tiled=True),
    )
    key_heads_local = split_heads(key_low, local_tokens)
    value_heads_local = split_heads(value_low, local_tokens)
    query_piece = lax.all_gather(query_low, "seq", axis=1, tiled=True)
    grad_piece = lax.all_gather(grad_context_rows, "seq", axis=1, tiled=True)
    back_block_size = block_length(query_piece.shape[1], local_tokens)

    def query_step(position, inner_state):
        grad_key, grad_value, queries_whole = inner_state
        block_start = position * back_block_size
        part_query, part_key, part_value = split_attend_back(
            split_heads(
                lax.dynamic_slice_in_dim(query_piece, block_start, back_block_size, 1),
                back_block_size,
            ),
            split_heads(
                lax.dynamic_slice_in_dim(grad_piece, block_start, back_block_size, 1),
                back_block_size,
            ),
            lax.dynamic_slice_in_dim(gathered_total, block_start, back_block_size, 1),
            lax.dynamic_slice_in_dim(gathered_spread, block_start, back_block_size, 1),
            lax.dynamic_slice_in_dim(segments, block_start, back_block_size, 1),
            key_heads_local,
            value_heads_local,
            own_ids,
            score_scale,
        )
        return (
            grad_key + part_key,
            grad_value + part_value,
            add_into(queries_whole, part_query, block_start),
        )

    grad_key, grad_value, queries_whole = lax.fori_loop(
        0, query_piece.shape[1] // back_block_size, query_step, (zero_local, zero_local, zero_whole)
    )
    grad_query = lax.psum_scatter(queries_whole, "seq", scatter_dimension=1, tiled=True)
    flat_shape = (row_count * local_tokens, model_width)
    grad_query_low = grad_query.reshape(flat_shape).astype(jnp.bfloat16)
    grad_key_low = grad_key.reshape(flat_shape).astype(jnp.bfloat16)
    grad_value_low = grad_value.reshape(flat_shape).astype(jnp.bfloat16)
    grad_query_bias = token_sum(grad_query_low)
    grad_query_weight = left_dot(flat_tokens, grad_query_low)
    grad_key_weight = left_dot(flat_tokens, grad_key_low)
    grad_value_bias = token_sum(grad_value_low)
    grad_value_weight = left_dot(flat_tokens, grad_value_low)
    grad_flat = (
        grad_first
        + right_dot(grad_query_low, query_weight)
        + right_dot(grad_key_low, key_weight)
        + right_dot(grad_value_low, value_weight)
    )
    tokens_grad = jnp.where(
        kept_rows, grad_flat.reshape(row_shape), cotangent.astype(jnp.float32)
    ).astype(jnp.bfloat16)
    early_grads = (
        grad_query_weight,
        grad_query_bias,
        grad_key_weight,
        grad_value_weight,
        grad_value_bias,
    )
    summed = lax.psum(
        (
            grad_query_weight,
            grad_query_bias,
            grad_key_weight,
            grad_value_weight,
            grad_value_bias,
            grad_out_weight,
            grad_out_bias,
            grad_first_gain,
            grad_first_shift,
            grad_up_weight,
            grad_up_bias,
            grad_down_weight,
            grad_down_bias,
            grad_second_gain,
            grad_second_shift,
        ),
        ("dp", "seq"),
    )
    early_grads = summed[:5]
    late_grads = summed[5:]
    return (
        layer_out,
        tokens_grad,
        early_grads[0],
        early_grads[1],
        early_grads[2],
        early_grads[3],
        early_grads[4],
        late_grads[0],
        late_grads[1],
        late_grads[2],
        late_grads[3],
        late_grads[4],
        late_grads[5],
        late_grads[6],
        late_grads[7],
        late_grads[8],
        late_grads[9],
    )


def deal_rows(
    tokens,
    segments,
    keep_flags,
    query_weight,
    query_bias,
    key_weight,
    value_weight,
    value_bias,
    out_weight,
    out_bias,
    first_gain,
    first_shift,
    up_weight,
    up_bias,
    down_weight,
    down_bias,
    second_gain,
    second_shift,
    cotangent,
):
    row_count, local_tokens, model = tokens.shape
    ring = lax.axis_size("seq")
    me = lax.axis_index("seq")
    rows = row_count // ring
    first_row = me * rows
    turns = [[(i, (i + turn) % ring) for i in range(ring)] for turn in range(ring)]
    back_turns = [[(i, (i - turn) % ring) for i in range(ring)] for turn in range(ring)]

    line = lambda vector: vector.reshape(1, -1)
    forward_weights = (
        query_weight,
        line(query_bias),
        key_weight,
        value_weight,
        line(value_bias),
    )
    firsts = jnp.stack([lax.rem(me + turn, ring) * rows for turn in range(ring)])
    sends, projected = prepare(firsts, rows, tokens, cotangent, forward_weights)

    def fetch(part, turn):
        return lax.ppermute(part, "seq", turns[turn])

    first = [
        fetch(lax.dynamic_slice_in_dim(tokens, firsts[turn], 1, 0), turn)
        for turn in range(1, ring)
    ]
    first, sends, projected = after((first, sends, projected))
    remote, remote_cotangent, before = [first], [], first
    for row in range(rows):
        for index, fetched in ((row, remote), (rows + row, remote_cotangent)):
            if index:
                parts = [after(sends[turn][index - 1], before) for turn in range(ring - 1)]
                fetched.append([fetch(part, turn + 1) for turn, part in enumerate(parts)])
        before = remote[row]
    own_segments = lax.dynamic_slice_in_dim(segments, first_row, rows, 0)
    own_segments = jnp.concatenate(
        [
            lax.dynamic_slice_in_dim(
                own_segments, lax.rem(me - turn + ring, ring) * local_tokens, local_tokens, 1
            )
            for turn in range(ring)
        ],
        1,
    )
    extra_index = jnp.arange(EXTRA, dtype=jnp.int32)[None, :, None]
    same = own_segments[:, None, :] == extra_index
    query_extra = jnp.where(same & (extra_index < 3), 1.0, 0.0)
    key_extra = jnp.where(
        extra_index < 3, jnp.where(same, 0.0, NEG_FILL), jnp.where(extra_index < 6, 1.0, 0.0)
    )
    keep = lax.dynamic_slice_in_dim(keep_flags, first_row, rows, 0)
    token_weights = (
        out_weight,
        line(out_bias),
        line(first_gain),
        line(first_shift),
        up_weight,
        line(up_bias),
        down_weight,
        line(down_bias),
        line(second_gain),
        line(second_shift),
    )
    back_weights = (query_weight, key_weight, value_weight)
    row_index = [(first_row + row).reshape(1) for row in range(rows)]
    sums = Sums()
    number, slots = sums.me.reshape(1), sums.devices
    early_number = sums.me_near.reshape(1)
    heads, contexts = [], []
    remote[0] = after(remote[0], query_extra, key_extra, keep, number, early_number)
    for row in range(rows):
        if row:
            remote[row] = after(remote[row], contexts[-1])
        query, key, value, context = attend(
            row, projected, remote[row], query_extra[row], key_extra[row], forward_weights
        )
        heads.append((query, key, value))
        contexts.append(context)
    remote_cotangent = after(remote_cotangent, contexts[-1])
    results = by_token(
        row_index[0],
        keep,
        number,
        tokens,
        remote,
        cotangent,
        remote_cotangent,
        contexts,
        token_weights,
        slots,
    )
    layer_outs = [results[row * ring : (row + 1) * ring] for row in range(rows)]
    results = results[rows * ring :]
    grad_heads, grad_first, late_near, late_far = results
    def give_back(parts, *before):
        return [
            part if turn == 0 else lax.ppermute(after(part, *before), "seq", back_turns[turn])
            for turn, part in enumerate(parts)
        ]

    def place(moved):
        by_turn = [jnp.concatenate(parts, 0) for parts in zip(*moved)]
        places = [
            [by_turn[(slot - index) % ring] for slot in range(ring)] for index in range(ring)
        ]
        whole = jnp.concatenate(places[0], 0)
        for index in range(1, ring):
            whole = jnp.where(me == index, jnp.concatenate(places[index], 0), whole)
        return whole

    parts = 2
    last = rows * parts - 1
    totals, biases = [None] * parts, [None] * parts
    tokens_grads = []
    here = early_number
    late = [late_near, sums.swap(late_far, 0, 1)]
    layer_outs = [give_back(parts_) for parts_ in layer_outs]
    for call in range(rows * parts):
        row, part = divmod(call, parts)
        if part == 0:
            grad_tokens = grad_first
        results = attend_back(
            (row, rows, part, parts),
            row_index[row],
            here,
            tokens,
            remote[row],
            (*heads[row], grad_heads),
            grad_tokens,
            back_weights,
            totals,
            biases,
            slots,
            1 if 1 < call < last else 200,
        )
        if part == parts - 1:
            tokens_grads.append(give_back(results[:ring]))
            results = results[ring:]
        else:
            grad_tokens, *results = results
        if call < last:
            totals[part], biases[part] = results
        if call == 0:
            late, layer_outs[0] = after((late, layer_outs[0]), results[0])
            late = sums.add_parts(after(late, layer_outs[0]), 1)
            here = after(early_number, *late)
            late = sums.meet(late, 1)
        if call == last - 1:
            late, layer_outs = after((late, layer_outs), results[0])
            late = sums.add_parts(after(late, layer_outs), 2)
            here = after(early_number, *late)
            late = sums.meet(late, 2)
    late, tokens_grads[:-1] = after((late, tokens_grads[:-1]), results[0])
    early_near, early_far = after(results, late, tokens_grads[:-1])
    early = sums.add_parts([early_near, sums.swap(early_far, 0, 1)], 1)
    late = add_up(late)
    late = [late, *sums.others(late, 2)]
    early, tokens_grads[-1] = after((sums.meet(early, 1), tokens_grads[-1]), late, tokens_grads[-1])
    early = add_up(early)
    late = jnp.concatenate(late, 0)
    late = after(late, early)
    late = [late, *sums.others(late, 1)]
    layer_out, tokens_grad = place(layer_outs), place(tokens_grads)
    early = add_up(after([early, *sums.others(early, 2)], late, layer_out, tokens_grad))
    late = after(late, early)
    late = [*late, *[sums.swap(array, 0, 1) for array in late]]
    early = [early, *sums.others(early, 1)]
    hidden_units = up_weight.shape[1]
    grad_up, grad_down, grad_out_weight, *late_lines = unpack(
        number,
        late,
        [(model, hidden_units), (hidden_units, model), (model, model)],
        model,
        [model] * 7 + [hidden_units],
    )
    early = after(early, late_lines)
    early = [*early, *[sums.swap(array, 0, 1) for array in early]]
    late_vectors = [line.reshape(-1) for line in late_lines]
    early = after(early, late_vectors)
    grad_query, grad_key, grad_value, query_bias_grad = unpack(
        early_number, early, [(model, model)] * 3, model, [model]
    )
    (
        grad_out_bias,
        grad_first_gain,
        grad_first_shift,
        grad_down_bias,
        grad_second_gain,
        grad_second_shift,
        grad_value_bias,
        grad_up_bias,
    ) = late_vectors
    return (
        layer_out,
        tokens_grad,
        grad_query,
        query_bias_grad.reshape(-1),
        grad_key,
        grad_value,
        grad_value_bias,
        grad_out_weight,
        grad_out_bias,
        grad_first_gain,
        grad_first_shift,
        grad_up,
        grad_up_bias,
        grad_down,
        grad_down_bias,
        grad_second_gain,
        grad_second_shift,
    )


def solution(mesh):
    dp, ring = mesh.shape["dp"], mesh.shape["seq"]

    def placed(function, mesh, rows):
        return jax.shard_map(
            function,
            mesh=mesh,
            in_specs=(
                P(rows, "seq", None),
                P(rows, None),
                P(rows),
                *([P()] * 15),
                P(rows, "seq", None),
            ),
            out_specs=(P(rows, "seq", None), P(rows, "seq", None), *([P()] * 15)),
            check_vma=False,
        )

    def layer(tokens, *others):
        row_count, model = tokens.shape[0] // dp, tokens.shape[2]
        powers = dp & (dp - 1) == 0 and ring & (ring - 1) == 0 and dp >= 4
        if not powers or row_count % ring or model % (16 * dp * ring):
            return placed(split_rows, mesh, "dp")(tokens, *others)
        axes = (FAR, MIDDLE, NEAR)
        finer = jax.sharding.Mesh(mesh.devices.reshape(dp // 4, 2, 2, ring), (*axes, SEQ))
        return placed(deal_rows, finer, axes)(tokens, *others)

    return layer
```

```python
import functools
import math

import jax
import jax.numpy as jnp
from jax import lax
from jax.experimental import pallas as pl
from jax.experimental.pallas import tpu as pltpu
from jax.sharding import PartitionSpec as P

HEADS = 8
EXTRA = 16
LANES = 128
LINE_ROWS = 2
NEG_FILL = -1e30
EPSILON = 1e-05
BLOCK_CAP = 512
LOG2E = 1.4426950408889634
LN2 = 0.6931471805599453
MIB = 1 << 20


def dot(left, right, left_dim, right_dim):
    return lax.dot_general(
        left, right, (((left_dim,), (right_dim,)), ((), ())), preferred_element_type=jnp.float32
    )


def three_parts(values):
    high = values.astype(jnp.bfloat16)
    rest = values - high.astype(jnp.float32)
    middle = rest.astype(jnp.bfloat16)
    low = (rest - middle.astype(jnp.float32)).astype(jnp.bfloat16)
    return high.astype(jnp.float32), middle.astype(jnp.float32), low.astype(jnp.float32)


def extra_rows(base, values, first):
    row = lax.broadcasted_iota(jnp.int32, base.shape, 0)
    for offset, part in enumerate(three_parts(values)):
        base = jnp.where(row == first + offset, part, base)
    return base


def upright(line):
    return jnp.broadcast_to(line, (8, line.shape[1])).T[:, :1]


def project(tokens, weights, query_column, value_column, width):
    shape = HEADS, width, tokens.shape[0]
    query = (dot(weights[0], tokens, 0, 1) + query_column) * (LOG2E * width**-0.5)
    yield query.astype(jnp.bfloat16).reshape(shape)
    yield dot(weights[1], tokens, 0, 1).astype(jnp.bfloat16).reshape(shape)
    yield (dot(weights[2], tokens, 0, 1) + value_column).astype(jnp.bfloat16).reshape(shape)


def prepare_kernel(rows, turns, width, firsts_ref, *refs):
    tokens_ref, cotangent_ref, *refs = refs
    weight_refs, refs = refs[:3], refs[3:]
    query_bias, value_bias, *refs = refs
    sends, refs = refs[: turns * (2 * rows - 1)], refs[turns * (2 * rows - 1) :]
    *projected, tokens_scratch, weights_scratch, sems = refs
    copies = [(ref, weights_scratch.at[i]) for i, ref in enumerate(weight_refs)]
    copies += [(tokens_ref.at[firsts_ref[0] + row], tokens_scratch.at[row]) for row in range(rows)]
    needed = len(copies)
    places = [(tokens_ref, row) for row in range(1, rows)]
    places += [(cotangent_ref, row) for row in range(rows)]
    for turn in range(turns):
        for index, (ref, row) in enumerate(places):
            source = ref.at[pl.ds(firsts_ref[1 + turn] + row, 1)]
            copies.append((source, sends[turn * len(places) + index]))
    copies = [
        pltpu.make_async_copy(source, target, sems.at[i])
        for i, (source, target) in enumerate(copies)
    ]
    for copy in copies:
        copy.start()
    for copy in copies[:needed]:
        copy.wait()
    weights = [weights_scratch[i] for i in range(3)]
    columns = upright(query_bias[...]), upright(value_bias[...])
    for row in range(rows):
        results = project(tokens_scratch[row], weights, *columns, width)
        for ref, result in zip(projected, results):
            ref[row] = result
    for copy in copies[needed:]:
        copy.wait()


def prepare(firsts, rows, tokens, cotangent, weights):
    turns = firsts.shape[0] - 1
    local, model = tokens.shape[1:]
    width = model // HEADS
    query_weight, query_bias, key_weight, value_weight, value_bias = weights
    anywhere = pl.BlockSpec(memory_space=pl.ANY)
    whole = lambda array: pl.BlockSpec(array.shape, lambda i, s: (0,) * array.ndim)
    low = lambda *shape: jax.ShapeDtypeStruct(shape, jnp.bfloat16)
    outs = [low(1, local, model)] * (turns * (2 * rows - 1))
    outs += [low(rows, HEADS, width, local)] * 3
    results = pl.pallas_call(
        functools.partial(prepare_kernel, rows, turns, width),
        out_shape=outs,
        grid_spec=pltpu.PrefetchScalarGridSpec(
            num_scalar_prefetch=1,
            grid=(1,),
            in_specs=[*[anywhere] * 5, whole(query_bias), whole(value_bias)],
            out_specs=[whole(a) for a in outs],
            scratch_shapes=[
                pltpu.VMEM((rows, local, model), jnp.bfloat16),
                pltpu.VMEM((3, model, model), jnp.bfloat16),
                pltpu.SemaphoreType.DMA((3 + rows + turns * (2 * rows - 1),)),
            ],
        ),
        compiler_params=pltpu.CompilerParams(vmem_limit_bytes=60 * MIB),
        cost_estimate=pl.CostEstimate(
            flops=2 * 10**10, bytes_accessed=1, transcendentals=0
        ),
        name="prepare",
    )(firsts, tokens, cotangent, query_weight, key_weight, value_weight, query_bias, value_bias)
    count = 2 * rows - 1
    return [results[turn * count : (turn + 1) * count] for turn in range(turns)], results[-3:]


def attend_kernel(row, pieces, width, block, *refs):
    token_refs, refs = refs[: pieces - 1], refs[pieces - 1 :]
    projected, refs = refs[:3], refs[3:]
    (
        query_extra,
        key_extra,
        query_weight,
        query_bias,
        key_weight,
        value_weight,
        value_bias,
        query_out,
        key_out,
        value_out,
        context_out,
        tokens_scratch,
        weights_scratch,
        query_scratch,
        key_scratch,
        value_scratch,
        context_scratch,
        scores_even,
        scores_odd,
        largest_even,
        largest_odd,
        log_totals,
        in_sems,
        out_sems,
        query_sems,
        context_sems,
    ) = refs
    length = query_scratch.shape[2]
    local = length // pieces
    scratches = query_scratch, key_scratch, value_scratch
    incoming = [(ref.at[0], tokens_scratch.at[i]) for i, ref in enumerate(token_refs)]
    weight_refs = query_weight, key_weight, value_weight
    incoming += [(ref, weights_scratch.at[i]) for i, ref in enumerate(weight_refs)]
    incoming += [
        (ref.at[row], scratch.at[:, pl.ds(0, width), pl.ds(0, local)])
        for ref, scratch in zip(projected, scratches)
    ]
    incoming = [
        pltpu.make_async_copy(source, target, in_sems.at[i])
        for i, (source, target) in enumerate(incoming)
    ]
    for copy in incoming:
        copy.start()
    row = lax.broadcasted_iota(jnp.int32, (EXTRA, length), 0)
    ones = (row < 3).astype(jnp.bfloat16)
    query_base = query_extra[...]
    for head in range(HEADS):
        query_scratch[head, width:] = query_base.astype(jnp.bfloat16)
        key_scratch[head, width:] = key_extra[...].astype(jnp.bfloat16)
        value_scratch[head, width:] = ones
    columns = upright(query_bias[...]), upright(value_bias[...])
    for copy in incoming:
        copy.wait()
    weights = [weights_scratch[i] for i in range(3)]
    for piece in range(1, pieces):
        span = pl.ds(piece * local, local)
        results = project(tokens_scratch[piece - 1], weights, *columns, width)
        for scratch, result in zip(scratches, results):
            scratch[:, :width, span] = result
    outgoing = [
        pltpu.make_async_copy(key_scratch, key_out.at[0], out_sems.at[0]),
        pltpu.make_async_copy(value_scratch, value_out.at[0], out_sems.at[1]),
    ]
    for copy in outgoing:
        copy.start()

    def pair_copies(pair):
        heads = pl.ds(pair * 2, 2)
        rows = pl.ds(pl.multiple_of(pair * 2 * width, 2 * width), 2 * width)
        return (
            pltpu.make_async_copy(
                query_scratch.at[heads], query_out.at[0, heads], query_sems.at[pair]
            ),
            pltpu.make_async_copy(
                context_scratch.at[rows], context_out.at[rows], context_sems.at[pair]
            ),
        )

    def score(head, scores_ref, largest_ref, start):
        span = pl.ds(start, block)
        scores = dot(key_scratch[head], query_scratch[head, :, span], 0, 0)
        scores_ref[:, span] = scores
        largest_ref[:, span] = jnp.max(scores, 0, keepdims=True)

    def weigh(head, scores_ref, largest_ref, start):
        span = pl.ds(start, block)
        largest = largest_ref[:, span]
        weights = jnp.exp2(scores_ref[:, span] - largest).astype(jnp.bfloat16)
        update = dot(value_scratch[head], weights, 1, 0)
        total = update[width : width + 1]
        context_scratch[pl.ds(pl.multiple_of(head * width, width), width), span] = (
            update[:width] / total
        )
        log_totals[pl.ds(head, 1), span] = largest + jnp.log(total) * LOG2E

    starts = range(0, length, block)
    for start in starts:
        score(0, scores_even, largest_even, start)

    def head_pair(pair, carry):
        head = pair * 2
        for start in starts:
            score(head + 1, scores_odd, largest_odd, start)
            weigh(head, scores_even, largest_even, start)
        following = jnp.minimum(head + 2, HEADS - 1)
        for start in starts:
            score(following, scores_even, largest_even, start)
            weigh(head + 1, scores_odd, largest_odd, start)
        for side in range(2):
            log_total = log_totals[pl.ds(head + side, 1), :]
            query_scratch[head + side, width:] = extra_rows(query_base, -log_total, 3).astype(
                jnp.bfloat16
            )
        for copy in pair_copies(pair):
            copy.start()
        return carry

    lax.fori_loop(0, HEADS // 2, head_pair, 0)
    for pair in range(HEADS // 2):
        outgoing.extend(pair_copies(pair))
    for copy in outgoing:
        copy.wait()


def attend(row, projected, remote, query_extra, key_extra, weights):
    pieces = 1 + len(remote)
    _, heads, width, local = projected[0].shape
    model = heads * width
    length = pieces * local
    whole = lambda array: pl.BlockSpec(array.shape, lambda i: (0,) * array.ndim)
    anywhere = pl.BlockSpec(memory_space=pl.ANY)
    low = jax.ShapeDtypeStruct((1, HEADS, width + EXTRA, length), jnp.bfloat16)
    outs = (low, low, low, jax.ShapeDtypeStruct((model, length), jnp.float32))
    query_weight, query_bias, key_weight, value_weight, value_bias = weights
    head_scratch = pltpu.VMEM(low.shape[1:], jnp.bfloat16)
    return pl.pallas_call(
        functools.partial(attend_kernel, row, pieces, width, min(256, length)),
        out_shape=outs,
        grid_spec=pltpu.PrefetchScalarGridSpec(
            num_scalar_prefetch=0,
            grid=(1,),
            in_specs=[
                *[anywhere] * (pieces + 2),
                whole(query_extra),
                whole(key_extra),
                anywhere,
                whole(query_bias),
                anywhere,
                anywhere,
                whole(value_bias),
            ],
            out_specs=[anywhere] * 4,
            scratch_shapes=[
                pltpu.VMEM((max(pieces - 1, 1), local, model), jnp.bfloat16),
                pltpu.VMEM((3, model, model), jnp.bfloat16),
                head_scratch,
                head_scratch,
                head_scratch,
                pltpu.VMEM((model, length), jnp.float32),
                pltpu.VMEM((length, length), jnp.float32),
                pltpu.VMEM((length, length), jnp.float32),
                pltpu.VMEM((1, length), jnp.float32),
                pltpu.VMEM((1, length), jnp.float32),
                pltpu.VMEM((HEADS, length), jnp.float32),
                pltpu.SemaphoreType.DMA((5 + pieces,)),
                pltpu.SemaphoreType.DMA((2,)),
                pltpu.SemaphoreType.DMA((HEADS // 2,)),
                pltpu.SemaphoreType.DMA((HEADS // 2,)),
            ],
        ),
        compiler_params=pltpu.CompilerParams(vmem_limit_bytes=60 * MIB),
        cost_estimate=pl.CostEstimate(
            flops=3 * 10**9, bytes_accessed=1, transcendentals=0
        ),
        name="attend",
    )(*remote, *projected, query_extra, key_extra, *weights)


def row_mean(values):
    return jnp.mean(values, -1, keepdims=True)


def normalise(values):
    centred = values - row_mean(values)
    scale = lax.rsqrt(row_mean(centred * centred) + EPSILON)
    return centred * scale, scale


def norm_back(grad, gain, normed, scale):
    entering = grad * gain
    return (entering - row_mean(entering) - normed * row_mean(entering * normed)) * scale


def column_sum(values):
    return jnp.sum(values, 0, keepdims=True)


def gelu_parts(values):
    phi = 0.5 + 0.5 * lax.erf(values * 0.5**0.5)
    bell = jnp.exp2(values * values * (-0.5 * LOG2E))
    return values * phi, phi + values * bell * 0.3989422804014327


def token_kernel(rows, pieces, steps, width, *refs):
    _, keep_ref, me_ref, refs = *refs[:3], refs[3:]
    own_tokens, own_cotangent, refs = *refs[:2], refs[2:]
    remote_count = rows * (pieces - 1)
    remote_tokens, refs = refs[:remote_count], refs[remote_count:]
    remote_cotangents, refs = refs[:remote_count], refs[remote_count:]
    context_refs, refs = refs[:rows], refs[rows:]
    (
        out_weight,
        out_bias,
        first_gain,
        first_shift,
        up_weight,
        up_bias,
        down_weight,
        down_bias,
        second_gain,
        second_shift,
    ) = refs[:10]
    refs = refs[10:]
    layer_outs, refs = refs[: rows * pieces], refs[rows * pieces :]
    (
        grad_out_heads,
        grad_first_out,
        near_out,
        far_out,
        up_scratch,
        down_scratch,
        result_scratch,
        packed_near,
        packed_far,
        sems,
        tokens_scratch,
        cotangent_scratch,
        context_scratch,
        act_scratch,
        slope_scratch,
        totals,
        lines,
        *line_sums,
    ) = refs
    (
        grad_out_bias,
        grad_first_gain,
        grad_first_shift,
        grad_down_bias,
        grad_second_gain,
        grad_second_shift,
        grad_value_bias,
        grad_up_bias,
    ) = line_sums
    row_index = pl.program_id(0)
    piece_index = pl.program_id(1)
    step_index = pl.program_id(2)
    tokens_len, model = tokens_scratch.shape
    hidden_units = up_weight.shape[1]
    kept = keep_ref[row_index] != 0
    span = pl.ds(pl.multiple_of(step_index * tokens_len, tokens_len), tokens_len)

    @pl.when(piece_index == 0)
    def _():
        tokens_scratch[...] = own_tokens[0, span]
        cotangent_scratch[...] = own_cotangent[0, span]

    first_step = (row_index == 0) & (piece_index == 0) & (step_index == 0)
    last_step = (row_index == rows - 1) & (piece_index == pieces - 1) & (step_index == steps - 1)
    fetches = [
        pltpu.make_async_copy(up_weight, up_scratch, sems.at[0]),
        pltpu.make_async_copy(down_weight, down_scratch, sems.at[1]),
    ]

    @pl.when(first_step)
    def _():
        for copy in fetches:
            copy.start()

    for row in range(rows):

        @pl.when(row_index == row)
        def _():
            context_scratch[...] = context_refs[row][...]

        for piece in range(1, pieces):

            @pl.when((row_index == row) & (piece_index == piece))
            def _():
                position = row * (pieces - 1) + piece - 1
                tokens_scratch[...] = remote_tokens[position][0, span]
                cotangent_scratch[...] = remote_cotangents[position][0, span]

    @pl.when(first_step)
    def _():
        for ref in (totals, lines, *line_sums):
            ref[...] = jnp.zeros(ref.shape, ref.dtype)

    tokens = tokens_scratch[...].astype(jnp.float32)
    context = context_scratch[...]
    context_low = context.astype(jnp.bfloat16)
    first_sum = tokens + (dot(context_low, out_weight[...], 0, 0) + out_bias[...])
    first_normed, first_scale = normalise(first_sum)
    hidden = first_normed * first_gain[...] + first_shift[...]
    hidden_low = hidden.astype(jnp.bfloat16)

    @pl.when(first_step)
    def _():
        for copy in fetches:
            copy.wait()

    pre_act = dot(hidden_low, up_scratch[...], 1, 0) + up_bias[...]
    activated, slope = gelu_parts(pre_act)
    act_low = activated.astype(jnp.bfloat16)
    act_scratch[...] = act_low
    slope_scratch[...] = slope
    branch = dot(act_low, down_scratch[...], 1, 0) + down_bias[...]
    second_normed, second_scale = normalise(hidden + branch)
    result = jnp.where(
        kept, second_normed * second_gain[...] + second_shift[...], tokens
    ).astype(jnp.bfloat16)
    gives = [
        pltpu.make_async_copy(result_scratch, ref.at[0, span], sems.at[2]) for ref in layer_outs
    ]

    @pl.when(jnp.logical_not(first_step))
    def _():
        gives[0].wait()

    result_scratch[...] = result
    for position, copy in enumerate(gives):

        @pl.when(row_index * pieces + piece_index == position)
        def _():
            copy.start()

    cotangent = cotangent_scratch[...].astype(jnp.float32)
    grad_out = jnp.where(kept, cotangent, 0.0)
    grad_second_gain[...] += column_sum(grad_out * second_normed)
    grad_second_shift[...] += column_sum(grad_out)
    grad_second = norm_back(grad_out, second_gain[...], second_normed, second_scale)
    grad_branch_low = grad_second.astype(jnp.bfloat16)
    grad_down_bias[...] += column_sum(grad_branch_low.astype(jnp.float32))
    grad_act = dot(grad_branch_low, down_scratch[...], 1, 1)
    grad_pre_low = (grad_act * slope_scratch[...]).astype(jnp.bfloat16)
    grad_hidden = grad_second + dot(grad_pre_low, up_scratch[...], 1, 1)
    totals[pl.ds(hidden_units, hidden_units), :] += dot(act_scratch[...], grad_branch_low, 0, 0)
    for start in range(0, hidden_units, model):
        totals[pl.ds(start, model), :] += dot(
            hidden_low, grad_pre_low[:, start : start + model], 0, 0
        )
    grad_up_bias[...] += column_sum(grad_pre_low.astype(jnp.float32))
    grad_first_gain[...] += column_sum(grad_hidden * first_normed)
    grad_first_shift[...] += column_sum(grad_hidden)
    grad_first = norm_back(grad_hidden, first_gain[...], first_normed, first_scale)
    grad_first_out[0] = jnp.where(kept, grad_first, cotangent)
    grad_attn_low = grad_first.astype(jnp.bfloat16)
    grad_out_bias[...] += column_sum(grad_attn_low.astype(jnp.float32))
    totals[pl.ds(2 * hidden_units, model), :] += dot(context_low, grad_attn_low, 1, 0)
    grad_context = dot(out_weight[...], grad_attn_low, 1, 1).astype(jnp.bfloat16)
    grad_context_wide = grad_context.astype(jnp.float32)
    ones = jnp.ones((EXTRA, tokens_len), jnp.bfloat16)
    grad_value_bias[...] += dot(ones, grad_context, 1, 1)[:1]
    product = grad_context_wide * context
    blank = jnp.zeros((EXTRA, tokens_len), jnp.float32)
    for head in range(HEADS):
        columns = slice(head * width, (head + 1) * width)
        grad_out_heads[0, head, :width] = grad_context[columns]
        spread = jnp.sum(product[columns], 0, keepdims=True)
        grad_out_heads[0, head, width:] = extra_rows(blank, -spread, 0).astype(jnp.bfloat16)

    @pl.when(last_step)
    def _():
        first = 0
        for ref in line_sums:
            set_lines(lines, first, ref[...])
            first += ref.shape[1] // LANES
        copies = [gives[0]]
        for half, out, sem in ((packed_far, far_out, 0), (packed_near, near_out, 1)):
            pack([totals], lines, *((None, half) if sem == 0 else (half, None)), me_ref[0])
            copies.append(pltpu.make_async_copy(half, out, sems.at[sem]))
            copies[-1].start()
        for copy in copies:
            copy.wait()


def set_lines(lines, first, values):
    width = lines.shape[2]
    for block in range(values.shape[1] // width):
        slot, row = divmod(first + block, LINE_ROWS)
        lines[slot, row : row + 1] = values[:, block * width : (block + 1) * width]


def pack(parts, lines, near, far, me):
    half, size, width = (near if far is None else far).shape
    columns = [(ref, start) for ref in parts for start in range(0, ref.shape[1], width)]
    height = parts[0].shape[0] // (2 * half)

    def one(slot, carry):
        for ref, first in ((near, 0), (far, half)):
            if ref is None:
                continue
            piece = (slot + first) ^ me
            rows = pl.ds(pl.multiple_of(piece * height, EXTRA), height)
            for block, (source, start) in enumerate(columns):
                ref[slot, pl.ds(block * height, height), :] = source[
                    rows, pl.ds(start, width)
                ].astype(jnp.bfloat16)
            ref[slot, pl.ds(len(columns) * height, EXTRA), :] = jnp.concatenate(
                [lines[piece], jnp.zeros_like(lines[piece])], 0
            ).astype(jnp.bfloat16)
        return carry

    lax.fori_loop(0, half, one, 0)


def packed_shape(slots, rows, model):
    return jax.ShapeDtypeStruct(
        (slots // 2, rows * (model // LANES) // slots + EXTRA, LANES), jnp.bfloat16
    )


def lines_shape(slots):
    return pltpu.VMEM((slots, EXTRA // 2, LANES), jnp.float32)


def by_token(
    row_index, keep, me, tokens, remote, cotangent, remote_cotangent, contexts, weights, slots
):
    rows = len(contexts)
    pieces = 1 + len(remote[0])
    local, model = tokens.shape[1:]
    length = pieces * local
    width = model // HEADS
    hidden_units = weights[4].shape[1]
    tokens_len = min(512, local)
    steps = local // tokens_len
    whole = lambda array: pl.BlockSpec(array.shape, lambda r, i, j, s, k, m: (0,) * array.ndim)
    own_spec = pl.BlockSpec((1, local, model), lambda r, i, j, s, k, m: (s[0] + r, 0, 0))
    f32 = lambda *shape: jax.ShapeDtypeStruct(shape, jnp.float32)
    anywhere = pl.BlockSpec(memory_space=pl.ANY)
    total_rows = 2 * hidden_units + model
    packed = packed_shape(slots, total_rows, model)
    piece_out = jax.ShapeDtypeStruct((1, local, model), jnp.bfloat16)
    gradient_outs = (packed, packed)
    line_lengths = [model] * 7 + [hidden_units]
    outs = (
        *([piece_out] * (rows * pieces)),
        jax.ShapeDtypeStruct((rows, HEADS, width + EXTRA, length), jnp.bfloat16),
        f32(rows, length, model),
        *gradient_outs,
    )
    out_specs = (
        *([anywhere] * (rows * pieces)),
        pl.BlockSpec(
            (1, HEADS, width + EXTRA, tokens_len),
            lambda r, i, j, s, k, m: (r, 0, 0, i * steps + j),
        ),
        pl.BlockSpec((1, tokens_len, model), lambda r, i, j, s, k, m: (r, i * steps + j, 0)),
        anywhere,
        anywhere,
    )

    def context_spec(row):
        def block(r, i, j, s, k, m):
            step = i * steps + j
            return 0, jnp.where(r < row, 0, jnp.where(r > row, pieces * steps - 1, step))

        return pl.BlockSpec((model, tokens_len), block)

    flat_remote = [array for arrays in remote for array in arrays]
    flat_remote_cotangent = [array for arrays in remote_cotangent for array in arrays]
    in_specs = (
        own_spec,
        own_spec,
        *[whole(a) for a in (*flat_remote, *flat_remote_cotangent)],
        *[context_spec(row) for row in range(rows)],
        *[anywhere if a.shape[0] * a.shape[1] > model * model else whole(a) for a in weights],
    )
    return pl.pallas_call(
        functools.partial(token_kernel, rows, pieces, steps, width),
        out_shape=outs,
        grid_spec=pltpu.PrefetchScalarGridSpec(
            num_scalar_prefetch=3,
            grid=(rows, pieces, steps),
            in_specs=in_specs,
            out_specs=out_specs,
            scratch_shapes=[
                pltpu.VMEM((model, hidden_units), jnp.bfloat16),
                pltpu.VMEM((hidden_units, model), jnp.bfloat16),
                pltpu.VMEM((tokens_len, model), jnp.bfloat16),
                pltpu.VMEM(packed.shape, jnp.bfloat16),
                pltpu.VMEM(packed.shape, jnp.bfloat16),
                pltpu.SemaphoreType.DMA((3,)),
                pltpu.VMEM((tokens_len, model), jnp.bfloat16),
                pltpu.VMEM((tokens_len, model), jnp.bfloat16),
                pltpu.VMEM((model, tokens_len), jnp.float32),
                pltpu.VMEM((tokens_len, hidden_units), jnp.bfloat16),
                pltpu.VMEM((tokens_len, hidden_units), jnp.float32),
                pltpu.VMEM((total_rows, model), jnp.float32),
                lines_shape(slots),
                *[pltpu.VMEM((1, n), jnp.float32) for n in line_lengths],
            ],
        ),
        compiler_params=pltpu.CompilerParams(vmem_limit_bytes=60 * MIB),
        cost_estimate=pl.CostEstimate(flops=1, bytes_accessed=1, transcendentals=0),
        name="by_token",
    )(
        row_index,
        keep,
        me,
        tokens,
        cotangent,
        *flat_remote,
        *flat_remote_cotangent,
        *contexts,
        *weights,
    )


def attend_back_kernel(pieces, width, block, place, *refs):
    row, rows, part, parts = place
    first_row, last_part = row == 0, part == parts - 1
    packing = row == rows - 1 and last_part
    row_ref, me_ref, refs = *refs[:2], refs[2:]
    token_refs, refs = refs[:pieces], refs[pieces:]
    head_refs, refs = refs[:4], refs[4:]
    grad_tokens_in, *weight_refs, refs = *refs[:4], refs[4:]
    if not first_row:
        totals_in, bias_in, refs = *refs[:2], refs[2:]
    earlier = part if packing else 0
    earlier_totals, refs = refs[:earlier], refs[earlier:]
    earlier_biases, refs = refs[:earlier], refs[earlier:]
    outs = pieces if last_part else 1
    grad_tokens, refs = refs[:outs], refs[outs:]
    if packing:
        packed_near, packed_far, *refs = refs
    else:
        totals_out, bias, *refs = refs
    (
        grad_query_scratch,
        grad_key_scratch,
        grad_value_scratch,
        tokens_scratch,
        grad_scratch,
        weights_scratch,
        totals,
        sems,
        *refs,
    ) = refs
    if packing:
        lines, bias, *earlier_scratch = refs
    query_ref, key_ref, value_ref, grad_ref = (ref.at[0] for ref in head_refs)
    pair = pl.program_id(0)
    pairs = pl.num_programs(0)
    length = query_ref.shape[2]
    local = length // pieces
    model, columns = weights_scratch.shape[1:]
    pair_width = 2 * width
    share = pl.ds(part * columns, columns)
    incoming = [(token_refs[0].at[row_ref[0]], tokens_scratch.at[0])]
    incoming += [(ref.at[0], tokens_scratch.at[i + 1]) for i, ref in enumerate(token_refs[1:])]
    incoming.append((grad_tokens_in.at[row if part == 0 else 0], grad_scratch))
    incoming += [(ref.at[:, share], weights_scratch.at[i]) for i, ref in enumerate(weight_refs)]
    if not first_row:
        incoming.append((totals_in, totals))
    if packing:
        incoming += list(zip(earlier_totals, earlier_scratch))
    incoming = [
        pltpu.make_async_copy(source, target, sems.at[i])
        for i, (source, target) in enumerate(incoming)
    ]

    @pl.when(pair == 0)
    def _():
        for copy in incoming:
            copy.start()

    grad_queries = [[], []]
    for side in range(2):
        key = key_ref[side]
        value = value_ref[side]
        grad_key = 0.0
        grad_value = 0.0
        for start in range(0, length, block):
            span = pl.ds(start, block)
            query = query_ref[side, :, span]
            grad = grad_ref[side, :, span]
            weights = jnp.exp2(dot(query, key, 0, 0))
            grad_weights = dot(grad, value, 0, 0)
            weights_low = weights.astype(jnp.bfloat16)
            grad_scores = (weights * grad_weights).astype(jnp.bfloat16)
            grad_value = grad_value + dot(grad[:width], weights_low, 1, 0)
            grad_key = grad_key + dot(query[:width], grad_scores, 1, 0)
            grad_queries[side].append(dot(grad_scores, key[:width], 1, 1))
        head = pl.ds(pl.multiple_of(pair * pair_width + side * width, width), width)
        grad_value_scratch[head, :] = grad_value.astype(jnp.bfloat16)
        grad_key_scratch[head, :] = (grad_key * LN2).astype(jnp.bfloat16)
    for index, start in enumerate(range(0, length, block)):
        both = jnp.concatenate([grad_queries[0][index], grad_queries[1][index]], 1)
        grad_query_scratch[pair, pl.ds(start, block)] = (both * width**-0.5).astype(jnp.bfloat16)

    @pl.when(pair == pairs - 1)
    def _():
        for copy in incoming:
            copy.wait()
        count = grad_query_scratch.shape[0]
        for index in range(count):
            lanes = pl.ds(index * pair_width, pair_width)
            total = column_sum(grad_query_scratch[index].astype(jnp.float32))
            bias[:, lanes] = total if first_row else bias_in[:, lanes] + total
        grad_query = jnp.concatenate([grad_query_scratch[index] for index in range(count)], 1)
        outgoing = []
        for position in range(3):
            lines_of = pl.ds(position * model, model)
            term = 0.0
            for piece in range(pieces):
                span = slice(piece * local, (piece + 1) * local)
                tokens = tokens_scratch[piece]
                if position == 0:
                    term = term + dot(tokens, grad_query[span], 0, 0)
                else:
                    source = grad_key_scratch if position == 1 else grad_value_scratch
                    term = term + dot(tokens, source[:, span], 0, 1)
            totals[lines_of, :] = term if first_row else totals[lines_of, :] + term
        if not packing:
            outgoing.append(pltpu.make_async_copy(totals, totals_out, sems.at[0]))
            outgoing[0].start()
        for piece in range(pieces):
            span = pl.ds(piece * local, local)
            total = (
                grad_scratch[span]
                + dot(grad_query[piece * local : (piece + 1) * local], weights_scratch[0], 1, 1)
                + dot(grad_key_scratch[:, span], weights_scratch[1], 0, 1)
                + dot(grad_value_scratch[:, span], weights_scratch[2], 0, 1)
            )
            if last_part:
                grad_tokens[piece][0] = total.astype(jnp.bfloat16)
            else:
                grad_scratch[span] = total
                outgoing.append(
                    pltpu.make_async_copy(
                        grad_scratch.at[span], grad_tokens[0].at[0, span], sems.at[1 + piece]
                    )
                )
                outgoing[-1].start()
        if packing:
            lines[...] = jnp.zeros(lines.shape, lines.dtype)
            first = 0
            for ref in (*earlier_biases, bias):
                set_lines(lines, first, ref[...])
                first += ref.shape[1] // LANES
            pack([*earlier_scratch, totals], lines, packed_near, packed_far, me_ref[0])
        for copy in outgoing:
            copy.wait()


def attend_back(
    place, row_index, me, tokens, remote, heads, grad_tokens, weights, totals, biases, slots, gflops
):
    row, rows, part, parts = place
    last_part = part == parts - 1
    packing = row == rows - 1 and last_part
    pieces = 1 + len(remote)
    local, model = tokens.shape[1:]
    length = pieces * local
    width = model // HEADS
    columns = model // parts
    pairs = HEADS // parts // 2
    anywhere = pl.BlockSpec(memory_space=pl.ANY)
    whole = lambda array: pl.BlockSpec(array.shape, lambda i, s, m: (0,) * array.ndim)
    head_spec = lambda array: pl.BlockSpec(
        (1, 2, *array.shape[2:]),
        lambda i, s, m: (row if array.shape[0] > 1 else 0, part * pairs + i, 0, 0),
    )
    f32 = lambda *shape: jax.ShapeDtypeStruct(shape, jnp.float32)
    if last_part:
        outs = [jax.ShapeDtypeStruct((1, local, model), jnp.bfloat16)] * pieces
        out_specs = [whole(a) for a in outs]
    else:
        outs, out_specs = [f32(1, length, model)], [anywhere]
    total, bias = f32(3 * model, columns), f32(1, columns)
    in_specs = [anywhere] * pieces + [head_spec(a) for a in heads] + [anywhere] * 4
    operands = [tokens, *remote, *heads, grad_tokens, *weights]
    if row:
        operands += [totals[part], biases[part]]
        in_specs += [anywhere, whole(bias)]
    scratch = [
        pltpu.VMEM((pairs, length, 2 * width), jnp.bfloat16),
        pltpu.VMEM((columns, length), jnp.bfloat16),
        pltpu.VMEM((columns, length), jnp.bfloat16),
        pltpu.VMEM((pieces, local, model), jnp.bfloat16),
        pltpu.VMEM((length, model), jnp.float32),
        pltpu.VMEM((3, model, columns), jnp.bfloat16),
        pltpu.VMEM(total.shape, jnp.float32),
        pltpu.SemaphoreType.DMA((pieces + 5 + parts,)),
    ]
    if packing:
        operands += [*totals[:part], *biases[:part]]
        in_specs += [anywhere] * part + [whole(bias)] * part
        packed = packed_shape(slots, 3 * model, model)
        outs += [packed] * 2
        out_specs += [whole(packed)] * 2
        scratch += [lines_shape(slots), pltpu.VMEM(bias.shape, jnp.float32)]
        scratch += [pltpu.VMEM(total.shape, jnp.float32)] * part
    else:
        outs += [total, bias]
        out_specs += [anywhere, whole(bias)]
    return pl.pallas_call(
        functools.partial(attend_back_kernel, pieces, width, min(256, length), place),
        out_shape=outs,
        grid_spec=pltpu.PrefetchScalarGridSpec(
            num_scalar_prefetch=2,
            grid=(pairs,),
            in_specs=in_specs,
            out_specs=out_specs,
            scratch_shapes=scratch,
        ),
        compiler_params=pltpu.CompilerParams(vmem_limit_bytes=60 * MIB),
        cost_estimate=pl.CostEstimate(
            flops=gflops * 10**9, bytes_accessed=1, transcendentals=0
        ),
        name="attend_back",
    )(row_index, me, *operands)


def unpack_kernel(moves, model, counts, me_ref, *refs):
    sources, refs = refs[: counts[0]], refs[counts[0] :]
    outs, refs = refs[: counts[1]], refs[counts[1] :]
    lines, refs = refs[: counts[2]], refs[counts[2] :]
    *blocks_out, slots, in_sems, out_sems = refs
    count = counts[0]
    _, size, width = slots.shape
    me = me_ref[0]
    share = slots.shape[0] // count
    copies = [
        pltpu.make_async_copy(source, slots.at[pl.ds(index * share, share)], in_sems.at[index])
        for index, source in enumerate(sources)
    ]
    for copy in copies:
        copy.start()
    for copy in copies:
        copy.wait()
    index = 0
    for line in lines:
        for block in range(line.shape[1] // width):
            piece, row = divmod(index, LINE_ROWS)
            extra = slots[piece ^ me, pl.ds(size - EXTRA, EXTRA), :].astype(jnp.float32)
            line[:, pl.ds(block * width, width)] = extra[row : row + 1]
            index += 1
    copies = []
    for square, (out, row, column, pieces) in enumerate(moves):
        for piece, start, rows, inside, offset in pieces:
            blocks_out[out][pl.ds(row + inside, rows), pl.ds(column + offset, width)] = slots[
                piece ^ me, pl.ds(start, rows), :
            ].astype(jnp.float32)
        part = pl.ds(row, model), pl.ds(column, model)
        copies.append(
            pltpu.make_async_copy(
                blocks_out[out].at[part], outs[out].at[part], out_sems.at[square]
            )
        )
        copies[-1].start()
    for copy in copies:
        copy.wait()


def unpack(me, arrays, shapes, model, lengths):
    share, size, width = arrays[0].shape
    slots = share * len(arrays)
    blocks = model // width
    height = (size - EXTRA) // blocks
    moves = [
        (out, row, column, [])
        for out, shape in enumerate(shapes)
        for row in range(0, shape[0], model)
        for column in range(0, shape[1], model)
    ]
    for piece in range(slots):
        done = 0
        while done < height:
            square, inside = divmod(piece * height + done, model)
            rows = min(height - done, model - inside)
            for block in range(blocks):
                moves[square][3].append(
                    (piece, block * height + done, rows, inside, block * width)
                )
            done += rows
    outs = [jax.ShapeDtypeStruct(shape, jnp.float32) for shape in shapes]
    lines = [jax.ShapeDtypeStruct((1, n), jnp.float32) for n in lengths]
    anywhere = pl.BlockSpec(memory_space=pl.ANY)
    return pl.pallas_call(
        functools.partial(unpack_kernel, moves, model, (len(arrays), len(outs), len(lines))),
        out_shape=[*outs, *lines],
        grid_spec=pltpu.PrefetchScalarGridSpec(
            num_scalar_prefetch=1,
            grid=(1,),
            in_specs=[anywhere] * len(arrays),
            out_specs=[
                *[anywhere] * len(outs),
                *[pl.BlockSpec(a.shape, lambda i, m: (0, 0)) for a in lines],
            ],
            scratch_shapes=[
                *[pltpu.VMEM(a.shape, jnp.float32) for a in outs],
                pltpu.VMEM((slots, size, width), jnp.bfloat16),
                pltpu.SemaphoreType.DMA((len(arrays),)),
                pltpu.SemaphoreType.DMA((len(moves),)),
            ],
        ),
        compiler_params=pltpu.CompilerParams(vmem_limit_bytes=60 * MIB),
        cost_estimate=pl.CostEstimate(
            flops=2 * 10**10, bytes_accessed=1, transcendentals=0
        ),
        name="unpack",
    )(me, *arrays)


NEAR, MIDDLE, FAR, SEQ = AXES = ("near", "middle", "far", "seq")
STAGES = ((NEAR,), (MIDDLE, SEQ), (FAR,))


def add_up(arrays):
    arrays = [a.astype(jnp.float32) for a in arrays]
    while len(arrays) > 1:
        arrays = [first + second for first, second in zip(arrays[::2], arrays[1::2], strict=True)]
    return arrays[0].astype(jnp.bfloat16)


def after(arrays, *others):
    return lax.optimization_barrier((arrays, others))[0]


class Sums:
    def __init__(self):
        self.sizes = [lax.axis_size(axes) for axes in STAGES]
        self.devices = math.prod(self.sizes)
        digits = [lax.axis_index(axes) for axes in STAGES]
        self.me = (digits[0] * self.sizes[1] + digits[1]) * self.sizes[2] + digits[2]
        self.me_near = self.me - digits[2]

    def swap(self, array, stage, turn):
        pairs = [(i, i ^ turn) for i in range(self.sizes[stage])]
        return lax.ppermute(array, STAGES[stage], pairs)

    def meet(self, parts, stage):
        return [parts[0], *[self.swap(parts[t], stage, t) for t in range(1, len(parts))]]

    def add_parts(self, arrays, stage):
        size = self.sizes[stage]
        share = arrays[0].shape[0] // size
        return [
            add_up([array[turn * share : (turn + 1) * share] for array in arrays])
            for turn in range(size)
        ]

    def others(self, held, stage):
        return [self.swap(held, stage, turn) for turn in range(1, self.sizes[stage])]


def norm_rows(values, gain, shift):
    row_mean = jnp.mean(values, -1, keepdims=True)
    centred = values - row_mean
    variance = jnp.mean(centred * centred, -1, keepdims=True)
    return centred * lax.rsqrt(variance + EPSILON) * gain + shift


def gelu_exact(values):
    return jax.nn.gelu(values, approximate=False)


def plain_dot(left, right):
    return jnp.dot(left, right, preferred_element_type=jnp.float32)


def left_dot(left, right):
    return lax.dot_general(
        left, right, (((0,), (0,)), ((), ())), preferred_element_type=jnp.float32
    )


def right_dot(left, right):
    return lax.dot_general(
        left, right, (((1,), (1,)), ((), ())), preferred_element_type=jnp.float32
    )


def token_sum(values):
    return jnp.sum(values.astype(jnp.float32), 0)


def split_heads(values, piece_len):
    return values.reshape(values.shape[0], piece_len, HEADS, values.shape[2] // HEADS)


def block_length(piece_len, local_len):
    return math.gcd(math.gcd(piece_len, local_len), BLOCK_CAP)


def masked_scores(query_heads, key_heads, query_ids, key_ids, score_scale):
    scores = (
        jnp.einsum("rqhd,rkhd->rhqk", query_heads, key_heads, preferred_element_type=jnp.float32)
        * score_scale
    )
    same_doc = query_ids[:, None, :, None] == key_ids[:, None, None, :]
    return jnp.where(same_doc, scores, NEG_FILL)


def split_attend_back(
    query_heads,
    grad_heads,
    log_total,
    spread,
    query_ids,
    key_heads,
    value_heads,
    key_ids,
    score_scale,
):
    scores = masked_scores(query_heads, key_heads, query_ids, key_ids, score_scale)
    weights = jnp.exp(scores - jnp.transpose(log_total, (0, 2, 1))[..., None])
    grad_value = jnp.einsum(
        "rhqk,rqhd->rkhd",
        weights.astype(jnp.bfloat16),
        grad_heads,
        preferred_element_type=jnp.float32,
    )
    grad_weights = jnp.einsum(
        "rqhd,rkhd->rhqk", grad_heads, value_heads, preferred_element_type=jnp.float32
    )
    grad_scores = (weights * (grad_weights - jnp.transpose(spread, (0, 2, 1))[..., None])).astype(
        jnp.bfloat16
    )
    grad_query = (
        jnp.einsum("rhqk,rkhd->rqhd", grad_scores, key_heads, preferred_element_type=jnp.float32)
        * score_scale
    )
    grad_key = (
        jnp.einsum("rhqk,rqhd->rkhd", grad_scores, query_heads, preferred_element_type=jnp.float32)
        * score_scale
    )
    return (grad_query, grad_key, grad_value)


def add_into(buffer, term, block_start):
    current = lax.dynamic_slice_in_dim(buffer, block_start, term.shape[1], 1)
    return lax.dynamic_update_slice_in_dim(buffer, current + term, block_start, 1)


def split_rows(
    tokens,
    segments,
    keep_flags,
    query_weight,
    query_bias,
    key_weight,
    value_weight,
    value_bias,
    out_weight,
    out_bias,
    first_gain,
    first_shift,
    up_weight,
    up_bias,
    down_weight,
    down_bias,
    second_gain,
    second_shift,
    cotangent,
):
    row_count, local_tokens, model_width = tokens.shape
    head_width = model_width // HEADS
    score_scale = head_width ** (-0.5)
    flat_tokens = tokens.reshape(row_count * local_tokens, model_width)
    row_shape = (row_count, local_tokens, model_width)
    query_low = (
        (plain_dot(flat_tokens, query_weight) + query_bias).astype(jnp.bfloat16).reshape(row_shape)
    )
    key_low = plain_dot(flat_tokens, key_weight).astype(jnp.bfloat16).reshape(row_shape)
    value_low = (
        (plain_dot(flat_tokens, value_weight) + value_bias).astype(jnp.bfloat16).reshape(row_shape)
    )
    query_heads = split_heads(query_low, local_tokens)
    own_start = lax.axis_index("seq") * local_tokens
    own_ids = lax.dynamic_slice_in_dim(segments, own_start, local_tokens, 1)
    initial = (
        jnp.full((row_count, HEADS, local_tokens), NEG_FILL, jnp.float32),
        jnp.zeros((row_count, HEADS, local_tokens), jnp.float32),
        jnp.zeros((row_count, HEADS, local_tokens, head_width), jnp.float32),
    )
    key_piece = lax.all_gather(key_low, "seq", axis=1, tiled=True)
    value_piece = lax.all_gather(value_low, "seq", axis=1, tiled=True)
    block_size = block_length(key_piece.shape[1], local_tokens)

    def key_step(position, inner_state):
        running_max, running_sum, running_acc = inner_state
        block_start = position * block_size
        key_heads = split_heads(
            lax.dynamic_slice_in_dim(key_piece, block_start, block_size, 1), block_size
        )
        value_heads = split_heads(
            lax.dynamic_slice_in_dim(value_piece, block_start, block_size, 1), block_size
        )
        key_ids = lax.dynamic_slice_in_dim(segments, block_start, block_size, 1)
        scores = masked_scores(query_heads, key_heads, own_ids, key_ids, score_scale)
        newest = jnp.maximum(running_max, jnp.max(scores, -1))
        factor = jnp.exp(running_max - newest)
        weights = jnp.exp(scores - newest[..., None])
        running_sum = running_sum * factor + jnp.sum(weights, -1)
        update = jnp.einsum(
            "rhqk,rkhd->rhqd",
            weights.astype(jnp.bfloat16),
            value_heads,
            preferred_element_type=jnp.float32,
        )
        return (newest, running_sum, running_acc * factor[..., None] + update)

    running_max, running_sum, running_acc = lax.fori_loop(
        0, key_piece.shape[1] // block_size, key_step, initial
    )
    context_heads = jnp.transpose(running_acc / running_sum[..., None], (0, 2, 1, 3))
    log_total = jnp.transpose(running_max + jnp.log(running_sum), (0, 2, 1))
    context_low = context_heads.reshape(row_count * local_tokens, model_width).astype(jnp.bfloat16)
    first_sum = flat_tokens.astype(jnp.float32) + (plain_dot(context_low, out_weight) + out_bias)
    hidden, first_back = jax.vjp(norm_rows, first_sum, first_gain, first_shift)
    hidden_low = hidden.astype(jnp.bfloat16)
    pre_act = plain_dot(hidden_low, up_weight) + up_bias
    activated, act_back = jax.vjp(gelu_exact, pre_act)
    act_low = activated.astype(jnp.bfloat16)
    second_sum = hidden + (plain_dot(act_low, down_weight) + down_bias)
    normed, second_back = jax.vjp(norm_rows, second_sum, second_gain, second_shift)
    kept_rows = (keep_flags != 0)[:, None, None]
    layer_out = jnp.where(kept_rows, normed.reshape(row_shape), tokens.astype(jnp.float32)).astype(
        jnp.bfloat16
    )
    grad_out = jnp.where(kept_rows, cotangent.astype(jnp.float32), 0.0).reshape(
        row_count * local_tokens, model_width
    )
    grad_second, grad_second_gain, grad_second_shift = second_back(grad_out)
    grad_branch_low = grad_second.astype(jnp.bfloat16)
    grad_down_bias = token_sum(grad_branch_low)
    grad_down_weight = left_dot(act_low, grad_branch_low)
    (grad_pre,) = act_back(right_dot(grad_branch_low, down_weight))
    grad_pre_low = grad_pre.astype(jnp.bfloat16)
    grad_up_bias = token_sum(grad_pre_low)
    grad_up_weight = left_dot(hidden_low, grad_pre_low)
    grad_hidden = grad_second + right_dot(grad_pre_low, up_weight)
    grad_first, grad_first_gain, grad_first_shift = first_back(grad_hidden)
    grad_attn_low = grad_first.astype(jnp.bfloat16)
    grad_out_bias = token_sum(grad_attn_low)
    grad_out_weight = left_dot(context_low, grad_attn_low)
    late_grads = (
        grad_out_weight,
        grad_out_bias,
        grad_first_gain,
        grad_first_shift,
        grad_up_weight,
        grad_up_bias,
        grad_down_weight,
        grad_down_bias,
        grad_second_gain,
        grad_second_shift,
    )
    grad_context_low = right_dot(grad_attn_low, out_weight).astype(jnp.bfloat16)
    grad_context_rows = grad_context_low.reshape(row_shape)
    grad_heads = split_heads(grad_context_rows, local_tokens)
    spread = jnp.sum(grad_heads.astype(jnp.float32) * context_heads, -1)
    zero_local = jnp.zeros((row_count, local_tokens, HEADS, head_width), jnp.float32)
    zero_whole = jnp.zeros(
        (row_count, local_tokens * lax.axis_size("seq"), HEADS, head_width), jnp.float32
    )
    gathered_total, gathered_spread = (
        lax.all_gather(log_total, "seq", axis=1, tiled=True),
        lax.all_gather(spread, "seq", axis=1, tiled=True),
    )
    key_heads_local = split_heads(key_low, local_tokens)
    value_heads_local = split_heads(value_low, local_tokens)
    query_piece = lax.all_gather(query_low, "seq", axis=1, tiled=True)
    grad_piece = lax.all_gather(grad_context_rows, "seq", axis=1, tiled=True)
    back_block_size = block_length(query_piece.shape[1], local_tokens)

    def query_step(position, inner_state):
        grad_key, grad_value, queries_whole = inner_state
        block_start = position * back_block_size
        part_query, part_key, part_value = split_attend_back(
            split_heads(
                lax.dynamic_slice_in_dim(query_piece, block_start, back_block_size, 1),
                back_block_size,
            ),
            split_heads(
                lax.dynamic_slice_in_dim(grad_piece, block_start, back_block_size, 1),
                back_block_size,
            ),
            lax.dynamic_slice_in_dim(gathered_total, block_start, back_block_size, 1),
            lax.dynamic_slice_in_dim(gathered_spread, block_start, back_block_size, 1),
            lax.dynamic_slice_in_dim(segments, block_start, back_block_size, 1),
            key_heads_local,
            value_heads_local,
            own_ids,
            score_scale,
        )
        return (
            grad_key + part_key,
            grad_value + part_value,
            add_into(queries_whole, part_query, block_start),
        )

    grad_key, grad_value, queries_whole = lax.fori_loop(
        0, query_piece.shape[1] // back_block_size, query_step, (zero_local, zero_local, zero_whole)
    )
    grad_query = lax.psum_scatter(queries_whole, "seq", scatter_dimension=1, tiled=True)
    flat_shape = (row_count * local_tokens, model_width)
    grad_query_low = grad_query.reshape(flat_shape).astype(jnp.bfloat16)
    grad_key_low = grad_key.reshape(flat_shape).astype(jnp.bfloat16)
    grad_value_low = grad_value.reshape(flat_shape).astype(jnp.bfloat16)
    grad_query_bias = token_sum(grad_query_low)
    grad_query_weight = left_dot(flat_tokens, grad_query_low)
    grad_key_weight = left_dot(flat_tokens, grad_key_low)
    grad_value_bias = token_sum(grad_value_low)
    grad_value_weight = left_dot(flat_tokens, grad_value_low)
    grad_flat = (
        grad_first
        + right_dot(grad_query_low, query_weight)
        + right_dot(grad_key_low, key_weight)
        + right_dot(grad_value_low, value_weight)
    )
    tokens_grad = jnp.where(
        kept_rows, grad_flat.reshape(row_shape), cotangent.astype(jnp.float32)
    ).astype(jnp.bfloat16)
    early_grads = (
        grad_query_weight,
        grad_query_bias,
        grad_key_weight,
        grad_value_weight,
        grad_value_bias,
    )
    summed = lax.psum(
        (
            grad_query_weight,
            grad_query_bias,
            grad_key_weight,
            grad_value_weight,
            grad_value_bias,
            grad_out_weight,
            grad_out_bias,
            grad_first_gain,
            grad_first_shift,
            grad_up_weight,
            grad_up_bias,
            grad_down_weight,
            grad_down_bias,
            grad_second_gain,
            grad_second_shift,
        ),
        ("dp", "seq"),
    )
    early_grads = summed[:5]
    late_grads = summed[5:]
    return (
        layer_out,
        tokens_grad,
        early_grads[0],
        early_grads[1],
        early_grads[2],
        early_grads[3],
        early_grads[4],
        late_grads[0],
        late_grads[1],
        late_grads[2],
        late_grads[3],
        late_grads[4],
        late_grads[5],
        late_grads[6],
        late_grads[7],
        late_grads[8],
        late_grads[9],
    )


def deal_rows(
    tokens,
    segments,
    keep_flags,
    query_weight,
    query_bias,
    key_weight,
    value_weight,
    value_bias,
    out_weight,
    out_bias,
    first_gain,
    first_shift,
    up_weight,
    up_bias,
    down_weight,
    down_bias,
    second_gain,
    second_shift,
    cotangent,
):
    row_count, local_tokens, model = tokens.shape
    ring = lax.axis_size("seq")
    me = lax.axis_index("seq")
    rows = row_count // ring
    first_row = me * rows
    turns = [[(i, (i + turn) % ring) for i in range(ring)] for turn in range(ring)]
    back_turns = [[(i, (i - turn) % ring) for i in range(ring)] for turn in range(ring)]

    line = lambda vector: vector.reshape(1, -1)
    forward_weights = (
        query_weight,
        line(query_bias),
        key_weight,
        value_weight,
        line(value_bias),
    )
    firsts = jnp.stack([lax.rem(me + turn, ring) * rows for turn in range(ring)])
    sends, projected = prepare(firsts, rows, tokens, cotangent, forward_weights)

    def fetch(part, turn):
        return lax.ppermute(part, "seq", turns[turn])

    first = [
        fetch(lax.dynamic_slice_in_dim(tokens, firsts[turn], 1, 0), turn)
        for turn in range(1, ring)
    ]
    first, sends, projected = after((first, sends, projected))
    remote, remote_cotangent, before = [first], [], first
    for row in range(rows):
        for index, fetched in ((row, remote), (rows + row, remote_cotangent)):
            if index:
                parts = [after(sends[turn][index - 1], before) for turn in range(ring - 1)]
                fetched.append([fetch(part, turn + 1) for turn, part in enumerate(parts)])
        before = remote[row]
    own_segments = lax.dynamic_slice_in_dim(segments, first_row, rows, 0)
    own_segments = jnp.concatenate(
        [
            lax.dynamic_slice_in_dim(
                own_segments, lax.rem(me - turn + ring, ring) * local_tokens, local_tokens, 1
            )
            for turn in range(ring)
        ],
        1,
    )
    extra_index = jnp.arange(EXTRA, dtype=jnp.int32)[None, :, None]
    same = own_segments[:, None, :] == extra_index
    query_extra = jnp.where(same & (extra_index < 3), 1.0, 0.0)
    key_extra = jnp.where(
        extra_index < 3, jnp.where(same, 0.0, NEG_FILL), jnp.where(extra_index < 6, 1.0, 0.0)
    )
    keep = lax.dynamic_slice_in_dim(keep_flags, first_row, rows, 0)
    token_weights = (
        out_weight,
        line(out_bias),
        line(first_gain),
        line(first_shift),
        up_weight,
        line(up_bias),
        down_weight,
        line(down_bias),
        line(second_gain),
        line(second_shift),
    )
    back_weights = (query_weight, key_weight, value_weight)
    row_index = [(first_row + row).reshape(1) for row in range(rows)]
    sums = Sums()
    number, slots = sums.me.reshape(1), sums.devices
    early_number = sums.me_near.reshape(1)
    heads, contexts = [], []
    remote[0] = after(remote[0], query_extra, key_extra, keep, number, early_number)
    for row in range(rows):
        if row:
            remote[row] = after(remote[row], contexts[-1])
        query, key, value, context = attend(
            row, projected, remote[row], query_extra[row], key_extra[row], forward_weights
        )
        heads.append((query, key, value))
        contexts.append(context)
    remote_cotangent = after(remote_cotangent, contexts[-1])
    results = by_token(
        row_index[0],
        keep,
        number,
        tokens,
        remote,
        cotangent,
        remote_cotangent,
        contexts,
        token_weights,
        slots,
    )
    layer_outs = [results[row * ring : (row + 1) * ring] for row in range(rows)]
    results = results[rows * ring :]
    grad_heads, grad_first, late_near, late_far = results
    def give_back(parts, *before):
        return [
            part if turn == 0 else lax.ppermute(after(part, *before), "seq", back_turns[turn])
            for turn, part in enumerate(parts)
        ]

    def place(moved):
        by_turn = [jnp.concatenate(parts, 0) for parts in zip(*moved)]
        places = [
            [by_turn[(slot - index) % ring] for slot in range(ring)] for index in range(ring)
        ]
        whole = jnp.concatenate(places[0], 0)
        for index in range(1, ring):
            whole = jnp.where(me == index, jnp.concatenate(places[index], 0), whole)
        return whole

    parts = 2
    last = rows * parts - 1
    totals, biases = [None] * parts, [None] * parts
    tokens_grads = []
    here = early_number
    late = [late_near, sums.swap(late_far, 0, 1)]
    layer_outs = [give_back(parts_) for parts_ in layer_outs]
    for call in range(rows * parts):
        row, part = divmod(call, parts)
        if part == 0:
            grad_tokens = grad_first
        results = attend_back(
            (row, rows, part, parts),
            row_index[row],
            here,
            tokens,
            remote[row],
            (*heads[row], grad_heads),
            grad_tokens,
            back_weights,
            totals,
            biases,
            slots,
            1 if 1 < call < last else 200,
        )
        if part == parts - 1:
            tokens_grads.append(give_back(results[:ring]))
            results = results[ring:]
        else:
            grad_tokens, *results = results
        if call < last:
            totals[part], biases[part] = results
        if call == 0:
            late, layer_outs[0] = after((late, layer_outs[0]), results[0])
            late = sums.add_parts(after(late, layer_outs[0]), 1)
            here = after(early_number, *late)
            late = sums.meet(late, 1)
        if call == last - 1:
            late, layer_outs = after((late, layer_outs), results[0])
            late = sums.add_parts(after(late, layer_outs), 2)
            here = after(early_number, *late)
            late = sums.meet(late, 2)
    late, tokens_grads[:-1] = after((late, tokens_grads[:-1]), results[0])
    early_near, early_far = after(results, late, tokens_grads[:-1])
    early = sums.add_parts([early_near, sums.swap(early_far, 0, 1)], 1)
    late = add_up(late)
    late = [late, *sums.others(late, 2)]
    early, tokens_grads[-1] = after((sums.meet(early, 1), tokens_grads[-1]), late, tokens_grads[-1])
    early = add_up(early)
    late = jnp.concatenate(late, 0)
    late = after(late, early)
    late = [late, *sums.others(late, 1)]
    layer_out, tokens_grad = place(layer_outs), place(tokens_grads)
    early = add_up(after([early, *sums.others(early, 2)], late, layer_out, tokens_grad))
    late = after(late, early)
    late = [*late, *[sums.swap(array, 0, 1) for array in late]]
    early = [early, *sums.others(early, 1)]
    hidden_units = up_weight.shape[1]
    grad_up, grad_down, grad_out_weight, *late_lines = unpack(
        number,
        late,
        [(model, hidden_units), (hidden_units, model), (model, model)],
        model,
        [model] * 7 + [hidden_units],
    )
    early = after(early, late_lines)
    early = [*early, *[sums.swap(array, 0, 1) for array in early]]
    late_vectors = [line.reshape(-1) for line in late_lines]
    early = after(early, late_vectors)
    grad_query, grad_key, grad_value, query_bias_grad = unpack(
        early_number, early, [(model, model)] * 3, model, [model]
    )
    (
        grad_out_bias,
        grad_first_gain,
        grad_first_shift,
        grad_down_bias,
        grad_second_gain,
        grad_second_shift,
        grad_value_bias,
        grad_up_bias,
    ) = late_vectors
    return (
        layer_out,
        tokens_grad,
        grad_query,
        query_bias_grad.reshape(-1),
        grad_key,
        grad_value,
        grad_value_bias,
        grad_out_weight,
        grad_out_bias,
        grad_first_gain,
        grad_first_shift,
        grad_up,
        grad_up_bias,
        grad_down,
        grad_down_bias,
        grad_second_gain,
        grad_second_shift,
    )


def solution(mesh):
    dp, ring = mesh.shape["dp"], mesh.shape["seq"]

    def placed(function, mesh, rows):
        return jax.shard_map(
            function,
            mesh=mesh,
            in_specs=(
                P(rows, "seq", None),
                P(rows, None),
                P(rows),
                *([P()] * 15),
                P(rows, "seq", None),
            ),
            out_specs=(P(rows, "seq", None), P(rows, "seq", None), *([P()] * 15)),
            check_vma=False,
        )

    def layer(tokens, *others):
        row_count, model = tokens.shape[0] // dp, tokens.shape[2]
        powers = dp & (dp - 1) == 0 and ring & (ring - 1) == 0 and dp >= 4
        if not powers or row_count % ring or model % (16 * dp * ring):
            return placed(split_rows, mesh, "dp")(tokens, *others)
        axes = (FAR, MIDDLE, NEAR)
        finer = jax.sharding.Mesh(mesh.devices.reshape(dp // 4, 2, 2, ring), (*axes, SEQ))
        return placed(deal_rows, finer, axes)(tokens, *others)

    return layer
```

```python
import functools
import math

import jax
import jax.numpy as jnp
from jax import lax
from jax.experimental import pallas as pl
from jax.experimental.pallas import tpu as pltpu
from jax.sharding import PartitionSpec as P

HEADS = 8
EXTRA = 16
LANES = 128
LINE_ROWS = 2
NEG_FILL = -1e30
EPSILON = 1e-05
BLOCK_CAP = 512
LOG2E = 1.4426950408889634
LN2 = 0.6931471805599453
MIB = 1 << 20


def dot(left, right, left_dim, right_dim):
    return lax.dot_general(
        left, right, (((left_dim,), (right_dim,)), ((), ())), preferred_element_type=jnp.float32
    )


def three_parts(values):
    high = values.astype(jnp.bfloat16)
    rest = values - high.astype(jnp.float32)
    middle = rest.astype(jnp.bfloat16)
    low = (rest - middle.astype(jnp.float32)).astype(jnp.bfloat16)
    return high.astype(jnp.float32), middle.astype(jnp.float32), low.astype(jnp.float32)


def extra_rows(base, values, first):
    row = lax.broadcasted_iota(jnp.int32, base.shape, 0)
    for offset, part in enumerate(three_parts(values)):
        base = jnp.where(row == first + offset, part, base)
    return base


def upright(line):
    return jnp.broadcast_to(line, (8, line.shape[1])).T[:, :1]


def project(tokens, weights, query_column, value_column, width):
    shape = HEADS, width, tokens.shape[0]
    query = (dot(weights[0], tokens, 0, 1) + query_column) * (LOG2E * width**-0.5)
    yield query.astype(jnp.bfloat16).reshape(shape)
    yield dot(weights[1], tokens, 0, 1).astype(jnp.bfloat16).reshape(shape)
    yield (dot(weights[2], tokens, 0, 1) + value_column).astype(jnp.bfloat16).reshape(shape)


def prepare_kernel(rows, turns, width, firsts_ref, *refs):
    tokens_ref, cotangent_ref, *refs = refs
    weight_refs, refs = refs[:3], refs[3:]
    query_bias, value_bias, *refs = refs
    sends, refs = refs[: turns * (2 * rows - 1)], refs[turns * (2 * rows - 1) :]
    *projected, tokens_scratch, weights_scratch, sems = refs
    copies = [(ref, weights_scratch.at[i]) for i, ref in enumerate(weight_refs)]
    copies += [(tokens_ref.at[firsts_ref[0] + row], tokens_scratch.at[row]) for row in range(rows)]
    needed = len(copies)
    places = [(tokens_ref, row) for row in range(1, rows)]
    places += [(cotangent_ref, row) for row in range(rows)]
    for turn in range(turns):
        for index, (ref, row) in enumerate(places):
            source = ref.at[pl.ds(firsts_ref[1 + turn] + row, 1)]
            copies.append((source, sends[turn * len(places) + index]))
    copies = [
        pltpu.make_async_copy(source, target, sems.at[i])
        for i, (source, target) in enumerate(copies)
    ]
    for copy in copies:
        copy.start()
    for copy in copies[:needed]:
        copy.wait()
    weights = [weights_scratch[i] for i in range(3)]
    columns = upright(query_bias[...]), upright(value_bias[...])
    for row in range(rows):
        results = project(tokens_scratch[row], weights, *columns, width)
        for ref, result in zip(projected, results):
            ref[row] = result
    for copy in copies[needed:]:
        copy.wait()


def prepare(firsts, rows, tokens, cotangent, weights):
    turns = firsts.shape[0] - 1
    local, model = tokens.shape[1:]
    width = model // HEADS
    query_weight, query_bias, key_weight, value_weight, value_bias = weights
    anywhere = pl.BlockSpec(memory_space=pl.ANY)
    whole = lambda array: pl.BlockSpec(array.shape, lambda i, s: (0,) * array.ndim)
    low = lambda *shape: jax.ShapeDtypeStruct(shape, jnp.bfloat16)
    outs = [low(1, local, model)] * (turns * (2 * rows - 1))
    outs += [low(rows, HEADS, width, local)] * 3
    results = pl.pallas_call(
        functools.partial(prepare_kernel, rows, turns, width),
        out_shape=outs,
        grid_spec=pltpu.PrefetchScalarGridSpec(
            num_scalar_prefetch=1,
            grid=(1,),
            in_specs=[*[anywhere] * 5, whole(query_bias), whole(value_bias)],
            out_specs=[whole(a) for a in outs],
            scratch_shapes=[
                pltpu.VMEM((rows, local, model), jnp.bfloat16),
                pltpu.VMEM((3, model, model), jnp.bfloat16),
                pltpu.SemaphoreType.DMA((3 + rows + turns * (2 * rows - 1),)),
            ],
        ),
        compiler_params=pltpu.CompilerParams(vmem_limit_bytes=60 * MIB),
        cost_estimate=pl.CostEstimate(
            flops=2 * 10**10, bytes_accessed=1, transcendentals=0
        ),
        name="prepare",
    )(firsts, tokens, cotangent, query_weight, key_weight, value_weight, query_bias, value_bias)
    count = 2 * rows - 1
    return [results[turn * count : (turn + 1) * count] for turn in range(turns)], results[-3:]


def attend_kernel(row, pieces, width, block, *refs):
    token_refs, refs = refs[: pieces - 1], refs[pieces - 1 :]
    projected, refs = refs[:3], refs[3:]
    (
        query_extra,
        key_extra,
        query_weight,
        query_bias,
        key_weight,
        value_weight,
        value_bias,
        query_out,
        key_out,
        value_out,
        context_out,
        tokens_scratch,
        weights_scratch,
        query_scratch,
        key_scratch,
        value_scratch,
        context_scratch,
        scores_even,
        scores_odd,
        largest_even,
        largest_odd,
        log_totals,
        in_sems,
        out_sems,
        query_sems,
        context_sems,
    ) = refs
    length = query_scratch.shape[2]
    local = length // pieces
    scratches = query_scratch, key_scratch, value_scratch
    incoming = [(ref.at[0], tokens_scratch.at[i]) for i, ref in enumerate(token_refs)]
    weight_refs = query_weight, key_weight, value_weight
    incoming += [(ref, weights_scratch.at[i]) for i, ref in enumerate(weight_refs)]
    incoming += [
        (ref.at[row], scratch.at[:, pl.ds(0, width), pl.ds(0, local)])
        for ref, scratch in zip(projected, scratches)
    ]
    incoming = [
        pltpu.make_async_copy(source, target, in_sems.at[i])
        for i, (source, target) in enumerate(incoming)
    ]
    for copy in incoming:
        copy.start()
    row = lax.broadcasted_iota(jnp.int32, (EXTRA, length), 0)
    ones = (row < 3).astype(jnp.bfloat16)
    query_base = query_extra[...]
    for head in range(HEADS):
        query_scratch[head, width:] = query_base.astype(jnp.bfloat16)
        key_scratch[head, width:] = key_extra[...].astype(jnp.bfloat16)
        value_scratch[head, width:] = ones
    columns = upright(query_bias[...]), upright(value_bias[...])
    for copy in incoming:
        copy.wait()
    weights = [weights_scratch[i] for i in range(3)]
    for piece in range(1, pieces):
        span = pl.ds(piece * local, local)
        results = project(tokens_scratch[piece - 1], weights, *columns, width)
        for scratch, result in zip(scratches, results):
            scratch[:, :width, span] = result
    outgoing = [
        pltpu.make_async_copy(key_scratch, key_out.at[0], out_sems.at[0]),
        pltpu.make_async_copy(value_scratch, value_out.at[0], out_sems.at[1]),
    ]
    for copy in outgoing:
        copy.start()

    def pair_copies(pair):
        heads = pl.ds(pair * 2, 2)
        rows = pl.ds(pl.multiple_of(pair * 2 * width, 2 * width), 2 * width)
        return (
            pltpu.make_async_copy(
                query_scratch.at[heads], query_out.at[0, heads], query_sems.at[pair]
            ),
            pltpu.make_async_copy(
                context_scratch.at[rows], context_out.at[rows], context_sems.at[pair]
            ),
        )

    def score(head, scores_ref, largest_ref, start):
        span = pl.ds(start, block)
        scores = dot(key_scratch[head], query_scratch[head, :, span], 0, 0)
        scores_ref[:, span] = scores
        largest_ref[:, span] = jnp.max(scores, 0, keepdims=True)

    def weigh(head, scores_ref, largest_ref, start):
        span = pl.ds(start, block)
        largest = largest_ref[:, span]
        weights = jnp.exp2(scores_ref[:, span] - largest).astype(jnp.bfloat16)
        update = dot(value_scratch[head], weights, 1, 0)
        total = update[width : width + 1]
        context_scratch[pl.ds(pl.multiple_of(head * width, width), width), span] = (
            update[:width] / total
        )
        log_totals[pl.ds(head, 1), span] = largest + jnp.log(total) * LOG2E

    starts = range(0, length, block)
    for start in starts:
        score(0, scores_even, largest_even, start)

    def head_pair(pair, carry):
        head = pair * 2
        for start in starts:
            score(head + 1, scores_odd, largest_odd, start)
            weigh(head, scores_even, largest_even, start)
        following = jnp.minimum(head + 2, HEADS - 1)
        for start in starts:
            score(following, scores_even, largest_even, start)
            weigh(head + 1, scores_odd, largest_odd, start)
        for side in range(2):
            log_total = log_totals[pl.ds(head + side, 1), :]
            query_scratch[head + side, width:] = extra_rows(query_base, -log_total, 3).astype(
                jnp.bfloat16
            )
        for copy in pair_copies(pair):
            copy.start()
        return carry

    lax.fori_loop(0, HEADS // 2, head_pair, 0)
    for pair in range(HEADS // 2):
        outgoing.extend(pair_copies(pair))
    for copy in outgoing:
        copy.wait()


def attend(row, projected, remote, query_extra, key_extra, weights):
    pieces = 1 + len(remote)
    _, heads, width, local = projected[0].shape
    model = heads * width
    length = pieces * local
    whole = lambda array: pl.BlockSpec(array.shape, lambda i: (0,) * array.ndim)
    anywhere = pl.BlockSpec(memory_space=pl.ANY)
    low = jax.ShapeDtypeStruct((1, HEADS, width + EXTRA, length), jnp.bfloat16)
    outs = (low, low, low, jax.ShapeDtypeStruct((model, length), jnp.float32))
    query_weight, query_bias, key_weight, value_weight, value_bias = weights
    head_scratch = pltpu.VMEM(low.shape[1:], jnp.bfloat16)
    return pl.pallas_call(
        functools.partial(attend_kernel, row, pieces, width, min(256, length)),
        out_shape=outs,
        grid_spec=pltpu.PrefetchScalarGridSpec(
            num_scalar_prefetch=0,
            grid=(1,),
            in_specs=[
                *[anywhere] * (pieces + 2),
                whole(query_extra),
                whole(key_extra),
                anywhere,
                whole(query_bias),
                anywhere,
                anywhere,
                whole(value_bias),
            ],
            out_specs=[anywhere] * 4,
            scratch_shapes=[
                pltpu.VMEM((max(pieces - 1, 1), local, model), jnp.bfloat16),
                pltpu.VMEM((3, model, model), jnp.bfloat16),
                head_scratch,
                head_scratch,
                head_scratch,
                pltpu.VMEM((model, length), jnp.float32),
                pltpu.VMEM((length, length), jnp.float32),
                pltpu.VMEM((length, length), jnp.float32),
                pltpu.VMEM((1, length), jnp.float32),
                pltpu.VMEM((1, length), jnp.float32),
                pltpu.VMEM((HEADS, length), jnp.float32),
                pltpu.SemaphoreType.DMA((5 + pieces,)),
                pltpu.SemaphoreType.DMA((2,)),
                pltpu.SemaphoreType.DMA((HEADS // 2,)),
                pltpu.SemaphoreType.DMA((HEADS // 2,)),
            ],
        ),
        compiler_params=pltpu.CompilerParams(vmem_limit_bytes=60 * MIB),
        cost_estimate=pl.CostEstimate(
            flops=3 * 10**9, bytes_accessed=1, transcendentals=0
        ),
        name="attend",
    )(*remote, *projected, query_extra, key_extra, *weights)


def row_mean(values):
    return jnp.mean(values, -1, keepdims=True)


def normalise(values):
    centred = values - row_mean(values)
    scale = lax.rsqrt(row_mean(centred * centred) + EPSILON)
    return centred * scale, scale


def norm_back(grad, gain, normed, scale):
    entering = grad * gain
    return (entering - row_mean(entering) - normed * row_mean(entering * normed)) * scale


def column_sum(values):
    return jnp.sum(values, 0, keepdims=True)


def gelu_parts(values):
    phi = 0.5 + 0.5 * lax.erf(values * 0.5**0.5)
    bell = jnp.exp2(values * values * (-0.5 * LOG2E))
    return values * phi, phi + values * bell * 0.3989422804014327


def token_kernel(rows, pieces, steps, width, *refs):
    _, keep_ref, me_ref, refs = *refs[:3], refs[3:]
    own_tokens, own_cotangent, refs = *refs[:2], refs[2:]
    remote_count = rows * (pieces - 1)
    remote_tokens, refs = refs[:remote_count], refs[remote_count:]
    remote_cotangents, refs = refs[:remote_count], refs[remote_count:]
    context_refs, refs = refs[:rows], refs[rows:]
    (
        out_weight,
        out_bias,
        first_gain,
        first_shift,
        up_weight,
        up_bias,
        down_weight,
        down_bias,
        second_gain,
        second_shift,
    ) = refs[:10]
    refs = refs[10:]
    layer_outs, refs = refs[: rows * pieces], refs[rows * pieces :]
    (
        grad_out_heads,
        grad_first_out,
        near_out,
        far_out,
        up_scratch,
        down_scratch,
        result_scratch,
        packed_near,
        packed_far,
        sems,
        tokens_scratch,
        cotangent_scratch,
        context_scratch,
        act_scratch,
        slope_scratch,
        totals,
        lines,
        *line_sums,
    ) = refs
    (
        grad_out_bias,
        grad_first_gain,
        grad_first_shift,
        grad_down_bias,
        grad_second_gain,
        grad_second_shift,
        grad_value_bias,
        grad_up_bias,
    ) = line_sums
    row_index = pl.program_id(0)
    piece_index = pl.program_id(1)
    step_index = pl.program_id(2)
    tokens_len, model = tokens_scratch.shape
    hidden_units = up_weight.shape[1]
    kept = keep_ref[row_index] != 0
    span = pl.ds(pl.multiple_of(step_index * tokens_len, tokens_len), tokens_len)

    @pl.when(piece_index == 0)
    def _():
        tokens_scratch[...] = own_tokens[0, span]
        cotangent_scratch[...] = own_cotangent[0, span]

    first_step = (row_index == 0) & (piece_index == 0) & (step_index == 0)
    last_step = (row_index == rows - 1) & (piece_index == pieces - 1) & (step_index == steps - 1)
    fetches = [
        pltpu.make_async_copy(up_weight, up_scratch, sems.at[0]),
        pltpu.make_async_copy(down_weight, down_scratch, sems.at[1]),
    ]

    @pl.when(first_step)
    def _():
        for copy in fetches:
            copy.start()

    for row in range(rows):

        @pl.when(row_index == row)
        def _():
            context_scratch[...] = context_refs[row][...]

        for piece in range(1, pieces):

            @pl.when((row_index == row) & (piece_index == piece))
            def _():
                position = row * (pieces - 1) + piece - 1
                tokens_scratch[...] = remote_tokens[position][0, span]
                cotangent_scratch[...] = remote_cotangents[position][0, span]

    @pl.when(first_step)
    def _():
        for ref in (totals, lines, *line_sums):
            ref[...] = jnp.zeros(ref.shape, ref.dtype)

    tokens = tokens_scratch[...].astype(jnp.float32)
    context = context_scratch[...]
    context_low = context.astype(jnp.bfloat16)
    first_sum = tokens + (dot(context_low, out_weight[...], 0, 0) + out_bias[...])
    first_normed, first_scale = normalise(first_sum)
    hidden = first_normed * first_gain[...] + first_shift[...]
    hidden_low = hidden.astype(jnp.bfloat16)

    @pl.when(first_step)
    def _():
        for copy in fetches:
            copy.wait()

    pre_act = dot(hidden_low, up_scratch[...], 1, 0) + up_bias[...]
    activated, slope = gelu_parts(pre_act)
    act_low = activated.astype(jnp.bfloat16)
    act_scratch[...] = act_low
    slope_scratch[...] = slope
    branch = dot(act_low, down_scratch[...], 1, 0) + down_bias[...]
    second_normed, second_scale = normalise(hidden + branch)
    result = jnp.where(
        kept, second_normed * second_gain[...] + second_shift[...], tokens
    ).astype(jnp.bfloat16)
    gives = [
        pltpu.make_async_copy(result_scratch, ref.at[0, span], sems.at[2]) for ref in layer_outs
    ]

    @pl.when(jnp.logical_not(first_step))
    def _():
        gives[0].wait()

    result_scratch[...] = result
    for position, copy in enumerate(gives):

        @pl.when(row_index * pieces + piece_index == position)
        def _():
            copy.start()

    cotangent = cotangent_scratch[...].astype(jnp.float32)
    grad_out = jnp.where(kept, cotangent, 0.0)
    grad_second_gain[...] += column_sum(grad_out * second_normed)
    grad_second_shift[...] += column_sum(grad_out)
    grad_second = norm_back(grad_out, second_gain[...], second_normed, second_scale)
    grad_branch_low = grad_second.astype(jnp.bfloat16)
    grad_down_bias[...] += column_sum(grad_branch_low.astype(jnp.float32))
    grad_act = dot(grad_branch_low, down_scratch[...], 1, 1)
    grad_pre_low = (grad_act * slope_scratch[...]).astype(jnp.bfloat16)
    grad_hidden = grad_second + dot(grad_pre_low, up_scratch[...], 1, 1)
    totals[pl.ds(hidden_units, hidden_units), :] += dot(act_scratch[...], grad_branch_low, 0, 0)
    for start in range(0, hidden_units, model):
        totals[pl.ds(start, model), :] += dot(
            hidden_low, grad_pre_low[:, start : start + model], 0, 0
        )
    grad_up_bias[...] += column_sum(grad_pre_low.astype(jnp.float32))
    grad_first_gain[...] += column_sum(grad_hidden * first_normed)
    grad_first_shift[...] += column_sum(grad_hidden)
    grad_first = norm_back(grad_hidden, first_gain[...], first_normed, first_scale)
    grad_first_out[0] = jnp.where(kept, grad_first, cotangent)
    grad_attn_low = grad_first.astype(jnp.bfloat16)
    grad_out_bias[...] += column_sum(grad_attn_low.astype(jnp.float32))
    totals[pl.ds(2 * hidden_units, model), :] += dot(context_low, grad_attn_low, 1, 0)
    grad_context = dot(out_weight[...], grad_attn_low, 1, 1).astype(jnp.bfloat16)
    grad_context_wide = grad_context.astype(jnp.float32)
    ones = jnp.ones((EXTRA, tokens_len), jnp.bfloat16)
    grad_value_bias[...] += dot(ones, grad_context, 1, 1)[:1]
    product = grad_context_wide * context
    blank = jnp.zeros((EXTRA, tokens_len), jnp.float32)
    for head in range(HEADS):
        columns = slice(head * width, (head + 1) * width)
        grad_out_heads[0, head, :width] = grad_context[columns]
        spread = jnp.sum(product[columns], 0, keepdims=True)
        grad_out_heads[0, head, width:] = extra_rows(blank, -spread, 0).astype(jnp.bfloat16)

    @pl.when(last_step)
    def _():
        first = 0
        for ref in line_sums:
            set_lines(lines, first, ref[...])
            first += ref.shape[1] // LANES
        copies = [gives[0]]
        for half, out, sem in ((packed_far, far_out, 0), (packed_near, near_out, 1)):
            pack([totals], lines, *((None, half) if sem == 0 else (half, None)), me_ref[0])
            copies.append(pltpu.make_async_copy(half, out, sems.at[sem]))
            copies[-1].start()
        for copy in copies:
            copy.wait()


def set_lines(lines, first, values):
    width = lines.shape[2]
    for block in range(values.shape[1] // width):
        slot, row = divmod(first + block, LINE_ROWS)
        lines[slot, row : row + 1] = values[:, block * width : (block + 1) * width]


def pack(parts, lines, near, far, me):
    half, size, width = (near if far is None else far).shape
    columns = [(ref, start) for ref in parts for start in range(0, ref.shape[1], width)]
    height = parts[0].shape[0] // (2 * half)

    def one(slot, carry):
        for ref, first in ((near, 0), (far, half)):
            if ref is None:
                continue
            piece = (slot + first) ^ me
            rows = pl.ds(pl.multiple_of(piece * height, EXTRA), height)
            for block, (source, start) in enumerate(columns):
                ref[slot, pl.ds(block * height, height), :] = source[
                    rows, pl.ds(start, width)
                ].astype(jnp.bfloat16)
            ref[slot, pl.ds(len(columns) * height, EXTRA), :] = jnp.concatenate(
                [lines[piece], jnp.zeros_like(lines[piece])], 0
            ).astype(jnp.bfloat16)
        return carry

    lax.fori_loop(0, half, one, 0)


def packed_shape(slots, rows, model):
    return jax.ShapeDtypeStruct(
        (slots // 2, rows * (model // LANES) // slots + EXTRA, LANES), jnp.bfloat16
    )


def lines_shape(slots):
    return pltpu.VMEM((slots, EXTRA // 2, LANES), jnp.float32)


def by_token(
    row_index, keep, me, tokens, remote, cotangent, remote_cotangent, contexts, weights, slots
):
    rows = len(contexts)
    pieces = 1 + len(remote[0])
    local, model = tokens.shape[1:]
    length = pieces * local
    width = model // HEADS
    hidden_units = weights[4].shape[1]
    tokens_len = min(512, local)
    steps = local // tokens_len
    whole = lambda array: pl.BlockSpec(array.shape, lambda r, i, j, s, k, m: (0,) * array.ndim)
    own_spec = pl.BlockSpec((1, local, model), lambda r, i, j, s, k, m: (s[0] + r, 0, 0))
    f32 = lambda *shape: jax.ShapeDtypeStruct(shape, jnp.float32)
    anywhere = pl.BlockSpec(memory_space=pl.ANY)
    total_rows = 2 * hidden_units + model
    packed = packed_shape(slots, total_rows, model)
    piece_out = jax.ShapeDtypeStruct((1, local, model), jnp.bfloat16)
    gradient_outs = (packed, packed)
    line_lengths = [model] * 7 + [hidden_units]
    outs = (
        *([piece_out] * (rows * pieces)),
        jax.ShapeDtypeStruct((rows, HEADS, width + EXTRA, length), jnp.bfloat16),
        f32(rows, length, model),
        *gradient_outs,
    )
    out_specs = (
        *([anywhere] * (rows * pieces)),
        pl.BlockSpec(
            (1, HEADS, width + EXTRA, tokens_len),
            lambda r, i, j, s, k, m: (r, 0, 0, i * steps + j),
        ),
        pl.BlockSpec((1, tokens_len, model), lambda r, i, j, s, k, m: (r, i * steps + j, 0)),
        anywhere,
        anywhere,
    )

    def context_spec(row):
        def block(r, i, j, s, k, m):
            step = i * steps + j
            return 0, jnp.where(r < row, 0, jnp.where(r > row, pieces * steps - 1, step))

        return pl.BlockSpec((model, tokens_len), block)

    flat_remote = [array for arrays in remote for array in arrays]
    flat_remote_cotangent = [array for arrays in remote_cotangent for array in arrays]
    in_specs = (
        own_spec,
        own_spec,
        *[whole(a) for a in (*flat_remote, *flat_remote_cotangent)],
        *[context_spec(row) for row in range(rows)],
        *[anywhere if a.shape[0] * a.shape[1] > model * model else whole(a) for a in weights],
    )
    return pl.pallas_call(
        functools.partial(token_kernel, rows, pieces, steps, width),
        out_shape=outs,
        grid_spec=pltpu.PrefetchScalarGridSpec(
            num_scalar_prefetch=3,
            grid=(rows, pieces, steps),
            in_specs=in_specs,
            out_specs=out_specs,
            scratch_shapes=[
                pltpu.VMEM((model, hidden_units), jnp.bfloat16),
                pltpu.VMEM((hidden_units, model), jnp.bfloat16),
                pltpu.VMEM((tokens_len, model), jnp.bfloat16),
                pltpu.VMEM(packed.shape, jnp.bfloat16),
                pltpu.VMEM(packed.shape, jnp.bfloat16),
                pltpu.SemaphoreType.DMA((3,)),
                pltpu.VMEM((tokens_len, model), jnp.bfloat16),
                pltpu.VMEM((tokens_len, model), jnp.bfloat16),
                pltpu.VMEM((model, tokens_len), jnp.float32),
                pltpu.VMEM((tokens_len, hidden_units), jnp.bfloat16),
                pltpu.VMEM((tokens_len, hidden_units), jnp.float32),
                pltpu.VMEM((total_rows, model), jnp.float32),
                lines_shape(slots),
                *[pltpu.VMEM((1, n), jnp.float32) for n in line_lengths],
            ],
        ),
        compiler_params=pltpu.CompilerParams(vmem_limit_bytes=60 * MIB),
        cost_estimate=pl.CostEstimate(flops=1, bytes_accessed=1, transcendentals=0),
        name="by_token",
    )(
        row_index,
        keep,
        me,
        tokens,
        cotangent,
        *flat_remote,
        *flat_remote_cotangent,
        *contexts,
        *weights,
    )


def attend_back_kernel(pieces, width, block, place, *refs):
    row, rows, part, parts = place
    first_row, last_part = row == 0, part == parts - 1
    packing = row == rows - 1 and last_part
    row_ref, me_ref, refs = *refs[:2], refs[2:]
    token_refs, refs = refs[:pieces], refs[pieces:]
    head_refs, refs = refs[:4], refs[4:]
    grad_tokens_in, *weight_refs, refs = *refs[:4], refs[4:]
    if not first_row:
        totals_in, bias_in, refs = *refs[:2], refs[2:]
    earlier = part if packing else 0
    earlier_totals, refs = refs[:earlier], refs[earlier:]
    earlier_biases, refs = refs[:earlier], refs[earlier:]
    outs = pieces if last_part else 1
    grad_tokens, refs = refs[:outs], refs[outs:]
    if packing:
        packed_near, packed_far, *refs = refs
    else:
        totals_out, bias, *refs = refs
    (
        grad_query_scratch,
        grad_key_scratch,
        grad_value_scratch,
        tokens_scratch,
        grad_scratch,
        weights_scratch,
        totals,
        sems,
        *refs,
    ) = refs
    if packing:
        lines, bias, *earlier_scratch = refs
    query_ref, key_ref, value_ref, grad_ref = (ref.at[0] for ref in head_refs)
    pair = pl.program_id(0)
    pairs = pl.num_programs(0)
    length = query_ref.shape[2]
    local = length // pieces
    model, columns = weights_scratch.shape[1:]
    pair_width = 2 * width
    share = pl.ds(part * columns, columns)
    incoming = [(token_refs[0].at[row_ref[0]], tokens_scratch.at[0])]
    incoming += [(ref.at[0], tokens_scratch.at[i + 1]) for i, ref in enumerate(token_refs[1:])]
    incoming.append((grad_tokens_in.at[row if part == 0 else 0], grad_scratch))
    incoming += [(ref.at[:, share], weights_scratch.at[i]) for i, ref in enumerate(weight_refs)]
    if not first_row:
        incoming.append((totals_in, totals))
    if packing:
        incoming += list(zip(earlier_totals, earlier_scratch))
    incoming = [
        pltpu.make_async_copy(source, target, sems.at[i])
        for i, (source, target) in enumerate(incoming)
    ]

    @pl.when(pair == 0)
    def _():
        for copy in incoming:
            copy.start()

    grad_queries = [[], []]
    for side in range(2):
        key = key_ref[side]
        value = value_ref[side]
        grad_key = 0.0
        grad_value = 0.0
        for start in range(0, length, block):
            span = pl.ds(start, block)
            query = query_ref[side, :, span]
            grad = grad_ref[side, :, span]
            weights = jnp.exp2(dot(query, key, 0, 0))
            grad_weights = dot(grad, value, 0, 0)
            weights_low = weights.astype(jnp.bfloat16)
            grad_scores = (weights * grad_weights).astype(jnp.bfloat16)
            grad_value = grad_value + dot(grad[:width], weights_low, 1, 0)
            grad_key = grad_key + dot(query[:width], grad_scores, 1, 0)
            grad_queries[side].append(dot(grad_scores, key[:width], 1, 1))
        head = pl.ds(pl.multiple_of(pair * pair_width + side * width, width), width)
        grad_value_scratch[head, :] = grad_value.astype(jnp.bfloat16)
        grad_key_scratch[head, :] = (grad_key * LN2).astype(jnp.bfloat16)
    for index, start in enumerate(range(0, length, block)):
        both = jnp.concatenate([grad_queries[0][index], grad_queries[1][index]], 1)
        grad_query_scratch[pair, pl.ds(start, block)] = (both * width**-0.5).astype(jnp.bfloat16)

    @pl.when(pair == pairs - 1)
    def _():
        for copy in incoming:
            copy.wait()
        count = grad_query_scratch.shape[0]
        for index in range(count):
            lanes = pl.ds(index * pair_width, pair_width)
            total = column_sum(grad_query_scratch[index].astype(jnp.float32))
            bias[:, lanes] = total if first_row else bias_in[:, lanes] + total
        grad_query = jnp.concatenate([grad_query_scratch[index] for index in range(count)], 1)
        outgoing = []
        for position in range(3):
            lines_of = pl.ds(position * model, model)
            term = 0.0
            for piece in range(pieces):
                span = slice(piece * local, (piece + 1) * local)
                tokens = tokens_scratch[piece]
                if position == 0:
                    term = term + dot(tokens, grad_query[span], 0, 0)
                else:
                    source = grad_key_scratch if position == 1 else grad_value_scratch
                    term = term + dot(tokens, source[:, span], 0, 1)
            totals[lines_of, :] = term if first_row else totals[lines_of, :] + term
        if not packing:
            outgoing.append(pltpu.make_async_copy(totals, totals_out, sems.at[0]))
            outgoing[0].start()
        for piece in range(pieces):
            span = pl.ds(piece * local, local)
            total = (
                grad_scratch[span]
                + dot(grad_query[piece * local : (piece + 1) * local], weights_scratch[0], 1, 1)
                + dot(grad_key_scratch[:, span], weights_scratch[1], 0, 1)
                + dot(grad_value_scratch[:, span], weights_scratch[2], 0, 1)
            )
            if last_part:
                grad_tokens[piece][0] = total.astype(jnp.bfloat16)
            else:
                grad_scratch[span] = total
                outgoing.append(
                    pltpu.make_async_copy(
                        grad_scratch.at[span], grad_tokens[0].at[0, span], sems.at[1 + piece]
                    )
                )
                outgoing[-1].start()
        if packing:
            lines[...] = jnp.zeros(lines.shape, lines.dtype)
            first = 0
            for ref in (*earlier_biases, bias):
                set_lines(lines, first, ref[...])
                first += ref.shape[1] // LANES
            pack([*earlier_scratch, totals], lines, packed_near, packed_far, me_ref[0])
        for copy in outgoing:
            copy.wait()


def attend_back(
    place, row_index, me, tokens, remote, heads, grad_tokens, weights, totals, biases, slots, gflops
):
    row, rows, part, parts = place
    last_part = part == parts - 1
    packing = row == rows - 1 and last_part
    pieces = 1 + len(remote)
    local, model = tokens.shape[1:]
    length = pieces * local
    width = model // HEADS
    columns = model // parts
    pairs = HEADS // parts // 2
    anywhere = pl.BlockSpec(memory_space=pl.ANY)
    whole = lambda array: pl.BlockSpec(array.shape, lambda i, s, m: (0,) * array.ndim)
    head_spec = lambda array: pl.BlockSpec(
        (1, 2, *array.shape[2:]),
        lambda i, s, m: (row if array.shape[0] > 1 else 0, part * pairs + i, 0, 0),
    )
    f32 = lambda *shape: jax.ShapeDtypeStruct(shape, jnp.float32)
    if last_part:
        outs = [jax.ShapeDtypeStruct((1, local, model), jnp.bfloat16)] * pieces
        out_specs = [whole(a) for a in outs]
    else:
        outs, out_specs = [f32(1, length, model)], [anywhere]
    total, bias = f32(3 * model, columns), f32(1, columns)
    in_specs = [anywhere] * pieces + [head_spec(a) for a in heads] + [anywhere] * 4
    operands = [tokens, *remote, *heads, grad_tokens, *weights]
    if row:
        operands += [totals[part], biases[part]]
        in_specs += [anywhere, whole(bias)]
    scratch = [
        pltpu.VMEM((pairs, length, 2 * width), jnp.bfloat16),
        pltpu.VMEM((columns, length), jnp.bfloat16),
        pltpu.VMEM((columns, length), jnp.bfloat16),
        pltpu.VMEM((pieces, local, model), jnp.bfloat16),
        pltpu.VMEM((length, model), jnp.float32),
        pltpu.VMEM((3, model, columns), jnp.bfloat16),
        pltpu.VMEM(total.shape, jnp.float32),
        pltpu.SemaphoreType.DMA((pieces + 5 + parts,)),
    ]
    if packing:
        operands += [*totals[:part], *biases[:part]]
        in_specs += [anywhere] * part + [whole(bias)] * part
        packed = packed_shape(slots, 3 * model, model)
        outs += [packed] * 2
        out_specs += [whole(packed)] * 2
        scratch += [lines_shape(slots), pltpu.VMEM(bias.shape, jnp.float32)]
        scratch += [pltpu.VMEM(total.shape, jnp.float32)] * part
    else:
        outs += [total, bias]
        out_specs += [anywhere, whole(bias)]
    return pl.pallas_call(
        functools.partial(attend_back_kernel, pieces, width, min(256, length), place),
        out_shape=outs,
        grid_spec=pltpu.PrefetchScalarGridSpec(
            num_scalar_prefetch=2,
            grid=(pairs,),
            in_specs=in_specs,
            out_specs=out_specs,
            scratch_shapes=scratch,
        ),
        compiler_params=pltpu.CompilerParams(vmem_limit_bytes=60 * MIB),
        cost_estimate=pl.CostEstimate(
            flops=gflops * 10**9, bytes_accessed=1, transcendentals=0
        ),
        name="attend_back",
    )(row_index, me, *operands)


def unpack_kernel(moves, model, counts, me_ref, *refs):
    sources, refs = refs[: counts[0]], refs[counts[0] :]
    outs, refs = refs[: counts[1]], refs[counts[1] :]
    lines, refs = refs[: counts[2]], refs[counts[2] :]
    *blocks_out, slots, in_sems, out_sems = refs
    count = counts[0]
    _, size, width = slots.shape
    me = me_ref[0]
    share = slots.shape[0] // count
    copies = [
        pltpu.make_async_copy(source, slots.at[pl.ds(index * share, share)], in_sems.at[index])
        for index, source in enumerate(sources)
    ]
    for copy in copies:
        copy.start()
    for copy in copies:
        copy.wait()
    index = 0
    for line in lines:
        for block in range(line.shape[1] // width):
            piece, row = divmod(index, LINE_ROWS)
            extra = slots[piece ^ me, pl.ds(size - EXTRA, EXTRA), :].astype(jnp.float32)
            line[:, pl.ds(block * width, width)] = extra[row : row + 1]
            index += 1
    copies = []
    for square, (out, row, column, pieces) in enumerate(moves):
        for piece, start, rows, inside, offset in pieces:
            blocks_out[out][pl.ds(row + inside, rows), pl.ds(column + offset, width)] = slots[
                piece ^ me, pl.ds(start, rows), :
            ].astype(jnp.float32)
        part = pl.ds(row, model), pl.ds(column, model)
        copies.append(
            pltpu.make_async_copy(
                blocks_out[out].at[part], outs[out].at[part], out_sems.at[square]
            )
        )
        copies[-1].start()
    for copy in copies:
        copy.wait()


def unpack(me, arrays, shapes, model, lengths):
    share, size, width = arrays[0].shape
    slots = share * len(arrays)
    blocks = model // width
    height = (size - EXTRA) // blocks
    moves = [
        (out, row, column, [])
        for out, shape in enumerate(shapes)
        for row in range(0, shape[0], model)
        for column in range(0, shape[1], model)
    ]
    for piece in range(slots):
        done = 0
        while done < height:
            square, inside = divmod(piece * height + done, model)
            rows = min(height - done, model - inside)
            for block in range(blocks):
                moves[square][3].append(
                    (piece, block * height + done, rows, inside, block * width)
                )
            done += rows
    outs = [jax.ShapeDtypeStruct(shape, jnp.float32) for shape in shapes]
    lines = [jax.ShapeDtypeStruct((1, n), jnp.float32) for n in lengths]
    anywhere = pl.BlockSpec(memory_space=pl.ANY)
    return pl.pallas_call(
        functools.partial(unpack_kernel, moves, model, (len(arrays), len(outs), len(lines))),
        out_shape=[*outs, *lines],
        grid_spec=pltpu.PrefetchScalarGridSpec(
            num_scalar_prefetch=1,
            grid=(1,),
            in_specs=[anywhere] * len(arrays),
            out_specs=[
                *[anywhere] * len(outs),
                *[pl.BlockSpec(a.shape, lambda i, m: (0, 0)) for a in lines],
            ],
            scratch_shapes=[
                *[pltpu.VMEM(a.shape, jnp.float32) for a in outs],
                pltpu.VMEM((slots, size, width), jnp.bfloat16),
                pltpu.SemaphoreType.DMA((len(arrays),)),
                pltpu.SemaphoreType.DMA((len(moves),)),
            ],
        ),
        compiler_params=pltpu.CompilerParams(vmem_limit_bytes=60 * MIB),
        cost_estimate=pl.CostEstimate(
            flops=2 * 10**10, bytes_accessed=1, transcendentals=0
        ),
        name="unpack",
    )(me, *arrays)


NEAR, MIDDLE, FAR, SEQ = AXES = ("near", "middle", "far", "seq")
STAGES = ((NEAR,), (MIDDLE, SEQ), (FAR,))


def add_up(arrays):
    arrays = [a.astype(jnp.float32) for a in arrays]
    while len(arrays) > 1:
        arrays = [first + second for first, second in zip(arrays[::2], arrays[1::2], strict=True)]
    return arrays[0].astype(jnp.bfloat16)


def after(arrays, *others):
    return lax.optimization_barrier((arrays, others))[0]


class Sums:
    def __init__(self):
        self.sizes = [lax.axis_size(axes) for axes in STAGES]
        self.devices = math.prod(self.sizes)
        digits = [lax.axis_index(axes) for axes in STAGES]
        self.me = (digits[0] * self.sizes[1] + digits[1]) * self.sizes[2] + digits[2]
        self.me_near = self.me - digits[2]

    def swap(self, array, stage, turn):
        pairs = [(i, i ^ turn) for i in range(self.sizes[stage])]
        return lax.ppermute(array, STAGES[stage], pairs)

    def meet(self, parts, stage):
        return [parts[0], *[self.swap(parts[t], stage, t) for t in range(1, len(parts))]]

    def add_parts(self, arrays, stage):
        size = self.sizes[stage]
        share = arrays[0].shape[0] // size
        return [
            add_up([array[turn * share : (turn + 1) * share] for array in arrays])
            for turn in range(size)
        ]

    def others(self, held, stage):
        return [self.swap(held, stage, turn) for turn in range(1, self.sizes[stage])]


def norm_rows(values, gain, shift):
    row_mean = jnp.mean(values, -1, keepdims=True)
    centred = values - row_mean
    variance = jnp.mean(centred * centred, -1, keepdims=True)
    return centred * lax.rsqrt(variance + EPSILON) * gain + shift


def gelu_exact(values):
    return jax.nn.gelu(values, approximate=False)


def plain_dot(left, right):
    return jnp.dot(left, right, preferred_element_type=jnp.float32)


def left_dot(left, right):
    return lax.dot_general(
        left, right, (((0,), (0,)), ((), ())), preferred_element_type=jnp.float32
    )


def right_dot(left, right):
    return lax.dot_general(
        left, right, (((1,), (1,)), ((), ())), preferred_element_type=jnp.float32
    )


def token_sum(values):
    return jnp.sum(values.astype(jnp.float32), 0)


def split_heads(values, piece_len):
    return values.reshape(values.shape[0], piece_len, HEADS, values.shape[2] // HEADS)


def block_length(piece_len, local_len):
    return math.gcd(math.gcd(piece_len, local_len), BLOCK_CAP)


def masked_scores(query_heads, key_heads, query_ids, key_ids, score_scale):
    scores = (
        jnp.einsum("rqhd,rkhd->rhqk", query_heads, key_heads, preferred_element_type=jnp.float32)
        * score_scale
    )
    same_doc = query_ids[:, None, :, None] == key_ids[:, None, None, :]
    return jnp.where(same_doc, scores, NEG_FILL)


def split_attend_back(
    query_heads,
    grad_heads,
    log_total,
    spread,
    query_ids,
    key_heads,
    value_heads,
    key_ids,
    score_scale,
):
    scores = masked_scores(query_heads, key_heads, query_ids, key_ids, score_scale)
    weights = jnp.exp(scores - jnp.transpose(log_total, (0, 2, 1))[..., None])
    grad_value = jnp.einsum(
        "rhqk,rqhd->rkhd",
        weights.astype(jnp.bfloat16),
        grad_heads,
        preferred_element_type=jnp.float32,
    )
    grad_weights = jnp.einsum(
        "rqhd,rkhd->rhqk", grad_heads, value_heads, preferred_element_type=jnp.float32
    )
    grad_scores = (weights * (grad_weights - jnp.transpose(spread, (0, 2, 1))[..., None])).astype(
        jnp.bfloat16
    )
    grad_query = (
        jnp.einsum("rhqk,rkhd->rqhd", grad_scores, key_heads, preferred_element_type=jnp.float32)
        * score_scale
    )
    grad_key = (
        jnp.einsum("rhqk,rqhd->rkhd", grad_scores, query_heads, preferred_element_type=jnp.float32)
        * score_scale
    )
    return (grad_query, grad_key, grad_value)


def add_into(buffer, term, block_start):
    current = lax.dynamic_slice_in_dim(buffer, block_start, term.shape[1], 1)
    return lax.dynamic_update_slice_in_dim(buffer, current + term, block_start, 1)


def split_rows(
    tokens,
    segments,
    keep_flags,
    query_weight,
    query_bias,
    key_weight,
    value_weight,
    value_bias,
    out_weight,
    out_bias,
    first_gain,
    first_shift,
    up_weight,
    up_bias,
    down_weight,
    down_bias,
    second_gain,
    second_shift,
    cotangent,
):
    row_count, local_tokens, model_width = tokens.shape
    head_width = model_width // HEADS
    score_scale = head_width ** (-0.5)
    flat_tokens = tokens.reshape(row_count * local_tokens, model_width)
    row_shape = (row_count, local_tokens, model_width)
    query_low = (
        (plain_dot(flat_tokens, query_weight) + query_bias).astype(jnp.bfloat16).reshape(row_shape)
    )
    key_low = plain_dot(flat_tokens, key_weight).astype(jnp.bfloat16).reshape(row_shape)
    value_low = (
        (plain_dot(flat_tokens, value_weight) + value_bias).astype(jnp.bfloat16).reshape(row_shape)
    )
    query_heads = split_heads(query_low, local_tokens)
    own_start = lax.axis_index("seq") * local_tokens
    own_ids = lax.dynamic_slice_in_dim(segments, own_start, local_tokens, 1)
    initial = (
        jnp.full((row_count, HEADS, local_tokens), NEG_FILL, jnp.float32),
        jnp.zeros((row_count, HEADS, local_tokens), jnp.float32),
        jnp.zeros((row_count, HEADS, local_tokens, head_width), jnp.float32),
    )
    key_piece = lax.all_gather(key_low, "seq", axis=1, tiled=True)
    value_piece = lax.all_gather(value_low, "seq", axis=1, tiled=True)
    block_size = block_length(key_piece.shape[1], local_tokens)

    def key_step(position, inner_state):
        running_max, running_sum, running_acc = inner_state
        block_start = position * block_size
        key_heads = split_heads(
            lax.dynamic_slice_in_dim(key_piece, block_start, block_size, 1), block_size
        )
        value_heads = split_heads(
            lax.dynamic_slice_in_dim(value_piece, block_start, block_size, 1), block_size
        )
        key_ids = lax.dynamic_slice_in_dim(segments, block_start, block_size, 1)
        scores = masked_scores(query_heads, key_heads, own_ids, key_ids, score_scale)
        newest = jnp.maximum(running_max, jnp.max(scores, -1))
        factor = jnp.exp(running_max - newest)
        weights = jnp.exp(scores - newest[..., None])
        running_sum = running_sum * factor + jnp.sum(weights, -1)
        update = jnp.einsum(
            "rhqk,rkhd->rhqd",
            weights.astype(jnp.bfloat16),
            value_heads,
            preferred_element_type=jnp.float32,
        )
        return (newest, running_sum, running_acc * factor[..., None] + update)

    running_max, running_sum, running_acc = lax.fori_loop(
        0, key_piece.shape[1] // block_size, key_step, initial
    )
    context_heads = jnp.transpose(running_acc / running_sum[..., None], (0, 2, 1, 3))
    log_total = jnp.transpose(running_max + jnp.log(running_sum), (0, 2, 1))
    context_low = context_heads.reshape(row_count * local_tokens, model_width).astype(jnp.bfloat16)
    first_sum = flat_tokens.astype(jnp.float32) + (plain_dot(context_low, out_weight) + out_bias)
    hidden, first_back = jax.vjp(norm_rows, first_sum, first_gain, first_shift)
    hidden_low = hidden.astype(jnp.bfloat16)
    pre_act = plain_dot(hidden_low, up_weight) + up_bias
    activated, act_back = jax.vjp(gelu_exact, pre_act)
    act_low = activated.astype(jnp.bfloat16)
    second_sum = hidden + (plain_dot(act_low, down_weight) + down_bias)
    normed, second_back = jax.vjp(norm_rows, second_sum, second_gain, second_shift)
    kept_rows = (keep_flags != 0)[:, None, None]
    layer_out = jnp.where(kept_rows, normed.reshape(row_shape), tokens.astype(jnp.float32)).astype(
        jnp.bfloat16
    )
    grad_out = jnp.where(kept_rows, cotangent.astype(jnp.float32), 0.0).reshape(
        row_count * local_tokens, model_width
    )
    grad_second, grad_second_gain, grad_second_shift = second_back(grad_out)
    grad_branch_low = grad_second.astype(jnp.bfloat16)
    grad_down_bias = token_sum(grad_branch_low)
    grad_down_weight = left_dot(act_low, grad_branch_low)
    (grad_pre,) = act_back(right_dot(grad_branch_low, down_weight))
    grad_pre_low = grad_pre.astype(jnp.bfloat16)
    grad_up_bias = token_sum(grad_pre_low)
    grad_up_weight = left_dot(hidden_low, grad_pre_low)
    grad_hidden = grad_second + right_dot(grad_pre_low, up_weight)
    grad_first, grad_first_gain, grad_first_shift = first_back(grad_hidden)
    grad_attn_low = grad_first.astype(jnp.bfloat16)
    grad_out_bias = token_sum(grad_attn_low)
    grad_out_weight = left_dot(context_low, grad_attn_low)
    late_grads = (
        grad_out_weight,
        grad_out_bias,
        grad_first_gain,
        grad_first_shift,
        grad_up_weight,
        grad_up_bias,
        grad_down_weight,
        grad_down_bias,
        grad_second_gain,
        grad_second_shift,
    )
    grad_context_low = right_dot(grad_attn_low, out_weight).astype(jnp.bfloat16)
    grad_context_rows = grad_context_low.reshape(row_shape)
    grad_heads = split_heads(grad_context_rows, local_tokens)
    spread = jnp.sum(grad_heads.astype(jnp.float32) * context_heads, -1)
    zero_local = jnp.zeros((row_count, local_tokens, HEADS, head_width), jnp.float32)
    zero_whole = jnp.zeros(
        (row_count, local_tokens * lax.axis_size("seq"), HEADS, head_width), jnp.float32
    )
    gathered_total, gathered_spread = (
        lax.all_gather(log_total, "seq", axis=1, tiled=True),
        lax.all_gather(spread, "seq", axis=1, tiled=True),
    )
    key_heads_local = split_heads(key_low, local_tokens)
    value_heads_local = split_heads(value_low, local_tokens)
    query_piece = lax.all_gather(query_low, "seq", axis=1, tiled=True)
    grad_piece = lax.all_gather(grad_context_rows, "seq", axis=1, tiled=True)
    back_block_size = block_length(query_piece.shape[1], local_tokens)

    def query_step(position, inner_state):
        grad_key, grad_value, queries_whole = inner_state
        block_start = position * back_block_size
        part_query, part_key, part_value = split_attend_back(
            split_heads(
                lax.dynamic_slice_in_dim(query_piece, block_start, back_block_size, 1),
                back_block_size,
            ),
            split_heads(
                lax.dynamic_slice_in_dim(grad_piece, block_start, back_block_size, 1),
                back_block_size,
            ),
            lax.dynamic_slice_in_dim(gathered_total, block_start, back_block_size, 1),
            lax.dynamic_slice_in_dim(gathered_spread, block_start, back_block_size, 1),
            lax.dynamic_slice_in_dim(segments, block_start, back_block_size, 1),
            key_heads_local,
            value_heads_local,
            own_ids,
            score_scale,
        )
        return (
            grad_key + part_key,
            grad_value + part_value,
            add_into(queries_whole, part_query, block_start),
        )

    grad_key, grad_value, queries_whole = lax.fori_loop(
        0, query_piece.shape[1] // back_block_size, query_step, (zero_local, zero_local, zero_whole)
    )
    grad_query = lax.psum_scatter(queries_whole, "seq", scatter_dimension=1, tiled=True)
    flat_shape = (row_count * local_tokens, model_width)
    grad_query_low = grad_query.reshape(flat_shape).astype(jnp.bfloat16)
    grad_key_low = grad_key.reshape(flat_shape).astype(jnp.bfloat16)
    grad_value_low = grad_value.reshape(flat_shape).astype(jnp.bfloat16)
    grad_query_bias = token_sum(grad_query_low)
    grad_query_weight = left_dot(flat_tokens, grad_query_low)
    grad_key_weight = left_dot(flat_tokens, grad_key_low)
    grad_value_bias = token_sum(grad_value_low)
    grad_value_weight = left_dot(flat_tokens, grad_value_low)
    grad_flat = (
        grad_first
        + right_dot(grad_query_low, query_weight)
        + right_dot(grad_key_low, key_weight)
        + right_dot(grad_value_low, value_weight)
    )
    tokens_grad = jnp.where(
        kept_rows, grad_flat.reshape(row_shape), cotangent.astype(jnp.float32)
    ).astype(jnp.bfloat16)
    early_grads = (
        grad_query_weight,
        grad_query_bias,
        grad_key_weight,
        grad_value_weight,
        grad_value_bias,
    )
    summed = lax.psum(
        (
            grad_query_weight,
            grad_query_bias,
            grad_key_weight,
            grad_value_weight,
            grad_value_bias,
            grad_out_weight,
            grad_out_bias,
            grad_first_gain,
            grad_first_shift,
            grad_up_weight,
            grad_up_bias,
            grad_down_weight,
            grad_down_bias,
            grad_second_gain,
            grad_second_shift,
        ),
        ("dp", "seq"),
    )
    early_grads = summed[:5]
    late_grads = summed[5:]
    return (
        layer_out,
        tokens_grad,
        early_grads[0],
        early_grads[1],
        early_grads[2],
        early_grads[3],
        early_grads[4],
        late_grads[0],
        late_grads[1],
        late_grads[2],
        late_grads[3],
        late_grads[4],
        late_grads[5],
        late_grads[6],
        late_grads[7],
        late_grads[8],
        late_grads[9],
    )


def deal_rows(
    tokens,
    segments,
    keep_flags,
    query_weight,
    query_bias,
    key_weight,
    value_weight,
    value_bias,
    out_weight,
    out_bias,
    first_gain,
    first_shift,
    up_weight,
    up_bias,
    down_weight,
    down_bias,
    second_gain,
    second_shift,
    cotangent,
):
    row_count, local_tokens, model = tokens.shape
    ring = lax.axis_size("seq")
    me = lax.axis_index("seq")
    rows = row_count // ring
    first_row = me * rows
    turns = [[(i, (i + turn) % ring) for i in range(ring)] for turn in range(ring)]
    back_turns = [[(i, (i - turn) % ring) for i in range(ring)] for turn in range(ring)]

    own_segments = lax.dynamic_slice_in_dim(segments, first_row, rows, 0)
    own_segments = jnp.concatenate(
        [
            lax.dynamic_slice_in_dim(
                own_segments, lax.rem(me - turn + ring, ring) * local_tokens, local_tokens, 1
            )
            for turn in range(ring)
        ],
        1,
    )
    extra_index = jnp.arange(EXTRA, dtype=jnp.int32)[None, :, None]
    same = own_segments[:, None, :] == extra_index
    query_extra = jnp.where(same & (extra_index < 3), 1.0, 0.0)
    key_extra = jnp.where(
        extra_index < 3, jnp.where(same, 0.0, NEG_FILL), jnp.where(extra_index < 6, 1.0, 0.0)
    )
    keep = lax.dynamic_slice_in_dim(keep_flags, first_row, rows, 0)
    line = lambda vector: vector.reshape(1, -1)
    forward_weights = (
        query_weight,
        line(query_bias),
        key_weight,
        value_weight,
        line(value_bias),
    )
    firsts = jnp.stack([lax.rem(me + turn, ring) * rows for turn in range(ring)])
    sends, projected = prepare(firsts, rows, tokens, cotangent, forward_weights)

    def fetch(part, turn):
        return lax.ppermute(part, "seq", turns[turn])

    first = [
        fetch(lax.dynamic_slice_in_dim(tokens, firsts[turn], 1, 0), turn)
        for turn in range(1, ring)
    ]
    first, sends, projected, query_extra, key_extra = after(
        (first, sends, projected, query_extra, key_extra)
    )
    remote, remote_cotangent, before = [first], [], first
    for row in range(rows):
        for index, fetched in ((row, remote), (rows + row, remote_cotangent)):
            if index:
                parts = [after(sends[turn][index - 1], before) for turn in range(ring - 1)]
                fetched.append([fetch(part, turn + 1) for turn, part in enumerate(parts)])
        before = remote[row]
    token_weights = (
        out_weight,
        line(out_bias),
        line(first_gain),
        line(first_shift),
        up_weight,
        line(up_bias),
        down_weight,
        line(down_bias),
        line(second_gain),
        line(second_shift),
    )
    back_weights = (query_weight, key_weight, value_weight)
    row_index = [(first_row + row).reshape(1) for row in range(rows)]
    sums = Sums()
    number, slots = sums.me.reshape(1), sums.devices
    early_number = sums.me_near.reshape(1)
    heads, contexts = [], []
    for row in range(rows):
        if row:
            remote[row] = after(remote[row], contexts[-1])
        query, key, value, context = attend(
            row, projected, remote[row], query_extra[row], key_extra[row], forward_weights
        )
        heads.append((query, key, value))
        contexts.append(context)
    remote_cotangent = after(remote_cotangent, contexts[-1])
    results = by_token(
        row_index[0],
        keep,
        number,
        tokens,
        remote,
        cotangent,
        remote_cotangent,
        contexts,
        token_weights,
        slots,
    )
    layer_outs = [results[row * ring : (row + 1) * ring] for row in range(rows)]
    results = results[rows * ring :]
    grad_heads, grad_first, late_near, late_far = results
    def give_back(parts, *before):
        return [
            part if turn == 0 else lax.ppermute(after(part, *before), "seq", back_turns[turn])
            for turn, part in enumerate(parts)
        ]

    def place(moved):
        by_turn = [jnp.concatenate(parts, 0) for parts in zip(*moved)]
        places = [
            [by_turn[(slot - index) % ring] for slot in range(ring)] for index in range(ring)
        ]
        whole = jnp.concatenate(places[0], 0)
        for index in range(1, ring):
            whole = jnp.where(me == index, jnp.concatenate(places[index], 0), whole)
        return whole

    parts = 2
    last = rows * parts - 1
    totals, biases = [None] * parts, [None] * parts
    tokens_grads = []
    here = early_number
    late = [late_near, sums.swap(late_far, 0, 1)]
    layer_outs = [give_back(parts_) for parts_ in layer_outs]
    for call in range(rows * parts):
        row, part = divmod(call, parts)
        if part == 0:
            grad_tokens = grad_first
        results = attend_back(
            (row, rows, part, parts),
            row_index[row],
            here,
            tokens,
            remote[row],
            (*heads[row], grad_heads),
            grad_tokens,
            back_weights,
            totals,
            biases,
            slots,
            1 if 1 < call < last else 200,
        )
        if part == parts - 1:
            tokens_grads.append(give_back(results[:ring]))
            results = results[ring:]
        else:
            grad_tokens, *results = results
        if call < last:
            totals[part], biases[part] = results
        if call == 0:
            late, layer_outs[0] = after((late, layer_outs[0]), results[0])
            late = sums.add_parts(after(late, layer_outs[0]), 1)
            here = after(early_number, *late)
            late = sums.meet(late, 1)
        if call == last - 1:
            late, layer_outs = after((late, layer_outs), results[0])
            late = sums.add_parts(after(late, layer_outs), 2)
            here = after(early_number, *late)
            late = sums.meet(late, 2)
    late, tokens_grads[:-1] = after((late, tokens_grads[:-1]), results[0])
    early_near, early_far = after(results, late, tokens_grads[:-1])
    early = sums.add_parts([early_near, sums.swap(early_far, 0, 1)], 1)
    late = after(add_up(late), early)
    late = [late, *sums.others(late, 2)]
    early, tokens_grads[-1] = after((sums.meet(early, 1), tokens_grads[-1]), late, tokens_grads[-1])
    early = add_up(early)
    late = jnp.concatenate(late, 0)
    late = after(late, early)
    late = [late, *sums.others(late, 1)]
    layer_out, tokens_grad = place(layer_outs), place(tokens_grads)
    early = add_up(after([early, *sums.others(early, 2)], late, layer_out, tokens_grad))
    late = after(late, early)
    late = [*late, *[sums.swap(array, 0, 1) for array in late]]
    early = [early, *sums.others(early, 1)]
    hidden_units = up_weight.shape[1]
    grad_up, grad_down, grad_out_weight, *late_lines = unpack(
        number,
        late,
        [(model, hidden_units), (hidden_units, model), (model, model)],
        model,
        [model] * 7 + [hidden_units],
    )
    early = after(early, late_lines)
    early = [*early, *[sums.swap(array, 0, 1) for array in early]]
    late_vectors = [line.reshape(-1) for line in late_lines]
    early = after(early, late_vectors)
    grad_query, grad_key, grad_value, query_bias_grad = unpack(
        early_number, early, [(model, model)] * 3, model, [model]
    )
    (
        grad_out_bias,
        grad_first_gain,
        grad_first_shift,
        grad_down_bias,
        grad_second_gain,
        grad_second_shift,
        grad_value_bias,
        grad_up_bias,
    ) = late_vectors
    return (
        layer_out,
        tokens_grad,
        grad_query,
        query_bias_grad.reshape(-1),
        grad_key,
        grad_value,
        grad_value_bias,
        grad_out_weight,
        grad_out_bias,
        grad_first_gain,
        grad_first_shift,
        grad_up,
        grad_up_bias,
        grad_down,
        grad_down_bias,
        grad_second_gain,
        grad_second_shift,
    )


def solution(mesh):
    dp, ring = mesh.shape["dp"], mesh.shape["seq"]

    def placed(function, mesh, rows):
        return jax.shard_map(
            function,
            mesh=mesh,
            in_specs=(
                P(rows, "seq", None),
                P(rows, None),
                P(rows),
                *([P()] * 15),
                P(rows, "seq", None),
            ),
            out_specs=(P(rows, "seq", None), P(rows, "seq", None), *([P()] * 15)),
            check_vma=False,
        )

    def layer(tokens, *others):
        row_count, model = tokens.shape[0] // dp, tokens.shape[2]
        powers = dp & (dp - 1) == 0 and ring & (ring - 1) == 0 and dp >= 4
        if not powers or row_count % ring or model % (16 * dp * ring):
            return placed(split_rows, mesh, "dp")(tokens, *others)
        axes = (FAR, MIDDLE, NEAR)
        finer = jax.sharding.Mesh(mesh.devices.reshape(dp // 4, 2, 2, ring), (*axes, SEQ))
        return placed(deal_rows, finer, axes)(tokens, *others)

    return layer
```
